32 devices in a mesh: dp: 4 (over y, core), seq: 8 (over z, x).
Axes of the slice: x: 2, y: 2, z: 4, core: 2. Of those that a mesh axis runs over, the one named last changes fastest.
Arguments:
- tokens: bfloat16 [4, 3072, 1024], P('dp', 'seq'), may hold values from -6 to 6
- gain_one: bfloat16 [1024], P(('dp', 'seq')), may hold values from 0.5 to 1.5
- w_in: bfloat16 [1024, 3328], P(('dp', 'seq')), may hold values from -0.1875 to 0.1875
- w_step: bfloat16 [1024, 24], P(('dp', 'seq')), may hold values from -0.375 to 0.375
- conv_weight: bfloat16 [4, 1792], P(None, ('dp', 'seq')), may hold values from -3 to 3
- conv_bias: bfloat16 [1792], P(('dp', 'seq')), may hold values from -3 to 3
- mamba_heads: float32 [2, 24], replicated, may hold values from -11.5 to 0.5
- skip_weight: float32 [24], replicated, may hold values from 0.5 to 1.5
- w_query: bfloat16 [1024, 512], P(('dp', 'seq')), may hold values from -0.1875 to 0.1875
- w_keyval: bfloat16 [1024, 256], P(('dp', 'seq')), may hold values from -0.1875 to 0.1875
- w_attn_out: bfloat16 [512, 1024], P(None, ('dp', 'seq')), may hold values from -2 to 2
- w_mix_out: bfloat16 [1536, 1024], P(None, ('dp', 'seq')), may hold values from -0.109375 to 0.109375
- gain_two: bfloat16 [1024], P(('dp', 'seq')), may hold values from 0.5 to 1.5
- w_gate_up: bfloat16 [1024, 4096], P(('dp', 'seq')), may hold values from -0.1875 to 0.1875
- w_down: bfloat16 [2048, 1024], P(None, ('dp', 'seq')), may hold values from -0.125 to 0.125
- cotangent: bfloat16 [4, 3072, 1024], P('dp', 'seq'), may hold values from -6 to 6
Outputs:
- output: bfloat16 [4, 3072, 1024], P('dp', 'seq')
- input_grad: float32 [4, 3072, 1024], P('dp', 'seq')
- grad_gain_one: float32 [1024], P(('dp', 'seq'))
- grad_w_in: float32 [1024, 3328], P(('dp', 'seq'))
- grad_w_step: float32 [1024, 24], P(('dp', 'seq'))
- grad_conv_weight: float32 [4, 1792], P(None, ('dp', 'seq'))
- grad_conv_bias: float32 [1792], P(('dp', 'seq'))
- grad_mamba_heads: float32 [2, 24], replicated
- grad_skip_weight: float32 [24], replicated
- grad_w_query: float32 [1024, 512], P(('dp', 'seq'))
- grad_w_keyval: float32 [1024, 256], P(('dp', 'seq'))
- grad_w_attn_out: float32 [512, 1024], P(None, ('dp', 'seq'))
- grad_w_mix_out: float32 [1536, 1024], P(None, ('dp', 'seq'))
- grad_gain_two: float32 [1024], P(('dp', 'seq'))
- grad_w_gate_up: float32 [1024, 4096], P(('dp', 'seq'))
- grad_w_down: float32 [2048, 1024], P(None, ('dp', 'seq'))
The draws below stay inside these ranges and needn't reach their ends.
All inputs are finite; a program needn't handle non-finite values.
Results may differ from the reference program's by a relative error of at most 0.017.
Values may be sent and summed in bfloat16 or wider, within the bound.
No kernel may reach another device: no remote copies, remote signals or barrier semaphores. Data moves between devices by JAX's collectives and lax.ppermute only.
A program may use at most 256 MiB of HBM per device.

```python
import math
import jax
import jax.numpy as jnp
from jax import lax

D = 1024
MHEADS = 24
MHEAD_DIM = 64
STATE = 128
CONV = 4
QHEADS = 8
KVHEADS = 2
HEAD_DIM = 64
FF = 2048
TOK_DEV = 384
SEQS = 4
LENGTH = 3072
CHANNELS = 1792


def draw_mamba_heads(key, part):
    key = jax.random.fold_in(key, 7)
    rate_key, bias_key = jax.random.split(key, 2)
    log_rates = jax.random.uniform(rate_key, (MHEADS,), jnp.float32, -11.5, -1.2)
    step_bias = jax.random.uniform(bias_key, (MHEADS,), jnp.float32, -1.5, 0.5)
    return jnp.stack([log_rates, step_bias], axis=0)


def level_of(rng, extent, cuts, least, top_value):
    loudness, own = 1.0, jax.random.fold_in(rng, 6)
    for axis_at, blocks in cuts:
        draws = jnp.exp(jax.random.uniform(jax.random.fold_in(own, axis_at), (blocks,), jnp.float32, least / len(cuts), top_value / len(cuts)))
        loudness = loudness * jnp.repeat(draws, extent[axis_at] // blocks).reshape([-1 if axis == axis_at else 1 for axis in range(len(extent))])
    return loudness


def centred(rng, dims, width, most, cuts=(), kind=jnp.bfloat16):
    array = width * jax.random.normal(rng, dims, jnp.float32)
    if cuts:
        array = array * level_of(rng, dims, cuts, -0.22, 0.18)
    return jnp.clip(array, -most, most).astype(kind)


def setup_inputs(seed: int = 0) -> dict:
    key_of = jax.random.split(jax.random.key(seed), 17)
    return {
        "tokens": centred(key_of[0], (SEQS, LENGTH, D), 1.0, 6.0, ((0, 4), (1, 8))),
        "gain_one": jnp.clip(1.0 + 0.1 * jax.random.normal(key_of[1], (D,), jnp.float32), 0.5, 1.5).astype(jnp.bfloat16),
        "w_in": centred(key_of[2], (D, 2 * MHEADS * MHEAD_DIM + 2 * STATE), D ** -0.5, 0.1875, ((0, 32),)),
        "w_step": centred(key_of[3], (D, MHEADS), (D // 4) ** -0.5, 0.375, ((0, 32),)),
        "conv_weight": centred(key_of[4], (CONV, CHANNELS), CONV ** -0.5, 3.0, ((1, 32),)),
        "conv_bias": centred(key_of[5], (CHANNELS,), 0.5, 3.0, ((0, 32),)),
        "mamba_heads": draw_mamba_heads(jax.random.fold_in(key_of[16], 71), 0),
        "skip_weight": jnp.clip(jax.random.uniform(key_of[7], (MHEADS,), jnp.float32, 0.5, 1.5), 0.5, 1.5),
        "w_query": centred(key_of[8], (D, QHEADS * HEAD_DIM), D ** -0.5, 0.1875, ((0, 32),)),
        "w_keyval": centred(key_of[9], (D, 2 * KVHEADS * HEAD_DIM), D ** -0.5, 0.1875, ((0, 32),)),
        "w_attn_out": centred(key_of[10], (QHEADS * HEAD_DIM, D), (max(1, 32768 // LENGTH)) ** -0.5, 2.0, ((1, 32),)),
        "w_mix_out": centred(key_of[11], (MHEADS * MHEAD_DIM, D), (MHEADS * MHEAD_DIM * 2) ** -0.5, 0.109375, ((1, 32),)),
        "gain_two": jnp.clip(1.0 + 0.1 * jax.random.normal(key_of[12], (D,), jnp.float32), 0.5, 1.5).astype(jnp.bfloat16),
        "w_gate_up": centred(key_of[13], (D, 2 * FF), D ** -0.5, 0.1875, ((0, 32),)),
        "w_down": centred(key_of[14], (FF, D), FF ** -0.5, 0.125, ((1, 32),)),
        "cotangent": centred(key_of[15], (SEQS, LENGTH, D), 1.0, 6.0, ((0, 4), (1, 8))),
    }


@jax.custom_vjp
def low(v):
    return lax.optimization_barrier(v.astype(jnp.bfloat16)).astype(jnp.float32)

@jax.custom_vjp
def low_back(v):
    return v

def low_keep(v):
    return (low(v), None)

def low_pass(kept, grad):
    return (grad,)

def back_keep(v):
    return (v, None)

def back_low(kept, grad):
    return (low(grad),)
low.defvjp(low_keep, low_pass)
low_back.defvjp(back_keep, back_low)
norm_epsilon = 1e-06
rope_base = 100000000000.0
masked_score = -1e+30
highest_precision = lax.Precision.HIGHEST

def matmul(left, right):
    return jnp.dot(left, right, precision=highest_precision)

def rms_norm(values, gain_vector):
    return values * lax.rsqrt(lax.optimization_barrier(jnp.mean(values * values, axis=-1, keepdims=True)) + norm_epsilon) * gain_vector

def rope_tables(positions, head_width):
    half_width = head_width // 2
    exponents = jnp.arange(half_width).astype(jnp.float32) * (2.0 / head_width)
    frequency = rope_base ** (-exponents)
    angles = positions.astype(jnp.float32)[:, None] * frequency[None, :]
    return (jnp.cos(angles), jnp.sin(angles))

def rotate(values, cosine, sine_table):
    half_width = values.shape[-1] // 2
    first_half = values[..., :half_width]
    second_half = values[..., half_width:]
    cosine_b = cosine[:, None, :]
    sine_b = sine_table[:, None, :]
    return jnp.concatenate([first_half * cosine_b - second_half * sine_b, second_half * cosine_b + first_half * sine_b], axis=-1)

def mamba_inputs(extended, step_raw, conv_weight, conv_bias, head_params):
    row_count = extended.shape[0] - (CONV - 1)
    conv_sum = conv_bias[None, :] + conv_weight[0][None, :] * extended[0:row_count]
    for offset in range(1, CONV):
        conv_sum = conv_sum + conv_weight[offset][None, :] * extended[offset:offset + row_count]
    activated = jax.nn.silu(conv_sum)
    inner_width = MHEADS * MHEAD_DIM
    inputs_x = activated[:, :inner_width].reshape(row_count, MHEADS, MHEAD_DIM)
    input_mat = activated[:, inner_width:inner_width + STATE]
    output_mat = activated[:, inner_width + STATE:]
    step_size = jax.nn.softplus(step_raw + head_params[1][None, :])
    log_decay = -jnp.exp(head_params[0])[None, :] * step_size
    return (inputs_x, input_mat, output_mat, log_decay, step_size)

def ssd_summary(inputs_x, input_mat, log_decay, step_size):
    cumulative = jnp.cumsum(log_decay, axis=0)
    weights_tail = jnp.exp(cumulative[-1][None, :] - cumulative) * step_size
    fresh_state = jnp.einsum('th,thp,tn->hpn', weights_tail, inputs_x, input_mat, precision=highest_precision)
    return (jnp.exp(cumulative[-1]), fresh_state)

def ssd_output(inputs_x, input_mat, output_mat, log_decay, step_size, carry_state):
    row_count = inputs_x.shape[0]
    cumulative = jnp.cumsum(log_decay, axis=0)
    by_head = cumulative.T
    indices = jnp.arange(row_count)
    causal_mask = (indices[:, None] >= indices[None, :])[None]
    gap_matrix = jnp.where(causal_mask, by_head[:, :, None] - by_head[:, None, :], 0.0)
    kernel = jnp.where(causal_mask, jnp.exp(gap_matrix), 0.0)
    intersection = jnp.dot(output_mat, input_mat.T, precision=highest_precision)
    mixing = kernel * intersection[None] * step_size.T[:, None, :]
    within = jnp.einsum('hts,shp->thp', mixing, inputs_x, precision=highest_precision)
    carried = jnp.einsum('tn,hpn->thp', output_mat, carry_state, precision=highest_precision) * jnp.exp(cumulative)[:, :, None]
    return within + carried

def attention_heads(queries, key_heads, value_heads):
    seq_len = queries.shape[0]
    block_rows = min(512, seq_len)
    group_size = QHEADS // KVHEADS
    grouped = queries.reshape(seq_len // block_rows, block_rows, KVHEADS, group_size, HEAD_DIM)
    key_pos = jnp.arange(seq_len).astype(jnp.int32)
    score_scale = 1.0 / math.sqrt(HEAD_DIM)

    def one_block(block_pair):
        block_queries, block_index = block_pair
        scores = low_back(jnp.einsum('tgjd,sgd->gjts', block_queries, key_heads, precision=highest_precision) * score_scale)
        query_pos = block_index * block_rows + jnp.arange(block_rows).astype(jnp.int32)
        allowed = key_pos[None, :] <= query_pos[:, None]
        scores = jnp.where(allowed, scores, masked_score)
        soft_weights = low(jax.nn.softmax(scores, axis=-1))
        return jnp.einsum('gjts,sgd->tgjd', soft_weights, value_heads, precision=highest_precision)
    block_index = jnp.arange(seq_len // block_rows).astype(jnp.int32)
    outputs = lax.map(jax.checkpoint(one_block), (grouped, block_index))
    return outputs.reshape(seq_len, QHEADS * HEAD_DIM)

def layer(tokens, gain_one, w_in, w_step, conv_weight, conv_bias, mamba_heads, skip_weight, w_query, w_keyval, w_attn_out, w_mix_out, gain_two, w_gate_up, w_down):
    seq_len = tokens.shape[0]
    inner_width = MHEADS * MHEAD_DIM
    key_width = KVHEADS * HEAD_DIM
    normed = low(rms_norm(tokens, gain_one))
    projected = low_back(matmul(normed, w_in))
    step_raw = low_back(matmul(normed, w_step))
    gate_z = projected[:, :inner_width]
    conv_input = low(projected[:, inner_width:])
    extended = jnp.concatenate([jnp.zeros((CONV - 1, conv_input.shape[1]), jnp.float32), conv_input], axis=0)
    inputs_x, input_mat, output_mat, log_decay, step_size = mamba_inputs(extended, step_raw, conv_weight, conv_bias, mamba_heads)
    blocks = seq_len // TOK_DEV

    def mamba_block(carry_state, pieces):
        block_x, block_in, block_out, block_decay, block_step = pieces
        block_y = ssd_output(block_x, block_in, block_out, block_decay, block_step, carry_state)
        factor, fresh_state = ssd_summary(block_x, block_in, block_decay, block_step)
        return (factor[:, None, None] * carry_state + fresh_state, block_y)
    start_state = jnp.zeros((MHEADS, MHEAD_DIM, STATE), jnp.float32)
    _, block_ys = lax.scan(jax.checkpoint(mamba_block), start_state, (inputs_x.reshape(blocks, TOK_DEV, MHEADS, MHEAD_DIM), input_mat.reshape(blocks, TOK_DEV, STATE), output_mat.reshape(blocks, TOK_DEV, STATE), log_decay.reshape(blocks, TOK_DEV, MHEADS), step_size.reshape(blocks, TOK_DEV, MHEADS)))
    mixed_y = block_ys.reshape(seq_len, MHEADS, MHEAD_DIM) + skip_weight[None, :, None] * inputs_x
    mixer = low(mixed_y.reshape(seq_len, inner_width) * jax.nn.silu(gate_z))
    mixed = low_back(matmul(mixer, w_mix_out))
    query_raw = low_back(matmul(normed, w_query))
    keyval_raw = low_back(matmul(normed, w_keyval))
    cosine, sine_table = rope_tables(jnp.arange(seq_len), HEAD_DIM)
    queries = low(rotate(query_raw.reshape(seq_len, QHEADS, HEAD_DIM), cosine, sine_table))
    key_heads = low(rotate(keyval_raw[:, :key_width].reshape(seq_len, KVHEADS, HEAD_DIM), cosine, sine_table))
    value_heads = low(keyval_raw[:, key_width:].reshape(seq_len, KVHEADS, HEAD_DIM))
    attention = low(low_back(attention_heads(queries, key_heads, value_heads)))
    attended = low_back(matmul(attention, w_attn_out))
    hidden = tokens + mixed + attended
    normed_two = low(rms_norm(hidden, gain_two))
    gate_up = low_back(matmul(normed_two, w_gate_up))
    activated = low(jax.nn.silu(gate_up[:, :FF]) * gate_up[:, FF:])
    return hidden + low_back(matmul(activated, w_down))

def reference(tokens, gain_one, w_in, w_step, conv_weight, conv_bias, mamba_heads, skip_weight, w_query, w_keyval, w_attn_out, w_mix_out, gain_two, w_gate_up, w_down, cotangent):
    weight_list = [gain_one, w_in, w_step, conv_weight, conv_bias, mamba_heads, skip_weight, w_query, w_keyval, w_attn_out, w_mix_out, gain_two, w_gate_up, w_down]
    floats = [weight_item.astype(jnp.float32) for weight_item in weight_list]

    def one_sequence(running, seq_pair):
        seq_tokens, seq_cotangent = seq_pair
        result, pull_back = jax.vjp(layer, seq_tokens.astype(jnp.float32), *floats)
        grads = pull_back(seq_cotangent.astype(jnp.float32))
        summed = tuple((running_sum + new_grad for running_sum, new_grad in zip(running, grads[1:])))
        return (summed, (result.astype(jnp.bfloat16), grads[0]))
    start_sums = tuple((jnp.zeros(weight_item.shape, jnp.float32) for weight_item in floats))
    sums, (outputs, input_grads) = lax.scan(one_sequence, start_sums, (tokens, cotangent))
    return (outputs, input_grads, sums[0], sums[1], sums[2], sums[3], sums[4], sums[5], sums[6], sums[7], sums[8], sums[9], sums[10], sums[11], sums[12], sums[13])
```

```python
from functools import partial
import math

import jax
import jax.numpy as jnp
from jax import lax
from jax.sharding import Mesh
from jax.sharding import PartitionSpec as P

MHEADS = 24
MHEAD_DIM = 64
STATE = 128
CONV = 4
QHEADS = 8
KVHEADS = 2
HEAD_DIM = 64
FF = 2048


norm_epsilon = 1e-06
rope_base = 100000000000.0
key_block = 1024
masked_score = -1e30
highest_precision = lax.Precision.HIGHEST


def rms_norm(values, gain_vector):
    return (
        values
        * lax.rsqrt(jnp.mean(values * values, axis=-1, keepdims=True) + norm_epsilon)
        * gain_vector
    )


def rope_tables(positions, head_width):
    half_width = head_width // 2
    exponents = jnp.arange(half_width).astype(jnp.float32) * (2.0 / head_width)
    frequency = rope_base ** (-exponents)
    angles = positions.astype(jnp.float32)[:, None] * frequency[None, :]
    return (jnp.cos(angles), jnp.sin(angles))


def rotate(values, cosine, sine_table):
    half_width = values.shape[-1] // 2
    first_half = values[..., :half_width]
    second_half = values[..., half_width:]
    cosine_b = cosine[:, None, :]
    sine_b = sine_table[:, None, :]
    return jnp.concatenate(
        [
            first_half * cosine_b - second_half * sine_b,
            second_half * cosine_b + first_half * sine_b,
        ],
        axis=-1,
    )


def outer_product(left, right):
    return lax.dot_general(
        left, right, (((0,), (0,)), ((), ())), preferred_element_type=jnp.float32
    )


def back_product(grad_rows, weight_matrix):
    return lax.dot_general(
        grad_rows, weight_matrix, (((1,), (1,)), ((), ())), preferred_element_type=jnp.float32
    )


def mamba_inputs(extended, step_raw, conv_weight, conv_bias, head_params):
    row_count = extended.shape[0] - (CONV - 1)
    conv_sum = conv_bias[None, :] + conv_weight[0][None, :] * extended[0:row_count]
    for offset in range(1, CONV):
        conv_sum = conv_sum + conv_weight[offset][None, :] * extended[offset : offset + row_count]
    activated = jax.nn.silu(conv_sum)
    inner_width = MHEADS * MHEAD_DIM
    inputs_x = activated[:, :inner_width].reshape(row_count, MHEADS, MHEAD_DIM)
    input_mat = activated[:, inner_width : inner_width + STATE]
    output_mat = activated[:, inner_width + STATE :]
    step_size = jax.nn.softplus(step_raw + head_params[1][None, :])
    log_decay = -jnp.exp(head_params[0])[None, :] * step_size
    return (inputs_x, input_mat, output_mat, log_decay, step_size)


def ssd_summary(inputs_x, input_mat, log_decay, step_size):
    cumulative = jnp.cumsum(log_decay, axis=0)
    weights_tail = jnp.exp(cumulative[-1][None, :] - cumulative) * step_size
    fresh_state = jnp.einsum(
        "th,thp,tn->hpn", weights_tail, inputs_x, input_mat, precision=highest_precision
    )
    return (jnp.exp(cumulative[-1]), fresh_state)


def ssd_output(inputs_x, input_mat, output_mat, log_decay, step_size, carry_state):
    row_count = inputs_x.shape[0]
    cumulative = jnp.cumsum(log_decay, axis=0)
    by_head = cumulative.T
    indices = jnp.arange(row_count)
    causal_mask = (indices[:, None] >= indices[None, :])[None]
    gap_matrix = jnp.where(causal_mask, by_head[:, :, None] - by_head[:, None, :], 0.0)
    kernel = jnp.where(causal_mask, jnp.exp(gap_matrix), 0.0)
    intersection = jnp.dot(output_mat, input_mat.T, precision=highest_precision)
    mixing = kernel * intersection[None] * step_size.T[:, None, :]
    within = jnp.einsum("hts,shp->thp", mixing, inputs_x, precision=highest_precision)
    carried = (
        jnp.einsum("tn,hpn->thp", output_mat, carry_state, precision=highest_precision)
        * jnp.exp(cumulative)[:, :, None]
    )
    return within + carried


def mamba_mix(
    inputs_x, input_mat, output_mat, log_decay, step_size, carry_state, gate_z, skip_vector
):
    row_count = inputs_x.shape[0]
    mixed_y = (
        ssd_output(inputs_x, input_mat, output_mat, log_decay, step_size, carry_state)
        + skip_vector[None, :, None] * inputs_x
    )
    return mixed_y.reshape(row_count, MHEADS * MHEAD_DIM) * jax.nn.silu(gate_z)


def mamba_local(
    extended, step_raw, gate_z, conv_weight, conv_bias, head_params, skip_vector, carry_state
):
    inputs_x, input_mat, output_mat, log_decay, step_size = mamba_inputs(
        extended, step_raw, conv_weight, conv_bias, head_params
    )
    mixer = mamba_mix(
        inputs_x, input_mat, output_mat, log_decay, step_size, carry_state, gate_z, skip_vector
    )
    factor, fresh_state = ssd_summary(inputs_x, input_mat, log_decay, step_size)
    end_state = factor[:, None, None] * carry_state + fresh_state
    return ((mixer, end_state), (output_mat, jnp.cumsum(log_decay, axis=0)))


def online_block(running, key_rows, first_key, queries, query_pos):
    best_score, weight_total, weighted = running
    row_count = key_rows.shape[0]
    key_width = KVHEADS * HEAD_DIM
    key_heads = key_rows[:, :key_width].reshape(row_count, KVHEADS, HEAD_DIM)
    value_heads = key_rows[:, key_width:].reshape(row_count, KVHEADS, HEAD_DIM)
    score_scale = 1.0 / math.sqrt(HEAD_DIM)
    scores = (
        jnp.einsum("tgjd,sgd->gjts", queries, key_heads, preferred_element_type=jnp.float32)
        * score_scale
    )
    key_pos = first_key + jnp.arange(row_count, dtype=jnp.int32)
    allowed = key_pos[None, :] <= query_pos[:, None]
    scores = jnp.where(allowed, scores, masked_score)
    new_best = jnp.maximum(best_score, jnp.max(scores, axis=-1))
    rescale = jnp.exp(best_score - new_best)
    soft_weights = jnp.where(allowed, jnp.exp(scores - new_best[..., None]), 0.0)
    weight_total = weight_total * rescale + jnp.sum(soft_weights, axis=-1)
    weighted = weighted * rescale[..., None] + jnp.einsum(
        "gjts,sgd->gjtd",
        soft_weights.astype(jnp.bfloat16),
        value_heads,
        preferred_element_type=jnp.float32,
    )
    return (new_best, weight_total, weighted)


def attend_piece(running, key_piece, first_key, queries, query_pos):
    row_count = key_piece.shape[0]
    block_rows = math.gcd(row_count, key_block)
    block_count = row_count // block_rows
    stacked = key_piece.reshape(block_count, block_rows, key_piece.shape[1])
    firsts = block_rows * jnp.arange(block_count, dtype=jnp.int32)
    last_query = query_pos[-1]

    def advance(state_now, item_pair):
        key_rows, block_first = item_pair
        updated = lax.cond(
            block_first <= last_query,
            lambda carried: online_block(carried, key_rows, block_first, queries, query_pos),
            lambda carried: carried,
            state_now,
        )
        return (updated, None)

    running, _ = lax.scan(advance, running, (stacked, firsts))
    return running


seq_axes = ("z", "x")
chip_axes = ("y", "z", "x")


def shifted(block, axis, distance):
    count = lax.axis_size(axis)
    return lax.ppermute(block, axis, [(i, (i + distance) % count) for i in range(count)])


def from_behind(block, distance):
    devices = range(lax.axis_size(seq_axes))
    route = [(i - distance, i) for i in devices if i - distance in devices]
    return lax.ppermute(block, seq_axes, route)


def own_half_first(values):
    cuts = 2 * lax.axis_size("y")
    width = values.shape[1] // cuts
    blocks = [values[:, i * width : (i + 1) * width] for i in range(cuts)]
    first = lax.axis_index("core") == 0
    own = [jnp.where(first, a, b) for a, b in zip(blocks[0::2], blocks[1::2])]
    other = [jnp.where(first, b, a) for a, b in zip(blocks[0::2], blocks[1::2])]
    return jnp.concatenate(own + other, axis=1)


def usual_order(values):
    cuts = 2 * lax.axis_size("y")
    width = values.shape[1] // cuts
    blocks = [values[:, i * width : (i + 1) * width] for i in range(cuts)]
    first = lax.axis_index("core") == 0
    merged = []
    for own, other in zip(blocks[: cuts // 2], blocks[cuts // 2 :]):
        merged += [jnp.where(first, own, other), jnp.where(first, other, own)]
    return jnp.concatenate(merged, axis=1)


def gather_rows(shard):
    own = lax.all_gather(shard, chip_axes, axis=0, tiled=True)
    return own, shifted(own, "core", 1)


def times_rows(values, pair):
    half = values.shape[1] // 2
    return jnp.dot(values[:, :half], pair[0], preferred_element_type=jnp.float32) + jnp.dot(
        values[:, half:], pair[1], preferred_element_type=jnp.float32
    )


def times_rows_back(values, pair):
    return jnp.concatenate([back_product(values, pair[0]), back_product(values, pair[1])], axis=1)


def swap_sum(total, axis, dim):
    count = lax.axis_size(axis)
    place = lax.axis_index(axis)
    kept = lax.dynamic_index_in_dim(total, place, dim, False)
    for step in range(1, count):
        part = lax.dynamic_index_in_dim(total, (place + step) % count, dim, False)
        kept = kept + shifted(part.astype(jnp.bfloat16), axis, step).astype(jnp.float32)
    return kept


def scatter_product(left, right):
    half = left.shape[1] // 2
    sizes = [lax.axis_size(axis) for axis in chip_axes]
    rows = half // math.prod(sizes)
    middle = right.shape[1] // 256 * 128
    pieces = []
    for columns, order in (
        (right[:, :middle], (("x", 2), ("y", 0), ("z", 0))),
        (right[:, middle:], (("y", 0), ("x", 1), ("z", 0))),
    ):
        sent = outer_product(left[:, half:], columns).astype(jnp.bfloat16)
        received = shifted(sent, "core", 1)
        total = outer_product(left[:, :half], columns) + received.astype(jnp.float32)
        total = total.reshape(*sizes, rows, columns.shape[1])
        for axis, dim in order:
            total = swap_sum(total, axis, dim)
        pieces.append(total)
    return jnp.concatenate(pieces, axis=1)


def sum_everywhere(values):
    for axis in ("core", "x", "y", "z"):
        count = lax.axis_size(axis)
        step = 1
        while step < count:
            values = values + lax.ppermute(values, axis, [(i, i ^ step) for i in range(count)])
            step *= 2
    return values


def spread_states(states, factor):
    width = states.shape[-1]
    rows = states.reshape(-1, width)
    last = jnp.zeros((16, width), jnp.float32).at[0, : factor.shape[0]].set(factor)
    packed = jnp.concatenate([rows, last], axis=0).astype(jnp.bfloat16)
    gathered = lax.all_gather(packed, seq_axes)
    decays = gathered[:, rows.shape[0], : factor.shape[0]].astype(jnp.float32)
    return gathered[:, : rows.shape[0]].reshape(-1, *states.shape), decays


def carried_from_before(gathered, decays):
    place = lax.axis_index(seq_axes)
    order = jnp.arange(decays.shape[0])[:, None]
    between = jnp.where(order < place, decays, 1.0)
    after = lax.cumprod(between, axis=0, reverse=True)
    after = jnp.concatenate([after[1:], jnp.ones_like(after[:1])], axis=0)
    weights = jnp.where(order < place, after, 0.0)
    return jnp.sum(weights[:, :, None, None] * gathered.astype(jnp.float32), axis=0)


def carried_from_after(gathered, decays):
    place = lax.axis_index(seq_axes)
    order = jnp.arange(decays.shape[0])[:, None]
    between = jnp.where(order > place, decays, 1.0)
    before = lax.cumprod(between, axis=0)
    before = jnp.concatenate([jnp.ones_like(before[:1]), before[:-1]], axis=0)
    weights = jnp.where(order > place, before, 0.0)
    return jnp.sum(weights[:, :, None, None] * gathered.astype(jnp.float32), axis=0)


def sum_key_grads(grad_rows):
    sizes = [lax.axis_size(axis) for axis in seq_axes]
    total = grad_rows.reshape(*sizes, -1, grad_rows.shape[1])
    return swap_sum(swap_sum(total, "x", 1), "z", 0)


def on_device(
    tokens,
    gain_one,
    w_in,
    w_step,
    conv_weight,
    conv_bias,
    mamba_heads,
    skip_weight,
    w_query,
    w_keyval,
    w_attn_out,
    w_mix_out,
    gain_two,
    w_gate_up,
    w_down,
    cotangent,
):
    inputs = own_half_first(tokens[0]).astype(jnp.float32)
    grad_output = own_half_first(cotangent[0])
    row_count = inputs.shape[0]
    inner_width = MHEADS * MHEAD_DIM
    channels = conv_weight.shape[1] * lax.axis_size(("y", "core", "z", "x"))
    key_width = KVHEADS * HEAD_DIM
    group_size = QHEADS // KVHEADS
    own_rows = gain_one.shape[0]
    taps = jnp.concatenate([conv_weight, conv_bias[None]], axis=0)
    tap_columns = -(-taps.size // own_rows)
    tap_shard = jnp.pad(taps.reshape(-1), (0, tap_columns * own_rows - taps.size))
    small_width = w_step.shape[1] + 2 + tap_columns
    first_shard = jnp.concatenate(
        [
            w_in,
            w_query,
            w_keyval,
            w_step,
            gain_one[:, None],
            gain_two[:, None],
            tap_shard.reshape(tap_columns, own_rows).T,
            jnp.zeros((own_rows, -small_width % 128), jnp.bfloat16),
        ],
        axis=1,
    )
    first_pair = gather_rows(first_shard)
    small_at = w_in.shape[1] + w_query.shape[1] + w_keyval.shape[1]
    gain_at = small_at + w_step.shape[1]
    gains = jnp.concatenate([half[:, gain_at : gain_at + 2] for half in first_pair], axis=0)
    gain_one_float = gains[:, 0].astype(jnp.float32)
    gain_two_float = gains[:, 1].astype(jnp.float32)
    tap_own, tap_other = (half[:, gain_at + 2 : gain_at + 2 + tap_columns] for half in first_pair)
    first_core = lax.axis_index("core") == 0
    y_size = lax.axis_size("y")
    tap_both = jnp.stack(
        [
            jnp.where(first_core, tap_own, tap_other).reshape(y_size, -1, own_rows, tap_columns),
            jnp.where(first_core, tap_other, tap_own).reshape(y_size, -1, own_rows, tap_columns),
        ],
        axis=1,
    )
    tap_both = jnp.swapaxes(tap_both, 3, 4).reshape(-1, tap_columns * own_rows)[:, : taps.size]
    tap_all = jnp.swapaxes(tap_both.reshape(-1, *taps.shape), 0, 1).reshape(taps.shape[0], channels)
    tap_all = tap_all.astype(jnp.float32)
    conv_float = tap_all[:CONV]
    conv_bias_float = tap_all[CONV]
    out_pair = gather_rows(jnp.concatenate([w_mix_out.T, w_attn_out.T], axis=1))
    up_pair = gather_rows(w_gate_up)
    down_pair = gather_rows(w_down.T)
    piece_index = lax.axis_index(seq_axes)

    normed = rms_norm(inputs, gain_one_float).astype(jnp.bfloat16)
    projected = times_rows(normed, first_pair)
    gate_z = projected[:, :inner_width]
    conv_input = projected[:, inner_width : inner_width + channels].astype(jnp.bfloat16)
    query_at = inner_width + channels
    query_raw = projected[:, query_at : query_at + QHEADS * HEAD_DIM]
    keyval_raw = projected[:, query_at + QHEADS * HEAD_DIM : small_at]
    step_raw = projected[:, small_at:gain_at]
    positions = piece_index * row_count + jnp.arange(row_count, dtype=jnp.int32)
    cosine, sine_table = rope_tables(positions, HEAD_DIM)
    queries = (
        rotate(query_raw.reshape(row_count, QHEADS, HEAD_DIM), cosine, sine_table)
        .astype(jnp.bfloat16)
        .reshape(row_count, KVHEADS, group_size, HEAD_DIM)
    )
    key_rotated = rotate(
        keyval_raw[:, :key_width].reshape(row_count, KVHEADS, HEAD_DIM), cosine, sine_table
    ).reshape(row_count, key_width)
    own_keys = jnp.concatenate([key_rotated, keyval_raw[:, key_width:]], axis=1).astype(
        jnp.bfloat16
    )
    all_keys = lax.all_gather(own_keys, seq_axes, axis=0, tiled=True)

    border = from_behind(conv_input[row_count - (CONV - 1) :], 1)
    extended = jnp.concatenate([border, conv_input], axis=0).astype(jnp.float32)
    inputs_x, input_mat, output_mat, log_decay, step_size = mamba_inputs(
        extended, step_raw, conv_float, conv_bias_float, mamba_heads
    )
    factor, fresh_state = ssd_summary(inputs_x, input_mat, log_decay, step_size)
    carry_state = carried_from_before(*spread_states(fresh_state, factor))
    mixer = mamba_mix(
        inputs_x, input_mat, output_mat, log_decay, step_size, carry_state, gate_z, skip_weight
    ).astype(jnp.bfloat16)
    start_state = (
        jnp.full((KVHEADS, group_size, row_count), masked_score, jnp.float32),
        jnp.zeros((KVHEADS, group_size, row_count), jnp.float32),
        jnp.zeros((KVHEADS, group_size, row_count, HEAD_DIM), jnp.float32),
    )
    best_score, weight_total, weighted = attend_piece(
        start_state, all_keys, jnp.int32(0), queries=queries, query_pos=positions
    )
    attended_heads = weighted / weight_total[..., None]
    log_total = best_score + jnp.log(weight_total)
    attention_rows = (
        jnp.transpose(attended_heads, (2, 0, 1, 3))
        .reshape(row_count, QHEADS * HEAD_DIM)
        .astype(jnp.bfloat16)
    )
    branches = jnp.concatenate([mixer, attention_rows], axis=1)
    hidden = inputs + times_rows_back(branches, out_pair)
    normed_two = rms_norm(hidden, gain_two_float).astype(jnp.bfloat16)
    gate_up = times_rows(normed_two, up_pair)
    gate_part = gate_up[:, :FF]
    up_part = gate_up[:, FF:]
    activated = (jax.nn.silu(gate_part) * up_part).astype(jnp.bfloat16)
    result = hidden + times_rows_back(activated, down_pair)
    output = usual_order(result.astype(jnp.bfloat16))[None]

    grad_out_float = grad_output.astype(jnp.float32)
    grad_activated = times_rows(grad_output, down_pair)
    grad_w_down = scatter_product(grad_output, activated)
    gate_sigmoid = jax.nn.sigmoid(gate_part)
    grad_gate = grad_activated * up_part * gate_sigmoid * (1.0 + gate_part * (1.0 - gate_sigmoid))
    grad_up = grad_activated * gate_part * gate_sigmoid
    grad_gate_up = jnp.concatenate([grad_gate, grad_up], axis=1).astype(jnp.bfloat16)
    grad_w_gate_up = scatter_product(normed_two, grad_gate_up)
    grad_normed_two = times_rows_back(grad_gate_up, up_pair)
    _, pull_two = jax.vjp(rms_norm, hidden, gain_two_float)
    grad_hidden_norm, grad_gain_two = pull_two(grad_normed_two)
    grad_hidden = grad_out_float + grad_hidden_norm
    grad_branch = grad_hidden.astype(jnp.bfloat16)
    grad_w_out = scatter_product(grad_branch, branches)
    grad_branches = times_rows(grad_branch, out_pair)
    grad_mixer = grad_branches[:, :inner_width]
    grad_attention = grad_branches[:, inner_width:].astype(jnp.bfloat16)
    grad_heads = grad_attention.reshape(row_count, KVHEADS, group_size, HEAD_DIM)
    row_dots = jnp.einsum("tgjd,gjtd->gjt", grad_heads.astype(jnp.float32), attended_heads)
    total_rows = all_keys.shape[0]
    block_rows = min(key_block, total_rows)
    stacked = all_keys.reshape(total_rows // block_rows, block_rows, 2 * key_width)
    firsts = block_rows * jnp.arange(total_rows // block_rows, dtype=jnp.int32)
    score_scale = 1.0 / math.sqrt(HEAD_DIM)
    last_query = positions[-1]

    def backward_block(grad_query_acc, item_pair):
        key_rows, first_key = item_pair

        def compute(acc_now):
            key_heads = key_rows[:, :key_width].reshape(block_rows, KVHEADS, HEAD_DIM)
            value_heads = key_rows[:, key_width:].reshape(block_rows, KVHEADS, HEAD_DIM)
            scores = (
                jnp.einsum("tgjd,sgd->gjts", queries, key_heads, preferred_element_type=jnp.float32)
                * score_scale
            )
            key_pos = first_key + jnp.arange(block_rows, dtype=jnp.int32)
            allowed = key_pos[None, :] <= positions[:, None]
            scores = jnp.where(allowed, scores, masked_score)
            soft_weights = jnp.where(allowed, jnp.exp(scores - log_total[..., None]), 0.0)
            grad_weights = jnp.einsum(
                "tgjd,sgd->gjts", grad_heads, value_heads, preferred_element_type=jnp.float32
            )
            grad_scores = (soft_weights * (grad_weights - row_dots[..., None])).astype(jnp.bfloat16)
            acc_next = (
                acc_now
                + jnp.einsum(
                    "gjts,sgd->gjtd", grad_scores, key_heads, preferred_element_type=jnp.float32
                )
                * score_scale
            )
            grad_key = (
                jnp.einsum(
                    "gjts,tgjd->sgd", grad_scores, queries, preferred_element_type=jnp.float32
                )
                * score_scale
            )
            grad_value = jnp.einsum(
                "gjts,tgjd->sgd",
                soft_weights.astype(jnp.bfloat16),
                grad_heads,
                preferred_element_type=jnp.float32,
            )
            return (
                acc_next,
                jnp.concatenate(
                    [
                        grad_key.reshape(block_rows, key_width),
                        grad_value.reshape(block_rows, key_width),
                    ],
                    axis=1,
                ),
            )

        def skipped(acc_now):
            return (acc_now, jnp.zeros((block_rows, 2 * key_width), jnp.float32))

        return lax.cond(first_key <= last_query, compute, skipped, grad_query_acc)

    grad_query_heads, grad_key_rows = lax.scan(
        backward_block,
        jnp.zeros((KVHEADS, group_size, row_count, HEAD_DIM), jnp.float32),
        (stacked, firsts),
    )
    own_grads = sum_key_grads(grad_key_rows.reshape(total_rows, 2 * key_width))
    grad_query_rows = jnp.transpose(grad_query_heads, (2, 0, 1, 3)).reshape(
        row_count, QHEADS, HEAD_DIM
    )
    grad_query = (
        rotate(grad_query_rows, cosine, -sine_table)
        .reshape(row_count, QHEADS * HEAD_DIM)
        .astype(jnp.bfloat16)
    )
    grad_key_raw = rotate(
        own_grads[:, :key_width].reshape(row_count, KVHEADS, HEAD_DIM), cosine, -sine_table
    ).reshape(row_count, key_width)
    grad_keyval = jnp.concatenate([grad_key_raw, own_grads[:, key_width:]], axis=1).astype(
        jnp.bfloat16
    )
    primal_out, pull_mamba, aux_values = jax.vjp(
        mamba_local,
        extended,
        step_raw,
        gate_z,
        conv_float,
        conv_bias_float,
        mamba_heads,
        skip_weight,
        carry_state,
        has_aux=True,
    )
    output_saved, cumulative = aux_values
    grad_y = (grad_mixer * jax.nn.silu(gate_z)).reshape(row_count, MHEADS, MHEAD_DIM)
    from_output = jnp.einsum(
        "th,thp,tn->hpn", jnp.exp(cumulative), grad_y, output_saved, precision=highest_precision
    )
    grad_end = carried_from_after(*spread_states(from_output, jnp.exp(cumulative[-1])))
    (
        grad_extended,
        grad_step_raw,
        grad_gate_z,
        grad_conv_weight,
        grad_conv_bias,
        grad_head_params,
        grad_skip,
        _,
    ) = pull_mamba((grad_mixer, grad_end))
    rim_back = from_behind(grad_extended[: CONV - 1], -1)
    grad_conv_input = grad_extended[CONV - 1 :] + jnp.concatenate(
        [jnp.zeros((row_count - (CONV - 1), grad_extended.shape[1]), jnp.float32), rim_back], axis=0
    )
    grad_gate_low = grad_gate_z.astype(jnp.bfloat16)
    grad_rest = jnp.concatenate(
        [
            grad_conv_input.astype(jnp.bfloat16),
            grad_query,
            grad_keyval,
            grad_step_raw.astype(jnp.bfloat16),
        ],
        axis=1,
    )
    grad_w_gate = scatter_product(normed, grad_gate_low)
    grad_w_rest = scatter_product(normed, grad_rest)
    grad_all = jnp.concatenate(
        [
            grad_gate_low,
            grad_rest,
            jnp.zeros((row_count, first_shard.shape[1] - gain_at), jnp.bfloat16),
        ],
        axis=1,
    )
    grad_normed = times_rows_back(grad_all, first_pair)
    _, pull_one = jax.vjp(rms_norm, inputs, gain_one_float)
    grad_input_norm, grad_gain_one = pull_one(grad_normed)
    input_grad = usual_order(grad_hidden + grad_input_norm)[None]

    gain_grads = usual_order(jnp.stack([grad_gain_one, grad_gain_two]))
    tap_grads = jnp.concatenate([grad_conv_weight, grad_conv_bias[None]], axis=0)
    summed_taps = sum_everywhere(
        (jnp.concatenate([tap_grads.reshape(-1), grad_head_params.reshape(-1), grad_skip]))
    )
    summed_gains = sum_everywhere(gain_grads)
    place = lax.axis_index(("y", "core", "z", "x"))
    own_gains = lax.dynamic_slice_in_dim(summed_gains, place * own_rows, own_rows, 1)
    own_channels = conv_weight.shape[1]
    own_taps = lax.dynamic_slice_in_dim(
        summed_taps[: tap_grads.size].reshape(tap_grads.shape),
        place * own_channels,
        own_channels,
        1,
    )
    head_grad = summed_taps[tap_grads.size : tap_grads.size + mamba_heads.size]
    skip_grad = summed_taps[tap_grads.size + mamba_heads.size :]
    rest_query = channels + w_query.shape[1]
    rest_keyval = rest_query + w_keyval.shape[1]
    return (
        output,
        input_grad,
        own_gains[0],
        jnp.concatenate([grad_w_gate, grad_w_rest[:, :channels]], axis=1),
        grad_w_rest[:, rest_keyval:],
        own_taps[:CONV],
        own_taps[CONV],
        head_grad.reshape(mamba_heads.shape),
        skip_grad,
        grad_w_rest[:, channels:rest_query],
        grad_w_rest[:, rest_query:rest_keyval],
        grad_w_out[:, inner_width:].T,
        grad_w_out[:, :inner_width].T,
        own_gains[1],
        grad_w_gate_up,
        grad_w_down.T,
    )


def solution(mesh):
    dp, seq = mesh.shape["dp"], mesh.shape["seq"]
    by_axis = Mesh(mesh.devices.reshape(dp // 2, 2, seq // 2, 2), ("y", "core", "z", "x"))
    every = ("y", "core", "z", "x")
    pieces = P(("y", "core"), seq_axes, None)
    rows = P(every, None)
    columns = P(None, every)
    return jax.shard_map(
        on_device,
        mesh=by_axis,
        in_specs=(
            pieces,
            P(every),
            rows,
            rows,
            columns,
            P(every),
            P(),
            P(),
            rows,
            rows,
            columns,
            columns,
            P(every),
            rows,
            columns,
            pieces,
        ),
        out_specs=(
            pieces,
            pieces,
            P(every),
            rows,
            rows,
            columns,
            P(every),
            P(),
            P(),
            rows,
            rows,
            columns,
            columns,
            P(every),
            rows,
            columns,
        ),
        check_vma=False,
    )
```

```python
import math

import jax
import jax.experimental.pallas as pl
import jax.experimental.pallas.tpu as pltpu
import jax.numpy as jnp
from jax import lax
from jax.sharding import Mesh
from jax.sharding import PartitionSpec as P

MHEADS = 24
MHEAD_DIM = 64
STATE = 128
CONV = 4
QHEADS = 8
KVHEADS = 2
HEAD_DIM = 64
FF = 2048


norm_epsilon = 1e-06
rope_base = 100000000000.0
masked_score = -1e30
highest_precision = lax.Precision.HIGHEST
seq_axes = ("z", "x")
every_axis = ("y", "core", "z", "x")


def rms_norm(values, gain_vector):
    return (
        values
        * lax.rsqrt(jnp.mean(values * values, axis=-1, keepdims=True) + norm_epsilon)
        * gain_vector
    )


def outer_product(left, right):
    return lax.dot_general(
        left, right, (((0,), (0,)), ((), ())), preferred_element_type=jnp.float32
    )


def back_product(grad_rows, weight_matrix):
    return lax.dot_general(
        grad_rows, weight_matrix, (((1,), (1,)), ((), ())), preferred_element_type=jnp.float32
    )


def turn_columns(positions):
    half = HEAD_DIM // 2
    exponents = jnp.arange(half).astype(jnp.float32) * (2.0 / HEAD_DIM)
    frequency = rope_base ** (-exponents)
    angles = frequency[:, None] * positions.astype(jnp.float32)[None, :]
    return (jnp.cos(angles), jnp.sin(angles))


def turn_rows(values, cosine, sine):
    half = HEAD_DIM // 2
    heads = values.reshape(-1, 2, half, values.shape[1])
    first, second = heads[:, 0], heads[:, 1]
    turned = [first * cosine - second * sine, second * cosine + first * sine]
    return jnp.stack(turned, axis=1).reshape(values.shape)


def conv_act(extended, conv_weight, conv_bias):
    row_count = extended.shape[0] - (CONV - 1)
    conv_sum = conv_bias[None, :] + conv_weight[0][None, :] * extended[0:row_count]
    for offset in range(1, CONV):
        conv_sum = conv_sum + conv_weight[offset][None, :] * extended[offset : offset + row_count]
    return jax.nn.silu(conv_sum)


log2_e = math.log2(math.e)
compiler_room = pltpu.CompilerParams(vmem_limit_bytes=48 * 1024 * 1024)


def group_rows(rows, head):
    group = head // (QHEADS // KVHEADS)
    own = rows[head * HEAD_DIM : (head + 1) * HEAD_DIM]
    blank = jnp.zeros_like(own)
    return jnp.concatenate([own if g == group else blank for g in range(KVHEADS)], axis=0)


def plain_dot(left, right):
    return jnp.dot(left, right, preferred_element_type=jnp.float32)


def hidden_keys(rows):
    key_at = lax.broadcasted_iota(jnp.int32, (rows, rows), 0)
    query_at = lax.broadcasted_iota(jnp.int32, (rows, rows), 1)
    return key_at > query_at


def slot_of(index, place_ref):
    z, x = lax.shift_right_logical(index, 1), lax.bitwise_and(index, 1)
    return 2 * (place_ref[0] - z) + lax.bitwise_xor(x, place_ref[1])


def attend_kernel(place_ref, query_ref, key_ref, value_ref, out_ref, log_ref, best_ref, sum_ref):
    rows = query_ref.shape[1]
    scale = log2_e / math.sqrt(HEAD_DIM)
    group_size = QHEADS // KVHEADS

    def scores_of(keys, head):
        return plain_dot(keys, group_rows(query_ref, head)) * scale

    def values_of(piece, head):
        group = head // group_size
        return value_ref[piece, group * HEAD_DIM : (group + 1) * HEAD_DIM, :]

    own = key_ref[0]
    for head in range(QHEADS):
        scores = jnp.where(hidden_keys(rows), masked_score, scores_of(own, head))
        best = jnp.max(scores, axis=0, keepdims=True)
        weights = jnp.exp2(scores - best)
        best_ref[head : head + 1, :] = best
        sum_ref[head : head + 1, :] = jnp.sum(weights, axis=0, keepdims=True)
        out_ref[head * HEAD_DIM : (head + 1) * HEAD_DIM, :] = plain_dot(
            values_of(0, head), weights.astype(jnp.bfloat16)
        )

    def piece_step(index, carry):
        piece = slot_of(index, place_ref)
        keys = key_ref[piece]
        for head in range(QHEADS):
            scores = scores_of(keys, head)
            old = best_ref[head : head + 1, :]
            best = jnp.maximum(old, jnp.max(scores, axis=0, keepdims=True))
            fade = jnp.exp2(old - best)
            weights = jnp.exp2(scores - best)
            best_ref[head : head + 1, :] = best
            sum_ref[head : head + 1, :] = sum_ref[head : head + 1, :] * fade + jnp.sum(
                weights, axis=0, keepdims=True
            )
            span = slice(head * HEAD_DIM, (head + 1) * HEAD_DIM)
            out_ref[span, :] = out_ref[span, :] * fade + plain_dot(
                values_of(piece, head), weights.astype(jnp.bfloat16)
            )
        return carry

    lax.fori_loop(0, 2 * place_ref[0] + place_ref[1], piece_step, 0)
    total = sum_ref[...]
    log_ref[...] = best_ref[...] + jnp.log2(total)
    for head in range(QHEADS):
        span = slice(head * HEAD_DIM, (head + 1) * HEAD_DIM)
        out_ref[span, :] = out_ref[span, :] / total[head : head + 1, :]


def in_vmem(count):
    return [pl.BlockSpec(memory_space=pltpu.VMEM)] * count


def attend(place, queries, keys, values):
    rows = queries.shape[1]
    flops = 4 * queries.size * rows * keys.shape[0]
    return pl.pallas_call(
        attend_kernel,
        out_shape=(
            jax.ShapeDtypeStruct(queries.shape, jnp.float32),
            jax.ShapeDtypeStruct((QHEADS, rows), jnp.float32),
        ),
        in_specs=[pl.BlockSpec(memory_space=pltpu.SMEM)] + in_vmem(3),
        out_specs=tuple(in_vmem(2)),
        scratch_shapes=[pltpu.VMEM((QHEADS, rows), jnp.float32)] * 2,
        compiler_params=compiler_room,
        cost_estimate=pl.CostEstimate(
            flops=flops,
            bytes_accessed=2 * (keys.size + values.size),
            transcendentals=flops // 256,
        ),
        name="attend",
    )(place, queries, keys, values)


def attend_back_kernel(
    place_ref,
    query_ref,
    query_rows_ref,
    grad_ref,
    grad_rows_ref,
    out_ref,
    log_ref,
    key_ref,
    key_cols_ref,
    value_ref,
    grad_query_ref,
    grad_key_ref,
    dots_ref,
):
    rows = query_ref.shape[1]
    key_width = KVHEADS * HEAD_DIM
    group_size = QHEADS // KVHEADS
    scale = log2_e / math.sqrt(HEAD_DIM)
    grad_query_ref[...] = jnp.zeros_like(grad_query_ref)
    for head in range(QHEADS):
        span = slice(head * HEAD_DIM, (head + 1) * HEAD_DIM)
        dots_ref[head : head + 1, :] = jnp.sum(
            grad_ref[span, :].astype(jnp.float32) * out_ref[span, :], axis=0, keepdims=True
        )

    def one_piece(piece, own):
        keys = key_ref[piece]
        values = value_ref[piece]
        grad_keys = jnp.zeros((rows, key_width), jnp.float32)
        grad_values = jnp.zeros((rows, key_width), jnp.float32)
        for head in range(QHEADS):
            group = head // group_size
            scores = plain_dot(keys, group_rows(query_ref, head)) * scale
            weights = jnp.exp2(scores - log_ref[head : head + 1, :])
            if own:
                weights = jnp.where(hidden_keys(rows), 0.0, weights)
            grad_weights = plain_dot(values, group_rows(grad_ref, head))
            grad_scores = (weights * (grad_weights - dots_ref[head : head + 1, :])).astype(
                jnp.bfloat16
            )
            span = slice(head * HEAD_DIM, (head + 1) * HEAD_DIM)
            grad_query_ref[span, :] += plain_dot(
                key_cols_ref[piece, group * HEAD_DIM : (group + 1) * HEAD_DIM, :], grad_scores
            )
            grad_keys += plain_dot(grad_scores, query_rows_ref[head])
            grad_values += plain_dot(weights.astype(jnp.bfloat16), grad_rows_ref[head])
        grad_key_ref[piece, :, :key_width] = grad_keys * (1.0 / math.sqrt(HEAD_DIM))
        grad_key_ref[piece, :, key_width:] = grad_values

    def clear(piece, carry):
        grad_key_ref[piece] = jnp.zeros(grad_key_ref.shape[1:], jnp.float32)
        return carry

    def earlier(index, carry):
        one_piece(slot_of(index, place_ref), False)
        return carry

    lax.fori_loop(1, key_ref.shape[0], clear, 0)
    one_piece(0, True)
    lax.fori_loop(0, 2 * place_ref[0] + place_ref[1], earlier, 0)
    grad_query_ref[...] = grad_query_ref[...] * (1.0 / math.sqrt(HEAD_DIM))


def padded_heads(rows):
    group_size = QHEADS // KVHEADS
    heads = []
    for head in range(QHEADS):
        group = head // group_size
        own = rows[:, head * HEAD_DIM : (head + 1) * HEAD_DIM]
        after = (KVHEADS - 1 - group) * HEAD_DIM
        heads.append(jnp.pad(own, ((0, 0), (group * HEAD_DIM, after))))
    return jnp.stack(heads)


def attend_back(place, queries, grads, grad_rows, outs, logs, keys, key_cols, values):
    rows = queries.shape[1]
    flops = 10 * queries.size * rows * keys.shape[0]
    return pl.pallas_call(
        attend_back_kernel,
        out_shape=(
            jax.ShapeDtypeStruct(queries.shape, jnp.float32),
            jax.ShapeDtypeStruct((*keys.shape[:2], 2 * keys.shape[2]), jnp.float32),
        ),
        in_specs=[pl.BlockSpec(memory_space=pltpu.SMEM)] + in_vmem(9),
        out_specs=tuple(in_vmem(2)),
        scratch_shapes=[pltpu.VMEM((QHEADS, rows), jnp.float32)],
        compiler_params=compiler_room,
        cost_estimate=pl.CostEstimate(
            flops=flops,
            bytes_accessed=8 * keys.size,
            transcendentals=flops // 640,
        ),
        name="attend_back",
    )(
        place,
        queries,
        padded_heads(queries.T),
        grads,
        padded_heads(grad_rows),
        outs,
        logs,
        keys,
        key_cols,
        values,
    )


ssd_rows = 128


def two_parts(values):
    high = values.astype(jnp.bfloat16)
    rest = values - high.astype(jnp.float32)
    middle = rest.astype(jnp.bfloat16)
    low = (rest - middle.astype(jnp.float32)).astype(jnp.bfloat16)
    return jnp.concatenate([high, middle, low], axis=1)


def head_columns(heads, parts):
    shape = (heads * parts, heads * MHEAD_DIM)
    head = lax.broadcasted_iota(jnp.int32, shape, 0) % heads
    channel = lax.broadcasted_iota(jnp.int32, shape, 1) // MHEAD_DIM
    return jnp.where(head == channel, 1.0, 0.0).astype(jnp.bfloat16)


def widen(values, spread):
    return plain_dot(two_parts(values), spread)


def head_sums(values, spread):
    heads = spread.shape[0]
    high = values.astype(jnp.bfloat16)
    low = (values - high.astype(jnp.float32)).astype(jnp.bfloat16)
    total = nt_dot(high, spread) + nt_dot(low, spread)
    return total


def nt_dot(left, right):
    return lax.dot_general(
        left, right, (((1,), (1,)), ((), ())), preferred_element_type=jnp.float32
    )


def split_pair(pair, axis):
    lane = lax.broadcasted_iota(jnp.int32, pair.shape, 1)
    blank = jnp.zeros_like(pair)
    return jnp.concatenate(
        [jnp.where(lane < MHEAD_DIM, pair, blank), jnp.where(lane < MHEAD_DIM, blank, pair)],
        axis=axis,
    )


def bf(values):
    return values.astype(jnp.bfloat16)


def ssd_kernel(act_ref, cum_ref, cum_rows_ref, step_ref, spread_ref, y_ref, grown_ref, state_ref, tail_ref):
    chunks, rows, inner = y_ref.shape
    spread = spread_ref[...]
    state_ref[...] = jnp.zeros_like(state_ref)
    tail_ref[...] = jnp.zeros_like(tail_ref)
    late = lax.broadcasted_iota(jnp.int32, (rows, rows), 0) >= lax.broadcasted_iota(
        jnp.int32, (rows, rows), 1
    )

    def one_chunk(chunk, before):
        act = act_ref[chunk]
        cum = cum_ref[chunk]
        cum_rows = cum_rows_ref[chunk]
        scaled = act[:, :inner] * widen(step_ref[chunk], spread)
        input_mat = act[:, inner : inner + STATE]
        output_low = bf(act[:, inner + STATE :])
        last = cum[rows - 1 : rows, :]
        grown_ref[chunk] = widen(jnp.exp(cum + before), spread)
        mixing = nt_dot(output_low, bf(input_mat))
        state = state_ref[...]
        from_state = plain_dot(output_low, bf(state)) * widen(jnp.exp(cum), spread)
        scaled_low = bf(scaled)
        for pair in range(MHEADS // 2):
            kernels = []
            for head in (2 * pair, 2 * pair + 1):
                gap = cum[:, head : head + 1] - cum_rows[head : head + 1, :]
                kernels.append(bf(jnp.exp(jnp.where(late, gap, masked_score)) * mixing))
            span = slice(2 * pair * MHEAD_DIM, (2 * pair + 2) * MHEAD_DIM)
            y_ref[chunk, :, span] = from_state[:, span] + plain_dot(
                jnp.concatenate(kernels, axis=1), split_pair(scaled_low[:, span], 0)
            )
        weighted = scaled * widen(jnp.exp(last - cum), spread)
        fade = widen(jnp.exp(jnp.broadcast_to(last, (8, last.shape[1]))), spread)[:1]
        state_ref[...] = state * fade + plain_dot(bf(input_mat.T), bf(weighted))
        return before + last

    total = lax.fori_loop(0, chunks, one_chunk, jnp.zeros((1, cum_ref.shape[2]), jnp.float32))
    tail_ref[...] = widen(jnp.exp(jnp.broadcast_to(total, (8, total.shape[1]))), spread)


def by_chunks(values):
    return values.reshape(-1, math.gcd(values.shape[0], ssd_rows), values.shape[1])


def ssd_local(act, cum, step_size):
    act, cum, step_size = by_chunks(act), by_chunks(cum), by_chunks(step_size)
    chunks, rows, _ = act.shape
    inner = MHEADS * MHEAD_DIM
    return pl.pallas_call(
        ssd_kernel,
        out_shape=(
            jax.ShapeDtypeStruct((chunks, rows, inner), jnp.float32),
            jax.ShapeDtypeStruct((chunks, rows, inner), jnp.float32),
            jax.ShapeDtypeStruct((STATE, inner), jnp.float32),
            jax.ShapeDtypeStruct((8, inner), jnp.float32),
        ),
        in_specs=in_vmem(5),
        out_specs=tuple(in_vmem(4)),
        compiler_params=compiler_room,
        cost_estimate=pl.CostEstimate(
            flops=chunks * rows * inner * 2000, bytes_accessed=act.size * 16, transcendentals=0
        ),
        name="ssd",
    )(act, cum, jnp.swapaxes(cum, 1, 2), step_size, head_columns(MHEADS, 3))


def ssd_back_kernel(
    act_ref,
    cum_ref,
    cum_rows_ref,
    step_ref,
    grad_ref,
    carry_ref,
    grad_end_ref,
    skip_ref,
    spread_ref,
    grad_act_ref,
    grad_step_ref,
    grad_log_ref,
    grad_skip_ref,
    states_ref,
    grad_state_ref,
    sums_ref,
):
    chunks, rows, _ = act_ref.shape
    inner = grad_ref.shape[2]
    heads = cum_ref.shape[2]
    spread = spread_ref[...]
    one_spread = spread[:heads]
    at_row = lax.broadcasted_iota(jnp.int32, (rows, rows), 0)
    at_column = lax.broadcasted_iota(jnp.int32, (rows, rows), 1)

    def fade_of(last):
        return widen(jnp.exp(jnp.broadcast_to(last, (8, heads))), spread)[:1]

    states_ref[0] = carry_ref[...]
    for chunk in range(chunks - 1):
        cum = cum_ref[chunk]
        last = cum[rows - 1 : rows, :]
        act = act_ref[chunk]
        weighted = act[:, :inner] * widen(jnp.exp(last - cum) * step_ref[chunk], spread)
        states_ref[chunk + 1] = states_ref[chunk] * fade_of(last) + plain_dot(
            bf(act[:, inner : inner + STATE].T), bf(weighted)
        )
    grad_state_ref[...] = grad_end_ref[...]
    grad_skip_ref[...] = jnp.zeros_like(grad_skip_ref)
    sums_ref[...] = jnp.zeros_like(sums_ref)

    def one_chunk(turn, carried):
        chunk = chunks - 1 - turn
        act = act_ref[chunk]
        cum = cum_ref[chunk]
        cum_rows = cum_rows_ref[chunk]
        step = step_ref[chunk]
        grad_y = grad_ref[chunk]
        last = cum[rows - 1 : rows, :]
        inputs_x = act[:, :inner]
        step_wide = widen(step, spread)
        tail = jnp.exp(last - cum)
        tail_wide = widen(tail, spread)
        scaled = inputs_x * step_wide
        scaled_low = bf(scaled)
        grad_low = bf(grad_y)
        input_low = bf(act[:, inner : inner + STATE])
        output_mat = act[:, inner + STATE :]
        output_low = bf(output_mat)
        state = states_ref[chunk]
        state_low = bf(state)
        grad_state = grad_state_ref[...]
        grad_state_low = bf(grad_state)

        grown_grad = grad_y * widen(jnp.exp(cum), spread)
        grown_low = bf(grown_grad)
        from_row = head_sums(grown_grad * plain_dot(output_low, state_low), one_spread)
        grad_output = nt_dot(grown_low, state_low)
        back = plain_dot(input_low, grad_state_low)
        from_column = head_sums(scaled * back, one_spread) * tail
        grad_input = nt_dot(bf(scaled * tail_wide), grad_state_low)
        fade = fade_of(last)
        both = jnp.sum(grad_state * state, axis=0, keepdims=True) * fade
        from_last = head_sums(jnp.broadcast_to(both, (8, inner)), one_spread)[:1]
        grad_state_ref[...] = grad_state * fade + plain_dot(bf(output_mat.T), grown_low)

        mixing = nt_dot(input_low, output_low)
        grad_mixing = jnp.zeros((rows, rows), jnp.float32)
        column_sums = jnp.zeros((rows, rows), jnp.float32)
        grad_step = jnp.zeros((rows, rows), jnp.float32)
        for pair in range(heads // 2):
            span = slice(2 * pair * MHEAD_DIM, (2 * pair + 2) * MHEAD_DIM)
            apart = split_pair(grad_low[:, span], 0)
            grad_kernels = nt_dot(scaled_low[:, span], apart)
            kernels = []
            for side in range(2):
                head = 2 * pair + side
                gap = cum_rows[head : head + 1, :] - cum[:, head : head + 1]
                decay = jnp.exp(jnp.where(at_row <= at_column, gap, masked_score))
                part = grad_kernels[:, side * rows : (side + 1) * rows] * decay
                grad_mixing = grad_mixing + part
                moved = part * mixing
                sums_ref[head : head + 1, :] = jnp.sum(moved, axis=0, keepdims=True)
                column = jnp.sum(moved, axis=1, keepdims=True)
                column_sums = jnp.where(at_column == head, column, column_sums)
                kernels.append(bf(decay * mixing))
            grad_scaled = plain_dot(jnp.concatenate(kernels, axis=1), apart)
            grad_scaled = grad_scaled + back[:, span] * tail_wide[:, span]
            grad_act_ref[chunk, :, span] = (
                grad_scaled * step_wide[:, span] + skip_ref[:, span] * grad_y[:, span]
            )
            by_step = grad_scaled * inputs_x[:, span]
            lane = lax.broadcasted_iota(jnp.int32, by_step.shape, 1)
            for side in range(2):
                mine = jnp.where((lane < MHEAD_DIM) == (side == 0), by_step, 0.0)
                column = jnp.sum(mine, axis=1, keepdims=True)
                grad_step = jnp.where(at_column == 2 * pair + side, column, grad_step)
        grad_mixing_low = bf(grad_mixing)
        grad_act_ref[chunk, :, inner : inner + STATE] = grad_input + plain_dot(
            grad_mixing_low, output_low
        )
        grad_act_ref[chunk, :, inner + STATE :] = grad_output + plain_dot(
            bf(grad_mixing.T), input_low
        )
        grad_step_ref[chunk] = grad_step[:, :heads]
        row_sums = sums_ref[...].T[:, :heads]
        ahead = row_sums - column_sums[:, :heads] + from_row
        from_here = jnp.where(at_row <= at_column, 1.0, 0.0)
        before = jnp.where(at_row > at_column, 1.0, 0.0)
        grad_log_ref[chunk] = (
            jnp.dot(from_here, ahead, precision=highest_precision)
            + jnp.dot(before, from_column, precision=highest_precision)
            + from_last
        )
        grad_skip_ref[...] += jnp.sum(inputs_x * grad_y, axis=0, keepdims=True)
        return carried

    lax.fori_loop(0, chunks, one_chunk, 0)


def ssd_back(act, cum, step_size, grad_y, carry_state, grad_end, skip_row):
    shape = act.shape
    act, cum, step_size, grad_y = (by_chunks(a) for a in (act, cum, step_size, grad_y))
    chunks, rows, width = act.shape
    inner = MHEADS * MHEAD_DIM
    grad_act, grad_step, grad_log, grad_skip = pl.pallas_call(
        ssd_back_kernel,
        out_shape=(
            jax.ShapeDtypeStruct(act.shape, jnp.float32),
            jax.ShapeDtypeStruct(cum.shape, jnp.float32),
            jax.ShapeDtypeStruct(cum.shape, jnp.float32),
            jax.ShapeDtypeStruct((1, inner), jnp.float32),
        ),
        in_specs=in_vmem(9),
        out_specs=tuple(in_vmem(4)),
        scratch_shapes=[
            pltpu.VMEM((chunks, STATE, inner), jnp.float32),
            pltpu.VMEM((STATE, inner), jnp.float32),
            pltpu.VMEM((rows, rows), jnp.float32),
        ],
        compiler_params=compiler_room,
        cost_estimate=pl.CostEstimate(
            flops=chunks * rows * inner * 5000, bytes_accessed=act.size * 16, transcendentals=0
        ),
        name="ssd_back",
    )(
        act,
        cum,
        jnp.swapaxes(cum, 1, 2),
        step_size,
        grad_y,
        carry_state,
        grad_end,
        skip_row,
        head_columns(MHEADS, 3),
    )
    flat = (shape[0], MHEADS)
    return grad_act.reshape(shape), grad_step.reshape(flat), grad_log.reshape(flat), grad_skip


def shifted(block, axis, distance):
    count = lax.axis_size(axis)
    return lax.ppermute(block, axis, [(i, (i + distance) % count) for i in range(count)])


def moved_along(block, axis, distance):
    count = lax.axis_size(axis)
    route = [(i, i + distance) for i in range(count) if 0 <= i + distance < count]
    return lax.ppermute(block, axis, route)


def width_order(width):
    sizes = {axis: lax.axis_size(axis) for axis in every_axis}
    rows = width // math.prod(sizes.values())
    rest = lax.broadcasted_iota(jnp.int32, (width, width), 1)
    inside, rest = rest % rows, rest // rows
    owner = {}
    for axis in ("z", "x", "y", "core"):
        owner[axis] = (rest % sizes[axis] + lax.axis_index(axis)) % sizes[axis]
        rest = rest // sizes[axis]
    usual = owner["y"]
    for axis in ("core", "z", "x"):
        usual = usual * sizes[axis] + owner[axis]
    usual = usual * rows + inside
    return (lax.broadcasted_iota(jnp.int32, (width, width), 0) == usual).astype(jnp.bfloat16)


def gather_stages(shard, first, after=None):
    if after is not None:
        shard, _ = lax.optimization_barrier((shard, after))
    parts = [shard] + [shifted(shard, "z", -k) for k in range(1, lax.axis_size("z"))]
    started = parts[-1]
    block = jnp.concatenate(parts, axis=0)[None, None]
    for axis in (first, "xy".replace(first, "")):
        parts = [block] + [shifted(block, axis, -k) for k in range(1, lax.axis_size(axis))]
        block = jnp.concatenate(parts, axis="yx".index(axis))
    own = block.reshape(-1, shard.shape[1])
    return (own, shifted(own, "core", 1)), started


def times_rows(values, pair):
    half = values.shape[1] // 2
    return plain_dot(values[:, :half], pair[0]) + plain_dot(values[:, half:], pair[1])


def times_rows_back(values, pair):
    return jnp.concatenate([back_product(values, pair[0]), back_product(values, pair[1])], axis=1)


def keep_own(total, axis, dim):
    kept = lax.index_in_dim(total, 0, dim, False)
    for step in range(1, lax.axis_size(axis)):
        part = lax.index_in_dim(total, step, dim, False)
        kept = kept + shifted(part.astype(jnp.bfloat16), axis, step).astype(jnp.float32)
    return kept


def scatter_product(left, right, first):
    half = left.shape[1] // 2
    sizes = [lax.axis_size(axis) for axis in ("y", "x", "z")]
    sent = outer_product(left[:, half:], right).astype(jnp.bfloat16)
    received = shifted(sent, "core", 1)
    total = outer_product(left[:, :half], right) + received.astype(jnp.float32)
    total = total.reshape(*sizes, -1, right.shape[1])
    for axis, dim in ((("x", 1), ("y", 0)) if first == "x" else (("y", 0), ("x", 0))):
        total = keep_own(total, axis, dim)
    return keep_own(total, "z", 0)


def sum_everywhere(values):
    for axis in ("core", "x", "y", "z"):
        count = lax.axis_size(axis)
        step = 1
        while step < count:
            values = values + lax.ppermute(values, axis, [(i, i ^ step) for i in range(count)])
            step *= 2
    return values


def carried(state, tail, direction):
    depth, width = state.shape
    half = width // 2
    at_x = lax.axis_index("x")
    is_second = (at_x == 1) if direction == 1 else (at_x == 0)
    packed = jnp.concatenate([state, tail], axis=0).astype(jnp.bfloat16)
    other = shifted(packed, "x", 1).astype(jnp.float32)
    own = packed.astype(jnp.float32)
    first = jnp.where(is_second, other, own)
    second = jnp.where(is_second, own, other)
    first_state, first_tail = first[:depth], first[depth : depth + 1]
    second_tail = second[depth : depth + 1]
    pair = jnp.concatenate(
        [second_tail * first_state + second[:depth], first[depth:] * second[depth:]], axis=0
    )
    mine = jnp.where(at_x == 0, pair[:, :half], pair[:, half:]).astype(jnp.bfloat16)
    total = jnp.zeros((depth, half), jnp.float32)
    fade = jnp.ones((1, half), jnp.float32)
    for step in range(1, lax.axis_size("z")):
        got = moved_along(mine, "z", direction * step).astype(jnp.float32)
        total = total + fade * got[:depth]
        fade = fade * got[depth : depth + 1]
    total = total.astype(jnp.bfloat16)
    rest = shifted(total, "x", 1)
    left, right = jnp.where(at_x == 0, total, rest), jnp.where(at_x == 0, rest, total)
    carry = jnp.concatenate([left, right], axis=1).astype(jnp.float32)
    return jnp.where(is_second, first_tail * carry + first_state, carry)


def gather_keys(own):
    slots = []
    for step in range(lax.axis_size("z")):
        block = moved_along(own, "z", step) if step else own
        slots += [block, shifted(block, "x", 1)]
    return jnp.stack(slots)


def sum_key_grads(slots):
    total = slots.reshape(-1, 2, *slots.shape[1:])
    swapped = shifted(total[:, 1].astype(jnp.bfloat16), "x", 1)
    kept = total[:, 0] + swapped.astype(jnp.float32)
    own = kept[0]
    for step in range(1, kept.shape[0]):
        own = own + moved_along(kept[step].astype(jnp.bfloat16), "z", -step).astype(jnp.float32)
    return own


def on_device(
    tokens,
    gain_one,
    w_in,
    w_step,
    conv_weight,
    conv_bias,
    mamba_heads,
    skip_weight,
    w_query,
    w_keyval,
    w_attn_out,
    w_mix_out,
    gain_two,
    w_gate_up,
    w_down,
    cotangent,
):
    width = tokens.shape[2]
    row_count = tokens.shape[1]
    inner_width = MHEADS * MHEAD_DIM
    device_count = math.prod(lax.axis_size(axis) for axis in every_axis)
    channels = conv_weight.shape[1] * device_count
    key_width = KVHEADS * HEAD_DIM
    query_width = QHEADS * HEAD_DIM
    own_rows = gain_one.shape[0]
    at_z, at_x = lax.axis_index("z"), lax.axis_index("x")
    place = jnp.stack([at_z, at_x]).astype(jnp.int32)

    taps = jnp.concatenate([conv_weight, conv_bias[None]], axis=0)
    tap_columns = -(-taps.size // own_rows)
    tap_shard = jnp.pad(taps.reshape(-1), (0, tap_columns * own_rows - taps.size))
    step_at = channels + w_keyval.shape[1]
    gain_at = step_at + w_step.shape[1]
    tap_at = gain_at + 2
    conv_shard = jnp.concatenate(
        [
            w_in[:, inner_width:],
            w_keyval,
            w_step,
            gain_one[:, None],
            gain_two[:, None],
            tap_shard.reshape(tap_columns, own_rows).T,
            jnp.zeros((own_rows, -(tap_at + tap_columns) % 128), jnp.bfloat16),
        ],
        axis=1,
    )
    gate_shard = jnp.concatenate([w_in[:, :inner_width], w_query], axis=1)
    out_shard = jnp.concatenate([w_mix_out.T, w_attn_out.T], axis=1)
    out_half = out_shard.shape[1] // 2
    down_shard = w_down.T
    down_half = down_shard.shape[1] // 2
    conv_pair, conv_started = gather_stages(conv_shard, "x")
    gate_pair, gate_started = gather_stages(gate_shard, "y")
    started = (conv_started, gate_started)
    out_pair_a, out_started = gather_stages(out_shard[:, :out_half], "x", started)
    out_pair_b, out_started_b = gather_stages(out_shard[:, out_half:], "y", started)
    started = (out_started, out_started_b)
    ff_pair_a, ff_started = gather_stages(w_gate_up[:, :FF], "x", started)
    ff_pair_b, ff_started_b = gather_stages(w_gate_up[:, FF:], "y", started)
    started = (ff_started, ff_started_b)
    down_pair_a, _ = gather_stages(down_shard[:, :down_half], "x", started)
    down_pair_b, _ = gather_stages(down_shard[:, down_half:], "y", started)

    order = width_order(width)
    inputs = plain_dot(tokens[0], order)
    grad_output = plain_dot(cotangent[0], order).astype(jnp.bfloat16)
    small = jnp.concatenate([half[:, gain_at : tap_at + tap_columns] for half in conv_pair], axis=0)
    gain_one_float = small[:, 0].astype(jnp.float32)
    gain_two_float = small[:, 1].astype(jnp.float32)
    tap_all = plain_dot(order, small[:, 2:]).reshape(device_count, own_rows, tap_columns)
    tap_all = jnp.swapaxes(tap_all, 1, 2).reshape(device_count, -1)[:, : taps.size]
    tap_all = jnp.swapaxes(tap_all.reshape(-1, *taps.shape), 0, 1).reshape(taps.shape[0], channels)

    normed = rms_norm(inputs, gain_one_float).astype(jnp.bfloat16)
    conv_projected = times_rows(normed, conv_pair)
    conv_input = conv_projected[:, :channels].astype(jnp.bfloat16)
    keyval_raw = conv_projected[:, channels:step_at]
    step_raw = conv_projected[:, step_at:gain_at]
    positions = (at_z * lax.axis_size("x") + at_x) * row_count + jnp.arange(
        row_count, dtype=jnp.int32
    )
    cosine, sine = turn_columns(positions)
    own_keys = turn_rows(keyval_raw[:, :key_width].T, cosine, sine).T
    own_keyval = jnp.concatenate([own_keys, keyval_raw[:, key_width:]], axis=1).astype(jnp.bfloat16)
    all_keyval = gather_keys(own_keyval)
    border = lax.ppermute(
        conv_input[row_count - (CONV - 1) :],
        seq_axes,
        [(i, i + 1) for i in range(lax.axis_size(seq_axes) - 1)],
    )
    extended = jnp.concatenate([border, conv_input], axis=0).astype(jnp.float32)
    act, pull_conv = jax.vjp(conv_act, extended, tap_all[:CONV], tap_all[CONV])
    step_size = jax.nn.softplus(step_raw + mamba_heads[1][None, :])
    log_decay = -jnp.exp(mamba_heads[0])[None, :] * step_size
    by_chunk = by_chunks(log_decay)
    chunk_rows = by_chunk.shape[1]
    lower = jnp.tril(jnp.ones((chunk_rows, chunk_rows), jnp.float32))
    cum = jnp.stack([jnp.dot(lower, c, precision=highest_precision) for c in by_chunk])
    cum = cum.reshape(log_decay.shape)
    y_local, grown, fresh_state, tail = ssd_local(act, cum, step_size)
    y_local = y_local.reshape(row_count, inner_width)
    grown = grown.reshape(row_count, inner_width)
    carry_state = carried(fresh_state, tail, 1)

    gate_projected = times_rows(normed, gate_pair)
    gate_z = gate_projected[:, :inner_width]
    query_cols = turn_rows(gate_projected[:, inner_width:].T, cosine, sine).astype(jnp.bfloat16)
    all_keys = all_keyval[:, :, :key_width]
    all_values = all_keyval[:, :, key_width:]
    attended_cols, logs = attend(place, query_cols, all_keys, jnp.swapaxes(all_values, 1, 2))
    attention_rows = attended_cols.T.astype(jnp.bfloat16)

    skip_row = jnp.repeat(skip_weight, MHEAD_DIM)[None, :]
    output_low = act[:, inner_width + STATE :].astype(jnp.bfloat16)
    ssm_y = (
        y_local
        + grown * plain_dot(output_low, carry_state.astype(jnp.bfloat16))
        + skip_row * act[:, :inner_width]
    )
    gate_sigmoid = jax.nn.sigmoid(gate_z)
    mixer = (ssm_y * gate_z * gate_sigmoid).astype(jnp.bfloat16)
    branches = jnp.concatenate([mixer, attention_rows], axis=1)
    branches_a, branches_b = branches[:, :out_half], branches[:, out_half:]
    hidden = (
        inputs + times_rows_back(branches_a, out_pair_a) + times_rows_back(branches_b, out_pair_b)
    )
    normed_two = rms_norm(hidden, gain_two_float).astype(jnp.bfloat16)
    gate_part = times_rows(normed_two, ff_pair_a)
    up_part = times_rows(normed_two, ff_pair_b)
    activated = (jax.nn.silu(gate_part) * up_part).astype(jnp.bfloat16)
    active_a, active_b = activated[:, :down_half], activated[:, down_half:]
    result = (
        hidden + times_rows_back(active_a, down_pair_a) + times_rows_back(active_b, down_pair_b)
    )
    output = back_product(result.astype(jnp.bfloat16), order).astype(jnp.bfloat16)[None]

    grad_activated = jnp.concatenate(
        [times_rows(grad_output, down_pair_a), times_rows(grad_output, down_pair_b)], axis=1
    )
    grad_down_a = scatter_product(grad_output, active_a, "x")
    grad_down_b = scatter_product(grad_output, active_b, "y")
    ff_sigmoid = jax.nn.sigmoid(gate_part)
    grad_gate = grad_activated * up_part * ff_sigmoid * (1.0 + gate_part * (1.0 - ff_sigmoid))
    grad_gate = grad_gate.astype(jnp.bfloat16)
    grad_up = (grad_activated * gate_part * ff_sigmoid).astype(jnp.bfloat16)
    grad_ff_a = scatter_product(normed_two, grad_gate, "x")
    grad_ff_b = scatter_product(normed_two, grad_up, "y")
    grad_normed_two = times_rows_back(grad_gate, ff_pair_a) + times_rows_back(grad_up, ff_pair_b)
    _, pull_two = jax.vjp(rms_norm, hidden, gain_two_float)
    grad_hidden_norm, grad_gain_two = pull_two(grad_normed_two)
    grad_hidden = grad_output.astype(jnp.float32) + grad_hidden_norm
    grad_branch = grad_hidden.astype(jnp.bfloat16)
    grad_branches = jnp.concatenate(
        [times_rows(grad_branch, out_pair_a), times_rows(grad_branch, out_pair_b)], axis=1
    )
    grad_out_a = scatter_product(grad_branch, branches_a, "x")
    grad_out_b = scatter_product(grad_branch, branches_b, "y")
    grad_mixer = grad_branches[:, :inner_width]
    grad_y = grad_mixer * gate_z * gate_sigmoid
    grad_gate_z = grad_mixer * ssm_y * gate_sigmoid * (1.0 + gate_z * (1.0 - gate_sigmoid))
    from_output = outer_product(output_low, (grown * grad_y).astype(jnp.bfloat16))
    grad_end = carried(from_output, tail, -1)

    grad_attention = grad_branches[:, inner_width:].astype(jnp.bfloat16)
    grad_query_cols, grad_slots = attend_back(
        place,
        query_cols,
        grad_attention.T,
        grad_attention,
        attended_cols,
        logs,
        all_keys,
        jnp.swapaxes(all_keys, 1, 2),
        all_values,
    )
    own_grads = sum_key_grads(grad_slots)
    grad_query = turn_rows(grad_query_cols, cosine, -sine).T.astype(jnp.bfloat16)
    grad_keys = turn_rows(own_grads[:, :key_width].T, cosine, -sine).T
    grad_keyval = jnp.concatenate([grad_keys, own_grads[:, key_width:]], axis=1).astype(
        jnp.bfloat16
    )

    grad_act, grad_step_size, grad_log, grad_skip = ssd_back(
        act, cum, step_size, grad_y, carry_state, grad_end, skip_row
    )
    grad_step_size = grad_step_size - grad_log * jnp.exp(mamba_heads[0])[None, :]
    grad_step_raw = grad_step_size * jax.nn.sigmoid(step_raw + mamba_heads[1][None, :])
    grad_heads = jnp.stack([jnp.sum(grad_log * log_decay, axis=0), jnp.sum(grad_step_raw, axis=0)])
    grad_extended, grad_conv_weight, grad_conv_bias = pull_conv(grad_act)
    rim_back = lax.ppermute(
        grad_extended[: CONV - 1],
        seq_axes,
        [(i + 1, i) for i in range(lax.axis_size(seq_axes) - 1)],
    )
    grad_conv_input = grad_extended[CONV - 1 :] + jnp.pad(
        rim_back, ((row_count - (CONV - 1), 0), (0, 0))
    )
    grad_gate_half = jnp.concatenate([grad_gate_z.astype(jnp.bfloat16), grad_query], axis=1)
    grad_conv_half = jnp.concatenate(
        [
            grad_conv_input.astype(jnp.bfloat16),
            grad_keyval,
            grad_step_raw.astype(jnp.bfloat16),
            jnp.zeros((row_count, conv_shard.shape[1] - gain_at), jnp.bfloat16),
        ],
        axis=1,
    )
    grad_in_gate = scatter_product(normed, grad_gate_half, "y")
    grad_in_conv = scatter_product(normed, grad_conv_half, "x")
    grad_normed = times_rows_back(grad_gate_half, gate_pair) + times_rows_back(
        grad_conv_half, conv_pair
    )
    _, pull_one = jax.vjp(rms_norm, inputs, gain_one_float)
    grad_input_norm, grad_gain_one = pull_one(grad_normed)
    input_grad = lax.dot_general(
        grad_hidden + grad_input_norm,
        order.astype(jnp.float32),
        (((1,), (1,)), ((), ())),
        precision=lax.Precision.HIGH,
        preferred_element_type=jnp.float32,
    )[None]

    def usual_gain(grad):
        rows = jnp.broadcast_to(grad[None], (8, width))
        return lax.dot_general(
            rows,
            order.astype(jnp.float32),
            (((1,), (1,)), ((), ())),
            precision=highest_precision,
        )[:1]

    def padded(row):
        return jnp.pad(row, ((0, 0), (0, channels - row.shape[1])))

    head_row = jnp.concatenate(
        [grad_heads[:1], grad_heads[1:], jnp.sum(grad_skip.reshape(MHEADS, -1), axis=1)[None]],
        axis=1,
    )
    summed = sum_everywhere(
        jnp.concatenate(
            [
                grad_conv_weight,
                grad_conv_bias[None],
                padded(usual_gain(grad_gain_two)),
                padded(head_row),
            ],
            axis=0,
        )
    )
    summed_gain = sum_everywhere(usual_gain(grad_gain_one))
    device = lax.axis_index(every_axis)
    own_channels = conv_weight.shape[1]
    own_taps = lax.dynamic_slice_in_dim(summed[: CONV + 1], device * own_channels, own_channels, 1)
    own_gain_two = lax.dynamic_slice_in_dim(summed[CONV + 1], device * own_rows, own_rows)
    own_gain_one = lax.dynamic_slice_in_dim(summed_gain[0], device * own_rows, own_rows)
    head_sums_row = summed[CONV + 2]
    return (
        output,
        input_grad,
        own_gain_one,
        jnp.concatenate([grad_in_gate[:, :inner_width], grad_in_conv[:, :channels]], axis=1),
        grad_in_conv[:, step_at:gain_at],
        own_taps[:CONV],
        own_taps[CONV],
        head_sums_row[: 2 * MHEADS].reshape(2, MHEADS),
        head_sums_row[2 * MHEADS : 3 * MHEADS],
        grad_in_gate[:, inner_width:],
        grad_in_conv[:, channels:step_at],
        jnp.concatenate([grad_out_a, grad_out_b], axis=1)[:, inner_width:].T,
        jnp.concatenate([grad_out_a, grad_out_b], axis=1)[:, :inner_width].T,
        own_gain_two,
        jnp.concatenate([grad_ff_a, grad_ff_b], axis=1),
        jnp.concatenate([grad_down_a, grad_down_b], axis=1).T,
    )


def solution(mesh):
    dp, seq = mesh.shape["dp"], mesh.shape["seq"]
    by_axis = Mesh(mesh.devices.reshape(dp // 2, 2, seq // 2, 2), every_axis)
    pieces = P(("y", "core"), seq_axes, None)
    rows = P(every_axis, None)
    columns = P(None, every_axis)
    vector = P(every_axis)
    weights = (rows, rows, columns, columns, vector, rows, columns)
    return jax.shard_map(
        on_device,
        mesh=by_axis,
        in_specs=(pieces, vector, rows, rows, columns, vector, P(), P(), *weights, pieces),
        out_specs=(pieces, pieces, vector, rows, rows, columns, vector, P(), P(), *weights),
        check_vma=False,
    )
```

```python
import math
from functools import partial

import jax
import jax.experimental.pallas as pl
import jax.experimental.pallas.tpu as pltpu
import jax.numpy as jnp
from jax import lax
from jax.sharding import Mesh
from jax.sharding import PartitionSpec as P

MHEADS = 24
MHEAD_DIM = 64
STATE = 128
CONV = 4
QHEADS = 8
KVHEADS = 2
HEAD_DIM = 64
FF = 2048


norm_epsilon = 1e-06
rope_base = 100000000000.0
masked_score = -1e30
highest_precision = lax.Precision.HIGHEST
seq_axes = ("z", "x")
every_axis = ("y", "core", "z", "x")


def rms_norm(values, gain_vector):
    return (
        values
        * lax.rsqrt(jnp.mean(values * values, axis=-1, keepdims=True) + norm_epsilon)
        * gain_vector
    )


def outer_product(left, right):
    return lax.dot_general(
        left, right, (((0,), (0,)), ((), ())), preferred_element_type=jnp.float32
    )


def back_product(grad_rows, weight_matrix):
    return lax.dot_general(
        grad_rows, weight_matrix, (((1,), (1,)), ((), ())), preferred_element_type=jnp.float32
    )


def turn_columns(positions):
    half = HEAD_DIM // 2
    exponents = jnp.arange(half).astype(jnp.float32) * (2.0 / HEAD_DIM)
    frequency = rope_base ** (-exponents)
    angles = frequency[:, None] * positions.astype(jnp.float32)[None, :]
    return (jnp.cos(angles), jnp.sin(angles))


def turn_rows(values, cosine, sine):
    half = HEAD_DIM // 2
    heads = values.reshape(-1, 2, half, values.shape[1])
    first, second = heads[:, 0], heads[:, 1]
    turned = [first * cosine - second * sine, second * cosine + first * sine]
    return jnp.stack(turned, axis=1).reshape(values.shape)


def conv_act(extended, conv_weight, conv_bias):
    row_count = extended.shape[0] - (CONV - 1)
    conv_sum = conv_bias[None, :] + conv_weight[0][None, :] * extended[0:row_count]
    for offset in range(1, CONV):
        conv_sum = conv_sum + conv_weight[offset][None, :] * extended[offset : offset + row_count]
    return jax.nn.silu(conv_sum)


log2_e = math.log2(math.e)
group_size = QHEADS // KVHEADS
score_scale = 1.0 / math.sqrt(HEAD_DIM)
compiler_room = pltpu.CompilerParams(vmem_limit_bytes=48 * 1024 * 1024)


def plain_dot(left, right):
    return jnp.dot(left, right, preferred_element_type=jnp.float32)


def head_span(head):
    return slice(head * HEAD_DIM, (head + 1) * HEAD_DIM)


def hidden_keys(rows):
    key_at = lax.broadcasted_iota(jnp.int32, (rows, rows), 0)
    query_at = lax.broadcasted_iota(jnp.int32, (rows, rows), 1)
    return key_at > query_at


def slot_of(index, place_ref):
    z, x = lax.shift_right_logical(index, 1), lax.bitwise_and(index, 1)
    return 2 * (place_ref[0] - z) + lax.bitwise_xor(x, place_ref[1])


def attend_kernel(place_ref, query_ref, keyval_ref, keyval_cols_ref, out_ref, log_ref, best_ref, sum_ref):
    rows = query_ref.shape[1]
    scale = log2_e * score_scale

    def scores_of(piece, head):
        group = head // group_size
        keys = keyval_ref[piece, :, 2 * group * HEAD_DIM : 2 * (group + 1) * HEAD_DIM]
        query = query_ref[head_span(head), :]
        return plain_dot(keys, jnp.concatenate([query, jnp.zeros_like(query)], axis=0)) * scale

    def values_of(piece, head):
        return keyval_cols_ref[piece, head_span(2 * (head // group_size) + 1), :]

    for head in range(QHEADS):
        scores = jnp.where(hidden_keys(rows), masked_score, scores_of(0, head))
        best = jnp.max(scores, axis=0, keepdims=True)
        weights = jnp.exp2(scores - best)
        best_ref[head : head + 1, :] = best
        sum_ref[head : head + 1, :] = jnp.sum(weights, axis=0, keepdims=True)
        out_ref[head_span(head), :] = plain_dot(values_of(0, head), weights.astype(jnp.bfloat16))

    def piece_step(index, carry):
        piece = slot_of(index, place_ref)
        for head in range(QHEADS):
            scores = scores_of(piece, head)
            old = best_ref[head : head + 1, :]
            best = jnp.maximum(old, jnp.max(scores, axis=0, keepdims=True))
            fade = jnp.exp2(old - best)
            weights = jnp.exp2(scores - best)
            best_ref[head : head + 1, :] = best
            sum_ref[head : head + 1, :] = sum_ref[head : head + 1, :] * fade + jnp.sum(
                weights, axis=0, keepdims=True
            )
            out_ref[head_span(head), :] = out_ref[head_span(head), :] * fade + plain_dot(
                values_of(piece, head), weights.astype(jnp.bfloat16)
            )
        return carry

    lax.fori_loop(0, 2 * place_ref[0] + place_ref[1], piece_step, 0)
    total = sum_ref[...]
    log_ref[...] = best_ref[...] + jnp.log2(total)
    for head in range(QHEADS):
        out_ref[head_span(head), :] = out_ref[head_span(head), :] / total[head : head + 1, :]


def in_vmem(count):
    return [pl.BlockSpec(memory_space=pltpu.VMEM)] * count


def attend(place, queries, keyvals, keyval_cols):
    rows = queries.shape[1]
    flops = 4 * queries.size * rows * keyvals.shape[0]
    return pl.pallas_call(
        attend_kernel,
        out_shape=(
            jax.ShapeDtypeStruct(queries.shape, jnp.float32),
            jax.ShapeDtypeStruct((QHEADS, rows), jnp.float32),
        ),
        in_specs=[pl.BlockSpec(memory_space=pltpu.SMEM)] + in_vmem(3),
        out_specs=tuple(in_vmem(2)),
        scratch_shapes=[pltpu.VMEM((QHEADS, rows), jnp.float32)] * 2,
        compiler_params=compiler_room,
        cost_estimate=pl.CostEstimate(
            flops=8 * flops, bytes_accessed=4 * keyvals.size, transcendentals=flops // 256
        ),
        name="attend",
    )(place, queries, keyvals, keyval_cols)


def attend_back_kernel(
    group,
    place_ref,
    query_ref,
    query_rows_ref,
    grad_ref,
    grad_rows_ref,
    out_ref,
    log_ref,
    keyval_ref,
    keyval_cols_ref,
    grad_query_ref,
    grad_keyval_ref,
    dots_ref,
    query_side_ref,
    grad_side_ref,
):
    rows = query_ref.shape[1]
    scale = log2_e * score_scale
    grad_query_ref[...] = jnp.zeros_like(grad_query_ref)
    for j in range(group_size):
        span = head_span(group * group_size + j)
        dots_ref[j : j + 1, :] = jnp.sum(
            grad_ref[span, :].astype(jnp.float32) * out_ref[span, :], axis=0, keepdims=True
        )
        query = (query_rows_ref[:, span].astype(jnp.float32) * score_scale).astype(jnp.bfloat16)
        grad = grad_rows_ref[:, span]
        query_side_ref[j] = jnp.concatenate([query, jnp.zeros_like(query)], axis=1)
        grad_side_ref[j] = jnp.concatenate([jnp.zeros_like(grad), grad], axis=1)

    def one_piece(piece, own):
        keyvals = keyval_ref[piece, :, 2 * group * HEAD_DIM : 2 * (group + 1) * HEAD_DIM]
        key_cols = keyval_cols_ref[piece, head_span(2 * group), :]
        total = jnp.zeros((rows, 2 * HEAD_DIM), jnp.float32)
        for j in range(group_size):
            head = group * group_size + j
            query, grad = query_ref[head_span(head), :], grad_ref[head_span(head), :]
            blank = jnp.zeros_like(query)
            scores = plain_dot(keyvals, jnp.concatenate([query, blank], axis=0)) * scale
            weights = jnp.exp2(scores - log_ref[head : head + 1, :])
            if own:
                weights = jnp.where(hidden_keys(rows), 0.0, weights)
            grad_weights = plain_dot(keyvals, jnp.concatenate([blank, grad], axis=0))
            grad_scores = (weights * (grad_weights - dots_ref[j : j + 1, :])).astype(jnp.bfloat16)
            grad_query_ref[head_span(j), :] += plain_dot(key_cols, grad_scores)
            total = total + plain_dot(grad_scores, query_side_ref[j])
            total = total + plain_dot(weights.astype(jnp.bfloat16), grad_side_ref[j])
        grad_keyval_ref[piece] = total

    def clear(piece, carry):
        grad_keyval_ref[piece] = jnp.zeros(grad_keyval_ref.shape[1:], jnp.float32)
        return carry

    def earlier(index, carry):
        one_piece(slot_of(index, place_ref), False)
        return carry

    lax.fori_loop(1, keyval_ref.shape[0], clear, 0)
    one_piece(0, True)
    lax.fori_loop(0, 2 * place_ref[0] + place_ref[1], earlier, 0)
    grad_query_ref[...] = grad_query_ref[...] * score_scale


def attend_back(group, place, queries, query_rows, grads, grad_rows, outs, logs, keyvals, keyval_cols):
    rows = queries.shape[1]
    flops = 10 * queries.size * rows * keyvals.shape[0] // KVHEADS
    return pl.pallas_call(
        partial(attend_back_kernel, group),
        out_shape=(
            jax.ShapeDtypeStruct((group_size * HEAD_DIM, rows), jnp.float32),
            jax.ShapeDtypeStruct((*keyvals.shape[:2], 2 * HEAD_DIM), jnp.float32),
        ),
        in_specs=[pl.BlockSpec(memory_space=pltpu.SMEM)] + in_vmem(8),
        out_specs=tuple(in_vmem(2)),
        scratch_shapes=[
            pltpu.VMEM((8, rows), jnp.float32),
            pltpu.VMEM((group_size, rows, 2 * HEAD_DIM), jnp.bfloat16),
            pltpu.VMEM((group_size, rows, 2 * HEAD_DIM), jnp.bfloat16),
        ],
        compiler_params=compiler_room,
        cost_estimate=pl.CostEstimate(
            flops=6 * flops, bytes_accessed=4 * keyvals.size, transcendentals=flops // 640
        ),
        name="attend_back_" + str(group),
    )(place, queries, query_rows, grads, grad_rows, outs, logs, keyvals, keyval_cols)


ssd_rows = 128


def two_parts(values):
    high = values.astype(jnp.bfloat16)
    rest = values - high.astype(jnp.float32)
    middle = rest.astype(jnp.bfloat16)
    low = (rest - middle.astype(jnp.float32)).astype(jnp.bfloat16)
    return jnp.concatenate([high, middle, low], axis=1)


def head_columns(heads, parts):
    shape = (heads * parts, heads * MHEAD_DIM)
    head = lax.broadcasted_iota(jnp.int32, shape, 0) % heads
    channel = lax.broadcasted_iota(jnp.int32, shape, 1) // MHEAD_DIM
    return jnp.where(head == channel, 1.0, 0.0).astype(jnp.bfloat16)


def widen(values, spread):
    return plain_dot(two_parts(values), spread)


def head_sums(values, spread):
    heads = spread.shape[0]
    high = values.astype(jnp.bfloat16)
    low = (values - high.astype(jnp.float32)).astype(jnp.bfloat16)
    total = nt_dot(high, spread) + nt_dot(low, spread)
    return total


def nt_dot(left, right):
    return lax.dot_general(
        left, right, (((1,), (1,)), ((), ())), preferred_element_type=jnp.float32
    )


def split_pair(pair, axis):
    lane = lax.broadcasted_iota(jnp.int32, pair.shape, 1)
    blank = jnp.zeros_like(pair)
    return jnp.concatenate(
        [jnp.where(lane < MHEAD_DIM, pair, blank), jnp.where(lane < MHEAD_DIM, blank, pair)],
        axis=axis,
    )


def bf(values):
    return values.astype(jnp.bfloat16)


def ssd_kernel(act_ref, cum_ref, cum_rows_ref, step_ref, spread_ref, y_ref, grown_ref, state_ref, tail_ref):
    chunks, rows, inner = y_ref.shape
    spread = spread_ref[...]
    state_ref[...] = jnp.zeros_like(state_ref)
    tail_ref[...] = jnp.zeros_like(tail_ref)
    late = lax.broadcasted_iota(jnp.int32, (rows, rows), 0) >= lax.broadcasted_iota(
        jnp.int32, (rows, rows), 1
    )

    def one_chunk(chunk, before):
        act = act_ref[chunk]
        cum = cum_ref[chunk]
        cum_rows = cum_rows_ref[chunk]
        scaled = act[:, :inner] * widen(step_ref[chunk], spread)
        input_mat = act[:, inner : inner + STATE]
        output_low = bf(act[:, inner + STATE :])
        last = cum[rows - 1 : rows, :]
        grown_ref[chunk] = widen(jnp.exp(cum + before), spread)
        mixing = nt_dot(output_low, bf(input_mat))
        state = state_ref[...]
        from_state = plain_dot(output_low, bf(state)) * widen(jnp.exp(cum), spread)
        scaled_low = bf(scaled)
        for pair in range(MHEADS // 2):
            kernels = []
            for head in (2 * pair, 2 * pair + 1):
                gap = cum[:, head : head + 1] - cum_rows[head : head + 1, :]
                kernels.append(bf(jnp.exp(jnp.where(late, gap, masked_score)) * mixing))
            span = slice(2 * pair * MHEAD_DIM, (2 * pair + 2) * MHEAD_DIM)
            y_ref[chunk, :, span] = from_state[:, span] + plain_dot(
                jnp.concatenate(kernels, axis=1), split_pair(scaled_low[:, span], 0)
            )
        weighted = scaled * widen(jnp.exp(last - cum), spread)
        fade = widen(jnp.exp(jnp.broadcast_to(last, (8, last.shape[1]))), spread)[:1]
        state_ref[...] = state * fade + plain_dot(bf(input_mat.T), bf(weighted))
        return before + last

    total = lax.fori_loop(0, chunks, one_chunk, jnp.zeros((1, cum_ref.shape[2]), jnp.float32))
    tail_ref[...] = widen(jnp.exp(jnp.broadcast_to(total, (8, total.shape[1]))), spread)


def by_chunks(values):
    return values.reshape(-1, math.gcd(values.shape[0], ssd_rows), values.shape[1])


def ssd_local(act, cum, step_size):
    act, cum, step_size = by_chunks(act), by_chunks(cum), by_chunks(step_size)
    chunks, rows, _ = act.shape
    inner = MHEADS * MHEAD_DIM
    return pl.pallas_call(
        ssd_kernel,
        out_shape=(
            jax.ShapeDtypeStruct((chunks, rows, inner), jnp.float32),
            jax.ShapeDtypeStruct((chunks, rows, inner), jnp.float32),
            jax.ShapeDtypeStruct((STATE, inner), jnp.float32),
            jax.ShapeDtypeStruct((8, inner), jnp.float32),
        ),
        in_specs=in_vmem(5),
        out_specs=tuple(in_vmem(4)),
        compiler_params=compiler_room,
        cost_estimate=pl.CostEstimate(
            flops=chunks * rows * inner * 10000, bytes_accessed=act.size * 16, transcendentals=0
        ),
        name="ssd",
    )(act, cum, jnp.swapaxes(cum, 1, 2), step_size, head_columns(MHEADS, 3))


def ssd_back_kernel(
    act_ref,
    cum_ref,
    cum_rows_ref,
    step_ref,
    grad_ref,
    carry_ref,
    grad_end_ref,
    skip_ref,
    spread_ref,
    grad_act_ref,
    grad_step_ref,
    grad_log_ref,
    grad_skip_ref,
    states_ref,
    grad_state_ref,
    sums_ref,
):
    chunks, rows, _ = act_ref.shape
    inner = grad_ref.shape[2]
    heads = cum_ref.shape[2]
    spread = spread_ref[...]
    one_spread = spread[:heads]
    at_row = lax.broadcasted_iota(jnp.int32, (rows, rows), 0)
    at_column = lax.broadcasted_iota(jnp.int32, (rows, rows), 1)

    def fade_of(last):
        return widen(jnp.exp(jnp.broadcast_to(last, (8, heads))), spread)[:1]

    states_ref[0] = carry_ref[...]
    for chunk in range(chunks - 1):
        cum = cum_ref[chunk]
        last = cum[rows - 1 : rows, :]
        act = act_ref[chunk]
        weighted = act[:, :inner] * widen(jnp.exp(last - cum) * step_ref[chunk], spread)
        states_ref[chunk + 1] = states_ref[chunk] * fade_of(last) + plain_dot(
            bf(act[:, inner : inner + STATE].T), bf(weighted)
        )
    grad_state_ref[...] = grad_end_ref[...]
    grad_skip_ref[...] = jnp.zeros_like(grad_skip_ref)
    sums_ref[...] = jnp.zeros_like(sums_ref)

    def one_chunk(turn, carried):
        chunk = chunks - 1 - turn
        act = act_ref[chunk]
        cum = cum_ref[chunk]
        cum_rows = cum_rows_ref[chunk]
        step = step_ref[chunk]
        grad_y = grad_ref[chunk]
        last = cum[rows - 1 : rows, :]
        inputs_x = act[:, :inner]
        step_wide = widen(step, spread)
        tail = jnp.exp(last - cum)
        tail_wide = widen(tail, spread)
        scaled = inputs_x * step_wide
        scaled_low = bf(scaled)
        grad_low = bf(grad_y)
        input_low = bf(act[:, inner : inner + STATE])
        output_mat = act[:, inner + STATE :]
        output_low = bf(output_mat)
        state = states_ref[chunk]
        state_low = bf(state)
        grad_state = grad_state_ref[...]
        grad_state_low = bf(grad_state)

        grown_grad = grad_y * widen(jnp.exp(cum), spread)
        grown_low = bf(grown_grad)
        from_row = head_sums(grown_grad * plain_dot(output_low, state_low), one_spread)
        grad_output = nt_dot(grown_low, state_low)
        back = plain_dot(input_low, grad_state_low)
        from_column = head_sums(scaled * back, one_spread) * tail
        grad_input = nt_dot(bf(scaled * tail_wide), grad_state_low)
        fade = fade_of(last)
        both = jnp.sum(grad_state * state, axis=0, keepdims=True) * fade
        from_last = head_sums(jnp.broadcast_to(both, (8, inner)), one_spread)[:1]
        grad_state_ref[...] = grad_state * fade + plain_dot(bf(output_mat.T), grown_low)

        mixing = nt_dot(input_low, output_low)
        grad_mixing = jnp.zeros((rows, rows), jnp.float32)
        column_sums = jnp.zeros((rows, rows), jnp.float32)
        grad_step = jnp.zeros((rows, rows), jnp.float32)
        for pair in range(heads // 2):
            span = slice(2 * pair * MHEAD_DIM, (2 * pair + 2) * MHEAD_DIM)
            apart = split_pair(grad_low[:, span], 0)
            grad_kernels = nt_dot(scaled_low[:, span], apart)
            kernels = []
            for side in range(2):
                head = 2 * pair + side
                gap = cum_rows[head : head + 1, :] - cum[:, head : head + 1]
                decay = jnp.exp(jnp.where(at_row <= at_column, gap, masked_score))
                part = grad_kernels[:, side * rows : (side + 1) * rows] * decay
                grad_mixing = grad_mixing + part
                moved = part * mixing
                sums_ref[head : head + 1, :] = jnp.sum(moved, axis=0, keepdims=True)
                column = jnp.sum(moved, axis=1, keepdims=True)
                column_sums = jnp.where(at_column == head, column, column_sums)
                kernels.append(bf(decay * mixing))
            grad_scaled = plain_dot(jnp.concatenate(kernels, axis=1), apart)
            grad_scaled = grad_scaled + back[:, span] * tail_wide[:, span]
            grad_act_ref[chunk, :, span] = (
                grad_scaled * step_wide[:, span] + skip_ref[:, span] * grad_y[:, span]
            )
            by_step = grad_scaled * inputs_x[:, span]
            lane = lax.broadcasted_iota(jnp.int32, by_step.shape, 1)
            for side in range(2):
                mine = jnp.where((lane < MHEAD_DIM) == (side == 0), by_step, 0.0)
                column = jnp.sum(mine, axis=1, keepdims=True)
                grad_step = jnp.where(at_column == 2 * pair + side, column, grad_step)
        grad_mixing_low = bf(grad_mixing)
        grad_act_ref[chunk, :, inner : inner + STATE] = grad_input + plain_dot(
            grad_mixing_low, output_low
        )
        grad_act_ref[chunk, :, inner + STATE :] = grad_output + plain_dot(
            bf(grad_mixing.T), input_low
        )
        grad_step_ref[chunk] = grad_step[:, :heads]
        row_sums = sums_ref[...].T[:, :heads]
        ahead = row_sums - column_sums[:, :heads] + from_row
        from_here = jnp.where(at_row <= at_column, 1.0, 0.0)
        before = jnp.where(at_row > at_column, 1.0, 0.0)
        grad_log_ref[chunk] = (
            jnp.dot(from_here, ahead, precision=highest_precision)
            + jnp.dot(before, from_column, precision=highest_precision)
            + from_last
        )
        grad_skip_ref[...] += jnp.sum(inputs_x * grad_y, axis=0, keepdims=True)
        return carried

    lax.fori_loop(0, chunks, one_chunk, 0)


def ssd_back(act, cum, step_size, grad_y, carry_state, grad_end, skip_row):
    shape = act.shape
    act, cum, step_size, grad_y = (by_chunks(a) for a in (act, cum, step_size, grad_y))
    chunks, rows, width = act.shape
    inner = MHEADS * MHEAD_DIM
    grad_act, grad_step, grad_log, grad_skip = pl.pallas_call(
        ssd_back_kernel,
        out_shape=(
            jax.ShapeDtypeStruct(act.shape, jnp.float32),
            jax.ShapeDtypeStruct(cum.shape, jnp.float32),
            jax.ShapeDtypeStruct(cum.shape, jnp.float32),
            jax.ShapeDtypeStruct((1, inner), jnp.float32),
        ),
        in_specs=in_vmem(9),
        out_specs=tuple(in_vmem(4)),
        scratch_shapes=[
            pltpu.VMEM((chunks, STATE, inner), jnp.float32),
            pltpu.VMEM((STATE, inner), jnp.float32),
            pltpu.VMEM((rows, rows), jnp.float32),
        ],
        compiler_params=compiler_room,
        cost_estimate=pl.CostEstimate(
            flops=chunks * rows * inner * 25000, bytes_accessed=act.size * 16, transcendentals=0
        ),
        name="ssd_back",
    )(
        act,
        cum,
        jnp.swapaxes(cum, 1, 2),
        step_size,
        grad_y,
        carry_state,
        grad_end,
        skip_row,
        head_columns(MHEADS, 3),
    )
    flat = (shape[0], MHEADS)
    return grad_act.reshape(shape), grad_step.reshape(flat), grad_log.reshape(flat), grad_skip


def shifted(block, axis, distance):
    count = lax.axis_size(axis)
    return lax.ppermute(block, axis, [(i, (i + distance) % count) for i in range(count)])


def moved_along(block, axis, distance):
    count = lax.axis_size(axis)
    route = [(i, i + distance) for i in range(count) if 0 <= i + distance < count]
    return lax.ppermute(block, axis, route)


def width_order(width):
    sizes = {axis: lax.axis_size(axis) for axis in every_axis}
    rows = width // math.prod(sizes.values())
    rest = lax.broadcasted_iota(jnp.int32, (width, width), 1)
    inside, rest = rest % rows, rest // rows
    owner = {}
    for axis in ("z", "x", "y", "core"):
        owner[axis] = (rest % sizes[axis] + lax.axis_index(axis)) % sizes[axis]
        rest = rest // sizes[axis]
    usual = owner["y"]
    for axis in ("core", "z", "x"):
        usual = usual * sizes[axis] + owner[axis]
    usual = usual * rows + inside
    return (lax.broadcasted_iota(jnp.int32, (width, width), 0) == usual).astype(jnp.bfloat16)


def after(values, *others):
    return lax.optimization_barrier((values, others))[0]


def gather_stages(shard):
    parts = [shard] + [shifted(shard, "z", -k) for k in range(1, lax.axis_size("z"))]
    started = parts[-1]
    block = jnp.concatenate(parts, axis=0)[None, None]
    middle = shard.shape[1] // 256 * 128
    halves = []
    for half, axes in ((block[..., :middle], "xy"), (block[..., middle:], "yx")):
        for axis in axes:
            parts = [half] + [shifted(half, axis, -k) for k in range(1, lax.axis_size(axis))]
            half = jnp.concatenate(parts, axis="yx".index(axis))
        halves.append(half.reshape(-1, half.shape[-1]))
    own = jnp.concatenate(halves, axis=1)
    return (own, shifted(own, "core", 1)), started


def times_rows(values, pair):
    half = values.shape[1] // 2
    return plain_dot(values[:, :half], pair[0]) + plain_dot(values[:, half:], pair[1])


def times_rows_back(values, pair):
    return jnp.concatenate([back_product(values, pair[0]), back_product(values, pair[1])], axis=1)


def keep_own(total, axis, dim, received=None):
    kept = lax.index_in_dim(total, 0, dim, False)
    for step in range(1, lax.axis_size(axis)):
        part = lax.index_in_dim(total, step, dim, False)
        got = shifted(part.astype(jnp.bfloat16), axis, step)
        if received is not None:
            received.append(got)
        kept = kept + got.astype(jnp.float32)
    return kept


def core_sum(left, right, received):
    half = left.shape[1] // 2
    sizes = [lax.axis_size(axis) for axis in ("y", "x", "z")]
    got = shifted(outer_product(left[:, half:], right).astype(jnp.bfloat16), "core", 1)
    received.append(got)
    total = outer_product(left[:, :half], right) + got.astype(jnp.float32)
    return total.reshape(*sizes, -1, right.shape[1])


def side_by_side(parts):
    return parts[0] if len(parts) == 1 else jnp.concatenate(parts, axis=-1)


def chip_sums(by_x, by_y, received):
    by_x = side_by_side([keep_own(total, "x", 1, received) for total in by_x])
    by_y = side_by_side([keep_own(total, "y", 0, received) for total in by_y])
    later = []
    by_x = keep_own(by_x, "y", 0, later)
    by_y = keep_own(by_y, "x", 0, later)
    return keep_own(jnp.concatenate([by_x, by_y], axis=-1), "z", 0), later


def sum_everywhere(values):
    for axis in ("core", "x", "y", "z"):
        count = lax.axis_size(axis)
        step = 1
        while step < count:
            values = values + lax.ppermute(values, axis, [(i, i ^ step) for i in range(count)])
            step *= 2
    return values


def carried(state, tail, direction):
    depth, width = state.shape
    half = width // 2
    at_x = lax.axis_index("x")
    is_second = (at_x == 1) if direction == 1 else (at_x == 0)
    packed = jnp.concatenate([state, tail], axis=0).astype(jnp.bfloat16)
    other = shifted(packed, "x", 1).astype(jnp.float32)
    own = packed.astype(jnp.float32)
    first = jnp.where(is_second, other, own)
    second = jnp.where(is_second, own, other)
    first_state, first_tail = first[:depth], first[depth : depth + 1]
    second_tail = second[depth : depth + 1]
    pair = jnp.concatenate(
        [second_tail * first_state + second[:depth], first[depth:] * second[depth:]], axis=0
    )
    mine = jnp.where(at_x == 0, pair[:, :half], pair[:, half:]).astype(jnp.bfloat16)
    total = jnp.zeros((depth, half), jnp.float32)
    fade = jnp.ones((1, half), jnp.float32)
    for step in range(1, lax.axis_size("z")):
        got = moved_along(mine, "z", direction * step).astype(jnp.float32)
        total = total + fade * got[:depth]
        fade = fade * got[depth : depth + 1]
    total = total.astype(jnp.bfloat16)
    rest = shifted(total, "x", 1)
    left, right = jnp.where(at_x == 0, total, rest), jnp.where(at_x == 0, rest, total)
    carry = jnp.concatenate([left, right], axis=1).astype(jnp.float32)
    return jnp.where(is_second, first_tail * carry + first_state, carry)


def gather_keys(own):
    blocks = [moved_along(own, "z", step) if step else own for step in range(lax.axis_size("z"))]
    blocks = jnp.stack(blocks)
    slots = jnp.stack([blocks, shifted(blocks, "x", 1)], axis=1)
    return slots.reshape(-1, *own.shape)


def swap_key_grads(slots):
    total = slots.reshape(-1, 2, *slots.shape[1:])
    swapped = shifted(total[:, 1].astype(jnp.bfloat16), "x", 1)
    return total[:, 0], swapped


def sum_key_grads(kept, swapped):
    kept = kept + swapped.astype(jnp.float32)
    own = kept[0]
    for step in range(1, kept.shape[0]):
        own = own + moved_along(kept[step].astype(jnp.bfloat16), "z", -step).astype(jnp.float32)
    return own


def on_device(
    tokens,
    gain_one,
    w_in,
    w_step,
    conv_weight,
    conv_bias,
    mamba_heads,
    skip_weight,
    w_query,
    w_keyval,
    w_attn_out,
    w_mix_out,
    gain_two,
    w_gate_up,
    w_down,
    cotangent,
):
    width = tokens.shape[2]
    row_count = tokens.shape[1]
    inner_width = MHEADS * MHEAD_DIM
    device_count = math.prod(lax.axis_size(axis) for axis in every_axis)
    channels = conv_weight.shape[1] * device_count
    key_width = KVHEADS * HEAD_DIM
    query_width = QHEADS * HEAD_DIM
    own_rows = gain_one.shape[0]
    at_z, at_x = lax.axis_index("z"), lax.axis_index("x")
    place = jnp.stack([at_z, at_x]).astype(jnp.int32)

    taps = jnp.concatenate([conv_weight, conv_bias[None]], axis=0)
    tap_columns = -(-taps.size // own_rows)
    tap_shard = jnp.pad(taps.reshape(-1), (0, tap_columns * own_rows - taps.size))
    step_at = channels + w_keyval.shape[1]
    gain_at = step_at + w_step.shape[1]
    tap_at = gain_at + 2
    conv_shard = jnp.concatenate(
        [
            w_in[:, inner_width:],
            w_keyval,
            w_step,
            gain_one[:, None],
            gain_two[:, None],
            tap_shard.reshape(tap_columns, own_rows).T,
            jnp.zeros((own_rows, -(tap_at + tap_columns) % 128), jnp.bfloat16),
        ],
        axis=1,
    )
    gate_shard = jnp.concatenate([w_in[:, :inner_width], w_query], axis=1)
    out_shard = jnp.concatenate([w_mix_out.T, w_attn_out.T], axis=1)
    down_shard = w_down.T
    late_shard = jnp.concatenate([out_shard, w_gate_up, down_shard], axis=1)
    late = lax.all_gather(late_shard, every_axis, axis=0, tiled=True)
    full_out, full_gate, full_up, full_down = jnp.split(
        late, [out_shard.shape[1], out_shard.shape[1] + FF, out_shard.shape[1] + 2 * FF], axis=1
    )
    conv_pair, started = gather_stages(conv_shard)
    gate_pair, _ = gather_stages(after(gate_shard, started))

    order = width_order(width)
    inputs = plain_dot(tokens[0], order)
    grad_output = cotangent[0]
    small = jnp.concatenate([half[:, gain_at : tap_at + tap_columns] for half in conv_pair], axis=0)
    gain_one_float = small[:, 0].astype(jnp.float32)
    small_rows = lax.dot_general(
        small, order, (((0,), (1,)), ((), ())), preferred_element_type=jnp.float32
    )
    gain_two_float = small_rows[1]
    tap_all = small_rows[2:].reshape(tap_columns, device_count, own_rows)
    tap_all = jnp.swapaxes(tap_all, 0, 1).reshape(device_count, -1)[:, : taps.size]
    tap_all = jnp.swapaxes(tap_all.reshape(-1, *taps.shape), 0, 1).reshape(taps.shape[0], channels)

    normed = rms_norm(inputs, gain_one_float).astype(jnp.bfloat16)
    conv_projected = times_rows(normed, conv_pair)
    conv_input = conv_projected[:, :channels].astype(jnp.bfloat16)
    keyval_raw = conv_projected[:, channels:step_at]
    step_raw = conv_projected[:, step_at:gain_at]
    positions = (at_z * lax.axis_size("x") + at_x) * row_count + jnp.arange(
        row_count, dtype=jnp.int32
    )
    cosine, sine = turn_columns(positions)
    keyval_cols = keyval_raw.T
    key_cols = turn_rows(keyval_cols[:key_width], cosine, sine)
    by_head = (KVHEADS, 1, HEAD_DIM, row_count)
    own_keyval = jnp.concatenate(
        [key_cols.reshape(by_head), keyval_cols[key_width:].reshape(by_head)], axis=1
    ).reshape(2 * key_width, row_count)
    all_keyval = gather_keys(own_keyval.T.astype(jnp.bfloat16))
    all_cols = jnp.swapaxes(all_keyval, 1, 2)
    border = lax.ppermute(
        conv_input[row_count - (CONV - 1) :],
        seq_axes,
        [(i, i + 1) for i in range(lax.axis_size(seq_axes) - 1)],
    )
    extended = jnp.concatenate([border, conv_input], axis=0).astype(jnp.float32)
    act, pull_conv = jax.vjp(conv_act, extended, tap_all[:CONV], tap_all[CONV])
    step_size = jax.nn.softplus(step_raw + mamba_heads[1][None, :])
    log_decay = -jnp.exp(mamba_heads[0])[None, :] * step_size
    by_chunk = by_chunks(log_decay)
    chunk_rows = by_chunk.shape[1]
    lower = jnp.tril(jnp.ones((chunk_rows, chunk_rows), jnp.float32))
    cum = jnp.stack([jnp.dot(lower, c, precision=highest_precision) for c in by_chunk])
    cum = cum.reshape(log_decay.shape)
    y_local, grown, fresh_state, tail = ssd_local(act, cum, step_size)
    y_local = y_local.reshape(row_count, inner_width)
    grown = grown.reshape(row_count, inner_width)
    carry_state = carried(fresh_state, tail, 1)

    gate_projected = times_rows(normed, gate_pair)
    gate_z = gate_projected[:, :inner_width]
    query_cols = turn_rows(gate_projected[:, inner_width:].T, cosine, sine).astype(jnp.bfloat16)
    attended_cols, logs = attend(place, query_cols, all_keyval, all_cols)
    attention_rows = attended_cols.T.astype(jnp.bfloat16)

    skip_row = jnp.repeat(skip_weight, MHEAD_DIM)[None, :]
    output_low = act[:, inner_width + STATE :].astype(jnp.bfloat16)
    ssm_y = (
        y_local
        + grown * plain_dot(output_low, carry_state.astype(jnp.bfloat16))
        + skip_row * act[:, :inner_width]
    )
    gate_sigmoid = jax.nn.sigmoid(gate_z)
    mixer = (ssm_y * gate_z * gate_sigmoid).astype(jnp.bfloat16)
    branches = jnp.concatenate([mixer, attention_rows], axis=1)
    hidden = tokens[0].astype(jnp.float32) + back_product(branches, full_out)
    normed_two = rms_norm(hidden, gain_two_float).astype(jnp.bfloat16)
    gate_part = plain_dot(normed_two, full_gate)
    up_part = plain_dot(normed_two, full_up)
    activated = (jax.nn.silu(gate_part) * up_part).astype(jnp.bfloat16)
    result = hidden + back_product(activated, full_down)
    output = result.astype(jnp.bfloat16)[None]

    def reordered(rows):
        return plain_dot(rows, order).astype(jnp.bfloat16)

    grad_activated = plain_dot(grad_output, full_down)
    core_got = []
    grad_output_rows = reordered(grad_output)
    down_half = FF // 2
    normed_two_rows = reordered(normed_two)
    ff_sigmoid = jax.nn.sigmoid(gate_part)
    grad_gate = grad_activated * up_part * ff_sigmoid * (1.0 + gate_part * (1.0 - ff_sigmoid))
    grad_gate = grad_gate.astype(jnp.bfloat16)
    grad_up = (grad_activated * gate_part * ff_sigmoid).astype(jnp.bfloat16)
    gate_total = core_sum(normed_two_rows, grad_gate, core_got)
    up_total = core_sum(normed_two_rows, grad_up, core_got)
    down_a = core_sum(grad_output_rows, activated[:, :down_half], [])
    down_b = core_sum(grad_output_rows, activated[:, down_half:], [])
    ff_got = []
    ff_sums, ff_later = chip_sums([gate_total, down_a], [up_total, down_b], ff_got)
    grad_normed_two = back_product(after(grad_gate, *core_got), full_gate) + back_product(grad_up, full_up)
    _, pull_two = jax.vjp(rms_norm, hidden, gain_two_float)
    grad_hidden_norm, grad_gain_two = pull_two(grad_normed_two)
    grad_hidden = grad_output.astype(jnp.float32) + grad_hidden_norm
    grad_branch = grad_hidden.astype(jnp.bfloat16)
    grad_branches = after(plain_dot(grad_branch, full_out), ff_got[1], ff_got[3])
    grad_mixer = grad_branches[:, :inner_width]
    grad_y = grad_mixer * gate_z * gate_sigmoid
    grad_gate_z = grad_mixer * ssm_y * gate_sigmoid * (1.0 + gate_z * (1.0 - gate_sigmoid))
    from_output = outer_product(output_low, (grown * grad_y).astype(jnp.bfloat16))
    grad_end = carried(from_output, tail, -1)

    grad_attention = grad_branches[:, inner_width:].astype(jnp.bfloat16)
    out_got = []
    out_total = core_sum(reordered(grad_branch), branches, out_got)
    in_gate_total = core_sum(normed, grad_gate_z.astype(jnp.bfloat16), out_got)
    grad_cols = grad_attention.T
    query_rows = query_cols.T
    def one_group(group, grad_cols):
        return attend_back(
            group,
            place,
            query_cols,
            query_rows,
            grad_cols,
            grad_attention,
            attended_cols,
            logs,
            all_keyval,
            all_cols,
        )

    query_a, slots_a = one_group(0, after(grad_cols, gate_total, up_total))
    query_a, slots_a = after((query_a, slots_a), ff_got[0], ff_got[2])
    kept_a, swapped_a = swap_key_grads(slots_a)
    query_b, slots_b = one_group(1, after(grad_cols, ff_got[0], ff_got[2], *out_got))
    before_ssd = (query_b, *ff_later, swapped_a)
    query_b, slots_b, kept_a, swapped_a = after((query_b, slots_b, kept_a, swapped_a), *before_ssd)
    own_a = sum_key_grads(kept_a, swapped_a)
    kept_b, swapped_b = swap_key_grads(slots_b)
    own_b = sum_key_grads(kept_b, swapped_b)
    own_grads = [own_a, own_b]
    key_got = [swapped_b]
    grad_query_cols = jnp.concatenate([query_a, query_b], axis=0)
    mid_got = []
    mid_sums, mid_later = chip_sums([in_gate_total], [out_total], mid_got)
    grad_query = turn_rows(grad_query_cols, cosine, -sine).T.astype(jnp.bfloat16)
    own_cols = jnp.concatenate(own_grads, axis=1).T.reshape(KVHEADS, 2, HEAD_DIM, row_count)
    grad_keys = turn_rows(own_cols[:, 0].reshape(key_width, row_count), cosine, -sine)
    grad_keyval = jnp.concatenate([grad_keys, own_cols[:, 1].reshape(key_width, row_count)], axis=0)
    grad_keyval = grad_keyval.T.astype(jnp.bfloat16)

    grad_act, grad_step_size, grad_log, grad_skip = ssd_back(
        act, cum, step_size, after(grad_y, *before_ssd), carry_state, grad_end, skip_row
    )
    grad_act, grad_step_size, grad_log = after(
        (grad_act, grad_step_size, grad_log), *mid_got, *key_got
    )
    grad_step_size = grad_step_size - grad_log * jnp.exp(mamba_heads[0])[None, :]
    grad_step_raw = grad_step_size * jax.nn.sigmoid(step_raw + mamba_heads[1][None, :])
    grad_heads = jnp.stack([jnp.sum(grad_log * log_decay, axis=0), jnp.sum(grad_step_raw, axis=0)])
    grad_extended, grad_conv_weight, grad_conv_bias = pull_conv(grad_act)
    rim_back = lax.ppermute(
        grad_extended[: CONV - 1],
        seq_axes,
        [(i + 1, i) for i in range(lax.axis_size(seq_axes) - 1)],
    )
    grad_conv_input = grad_extended[CONV - 1 :] + jnp.pad(
        rim_back, ((row_count - (CONV - 1), 0), (0, 0))
    )
    grad_conv_low = after(grad_conv_input.astype(jnp.bfloat16), ff_sums)
    grad_step_low = jnp.pad(
        grad_step_raw.astype(jnp.bfloat16), ((0, 0), (0, conv_shard.shape[1] - gain_at))
    )
    grad_few = jnp.concatenate([grad_query, grad_keyval, grad_step_low], axis=1)
    last_core_got, last_got = [], []
    conv_total = core_sum(normed, grad_conv_low, last_core_got)
    few_total = core_sum(normed, grad_few, [])
    last_sums, _ = chip_sums([conv_total], [few_total], last_got)
    grad_gate_half = jnp.concatenate([grad_gate_z.astype(jnp.bfloat16), grad_query], axis=1)
    grad_conv_half = jnp.concatenate([grad_conv_low, grad_keyval, grad_step_low], axis=1)
    grad_normed = times_rows_back(grad_gate_half, gate_pair) + times_rows_back(
        grad_conv_half, conv_pair
    )
    _, pull_one = jax.vjp(rms_norm, inputs, gain_one_float)
    grad_input_norm, grad_gain_one = pull_one(grad_normed)
    input_grad = lax.dot_general(
        grad_input_norm,
        order.astype(jnp.float32),
        (((1,), (1,)), ((), ())),
        precision=lax.Precision.HIGH,
        preferred_element_type=jnp.float32,
    )
    input_grad = (grad_hidden + input_grad)[None]

    def usual_gain(grad):
        rows = jnp.broadcast_to(grad[None], (8, width))
        return lax.dot_general(
            rows,
            order.astype(jnp.float32),
            (((1,), (1,)), ((), ())),
            precision=highest_precision,
        )[:1]

    def padded(row):
        return jnp.pad(row, ((0, 0), (0, channels - row.shape[1])))

    head_row = jnp.concatenate(
        [grad_heads[:1], grad_heads[1:], jnp.sum(grad_skip.reshape(MHEADS, -1), axis=1)[None]],
        axis=1,
    )
    summed = sum_everywhere(
        after(jnp.concatenate(
            [
                grad_conv_weight,
                grad_conv_bias[None],
                padded(grad_gain_two[None]),
                padded(usual_gain(grad_gain_one)),
                padded(head_row),
            ],
            axis=0,
        ), *last_core_got)
    )
    device = lax.axis_index(every_axis)
    own_channels = conv_weight.shape[1]
    own_taps = lax.dynamic_slice_in_dim(summed[: CONV + 1], device * own_channels, own_channels, 1)
    own_gain_two = lax.dynamic_slice_in_dim(summed[CONV + 1], device * own_rows, own_rows)
    own_gain_one = lax.dynamic_slice_in_dim(summed[CONV + 2], device * own_rows, own_rows)
    head_sums_row = summed[CONV + 3]
    query_at = channels + query_width
    step_from = query_at + w_keyval.shape[1]
    return (
        output,
        input_grad,
        own_gain_one,
        jnp.concatenate([mid_sums[:, :inner_width], last_sums[:, :channels]], axis=1),
        last_sums[:, step_from : step_from + w_step.shape[1]],
        own_taps[:CONV],
        own_taps[CONV],
        head_sums_row[: 2 * MHEADS].reshape(2, MHEADS),
        head_sums_row[2 * MHEADS : 3 * MHEADS],
        last_sums[:, channels:query_at],
        last_sums[:, query_at:step_from],
        mid_sums[:, 2 * inner_width :].T,
        mid_sums[:, inner_width : 2 * inner_width].T,
        own_gain_two,
        jnp.concatenate([ff_sums[:, :FF], ff_sums[:, FF + down_half : 2 * FF + down_half]], axis=1),
        jnp.concatenate(
            [ff_sums[:, FF : FF + down_half], ff_sums[:, 2 * FF + down_half :]], axis=1
        ).T,
    )


def solution(mesh):
    dp, seq = mesh.shape["dp"], mesh.shape["seq"]
    by_axis = Mesh(mesh.devices.reshape(dp // 2, 2, seq // 2, 2), every_axis)
    pieces = P(("y", "core"), seq_axes, None)
    rows = P(every_axis, None)
    columns = P(None, every_axis)
    vector = P(every_axis)
    weights = (rows, rows, columns, columns, vector, rows, columns)
    return jax.shard_map(
        on_device,
        mesh=by_axis,
        in_specs=(pieces, vector, rows, rows, columns, vector, P(), P(), *weights, pieces),
        out_specs=(pieces, pieces, vector, rows, rows, columns, vector, P(), P(), *weights),
        check_vma=False,
    )
```

```python
import math
from functools import partial

import jax
import jax.experimental.pallas as pl
import jax.experimental.pallas.tpu as pltpu
import jax.numpy as jnp
from jax import lax
from jax.sharding import Mesh
from jax.sharding import PartitionSpec as P

MHEADS = 24
MHEAD_DIM = 64
STATE = 128
CONV = 4
QHEADS = 8
KVHEADS = 2
HEAD_DIM = 64
FF = 2048


norm_epsilon = 1e-06
rope_base = 100000000000.0
masked_score = -1e30
highest_precision = lax.Precision.HIGHEST
seq_axes = ("z", "x")
every_axis = ("y", "core", "z", "x")


def rms_norm(values, gain_vector):
    return (
        values
        * lax.rsqrt(jnp.mean(values * values, axis=-1, keepdims=True) + norm_epsilon)
        * gain_vector
    )


def outer_product(left, right):
    return lax.dot_general(
        left, right, (((0,), (0,)), ((), ())), preferred_element_type=jnp.float32
    )


def back_product(grad_rows, weight_matrix):
    return lax.dot_general(
        grad_rows, weight_matrix, (((1,), (1,)), ((), ())), preferred_element_type=jnp.float32
    )


def turn_columns(positions):
    half = HEAD_DIM // 2
    exponents = jnp.arange(half).astype(jnp.float32) * (2.0 / HEAD_DIM)
    frequency = rope_base ** (-exponents)
    angles = frequency[:, None] * positions.astype(jnp.float32)[None, :]
    return (jnp.cos(angles), jnp.sin(angles))


def turn_rows(values, cosine, sine):
    half = HEAD_DIM // 2
    heads = values.reshape(-1, 2, half, values.shape[1])
    first, second = heads[:, 0], heads[:, 1]
    turned = [first * cosine - second * sine, second * cosine + first * sine]
    return jnp.stack(turned, axis=1).reshape(values.shape)


def conv_act(extended, conv_weight, conv_bias):
    row_count = extended.shape[0] - (CONV - 1)
    conv_sum = conv_bias[None, :] + conv_weight[0][None, :] * extended[0:row_count]
    for offset in range(1, CONV):
        conv_sum = conv_sum + conv_weight[offset][None, :] * extended[offset : offset + row_count]
    return jax.nn.silu(conv_sum)


log2_e = math.log2(math.e)
group_size = QHEADS // KVHEADS
score_scale = 1.0 / math.sqrt(HEAD_DIM)
compiler_room = pltpu.CompilerParams(vmem_limit_bytes=48 * 1024 * 1024)


def plain_dot(left, right):
    return jnp.dot(left, right, preferred_element_type=jnp.float32)


def head_span(head):
    return slice(head * HEAD_DIM, (head + 1) * HEAD_DIM)


def hidden_keys(rows):
    key_at = lax.broadcasted_iota(jnp.int32, (rows, rows), 0)
    query_at = lax.broadcasted_iota(jnp.int32, (rows, rows), 1)
    return key_at > query_at


def slot_of(index, place_ref):
    z, x = lax.shift_right_logical(index, 1), lax.bitwise_and(index, 1)
    return 2 * (place_ref[0] - z) + lax.bitwise_xor(x, place_ref[1])


def attend_kernel(place_ref, query_ref, keyval_ref, keyval_cols_ref, out_ref, log_ref, best_ref, sum_ref):
    rows = query_ref.shape[1]
    scale = log2_e * score_scale

    def scores_of(piece, head):
        group = head // group_size
        keys = keyval_ref[piece, :, 2 * group * HEAD_DIM : 2 * (group + 1) * HEAD_DIM]
        query = query_ref[head_span(head), :]
        return plain_dot(keys, jnp.concatenate([query, jnp.zeros_like(query)], axis=0)) * scale

    def values_of(piece, head):
        return keyval_cols_ref[piece, head_span(2 * (head // group_size) + 1), :]

    for head in range(QHEADS):
        scores = jnp.where(hidden_keys(rows), masked_score, scores_of(0, head))
        best = jnp.max(scores, axis=0, keepdims=True)
        weights = jnp.exp2(scores - best)
        best_ref[head : head + 1, :] = best
        sum_ref[head : head + 1, :] = jnp.sum(weights, axis=0, keepdims=True)
        out_ref[head_span(head), :] = plain_dot(values_of(0, head), weights.astype(jnp.bfloat16))

    def piece_step(index, carry):
        piece = slot_of(index, place_ref)
        for head in range(QHEADS):
            scores = scores_of(piece, head)
            old = best_ref[head : head + 1, :]
            best = jnp.maximum(old, jnp.max(scores, axis=0, keepdims=True))
            fade = jnp.exp2(old - best)
            weights = jnp.exp2(scores - best)
            best_ref[head : head + 1, :] = best
            sum_ref[head : head + 1, :] = sum_ref[head : head + 1, :] * fade + jnp.sum(
                weights, axis=0, keepdims=True
            )
            out_ref[head_span(head), :] = out_ref[head_span(head), :] * fade + plain_dot(
                values_of(piece, head), weights.astype(jnp.bfloat16)
            )
        return carry

    lax.fori_loop(0, 2 * place_ref[0] + place_ref[1], piece_step, 0)
    total = sum_ref[...]
    log_ref[...] = best_ref[...] + jnp.log2(total)
    for head in range(QHEADS):
        out_ref[head_span(head), :] = out_ref[head_span(head), :] / total[head : head + 1, :]


def in_vmem(count):
    return [pl.BlockSpec(memory_space=pltpu.VMEM)] * count


def attend(place, queries, keyvals, keyval_cols):
    rows = queries.shape[1]
    flops = 4 * queries.size * rows * keyvals.shape[0]
    return pl.pallas_call(
        attend_kernel,
        out_shape=(
            jax.ShapeDtypeStruct(queries.shape, jnp.float32),
            jax.ShapeDtypeStruct((QHEADS, rows), jnp.float32),
        ),
        in_specs=[pl.BlockSpec(memory_space=pltpu.SMEM)] + in_vmem(3),
        out_specs=tuple(in_vmem(2)),
        scratch_shapes=[pltpu.VMEM((QHEADS, rows), jnp.float32)] * 2,
        compiler_params=compiler_room,
        cost_estimate=pl.CostEstimate(
            flops=8 * flops, bytes_accessed=4 * keyvals.size, transcendentals=flops // 256
        ),
        name="attend",
    )(place, queries, keyvals, keyval_cols)


def attend_back_kernel(
    group,
    place_ref,
    query_ref,
    query_rows_ref,
    grad_ref,
    grad_rows_ref,
    out_ref,
    log_ref,
    keyval_ref,
    keyval_cols_ref,
    grad_query_ref,
    grad_keyval_ref,
    dots_ref,
    query_side_ref,
    grad_side_ref,
):
    rows = query_ref.shape[1]
    scale = log2_e * score_scale
    grad_query_ref[...] = jnp.zeros_like(grad_query_ref)
    for j in range(group_size):
        span = head_span(group * group_size + j)
        dots_ref[j : j + 1, :] = jnp.sum(
            grad_ref[span, :].astype(jnp.float32) * out_ref[span, :], axis=0, keepdims=True
        )
        query = (query_rows_ref[:, span].astype(jnp.float32) * score_scale).astype(jnp.bfloat16)
        grad = grad_rows_ref[:, span]
        query_side_ref[j] = jnp.concatenate([query, jnp.zeros_like(query)], axis=1)
        grad_side_ref[j] = jnp.concatenate([jnp.zeros_like(grad), grad], axis=1)

    def one_piece(piece, own):
        keyvals = keyval_ref[piece, :, 2 * group * HEAD_DIM : 2 * (group + 1) * HEAD_DIM]
        key_cols = keyval_cols_ref[piece, head_span(2 * group), :]
        total = jnp.zeros((rows, 2 * HEAD_DIM), jnp.float32)
        for j in range(group_size):
            head = group * group_size + j
            query, grad = query_ref[head_span(head), :], grad_ref[head_span(head), :]
            blank = jnp.zeros_like(query)
            scores = plain_dot(keyvals, jnp.concatenate([query, blank], axis=0)) * scale
            weights = jnp.exp2(scores - log_ref[head : head + 1, :])
            if own:
                weights = jnp.where(hidden_keys(rows), 0.0, weights)
            grad_weights = plain_dot(keyvals, jnp.concatenate([blank, grad], axis=0))
            grad_scores = (weights * (grad_weights - dots_ref[j : j + 1, :])).astype(jnp.bfloat16)
            grad_query_ref[head_span(j), :] += plain_dot(key_cols, grad_scores)
            total = total + plain_dot(grad_scores, query_side_ref[j])
            total = total + plain_dot(weights.astype(jnp.bfloat16), grad_side_ref[j])
        grad_keyval_ref[piece] = total

    def clear(piece, carry):
        grad_keyval_ref[piece] = jnp.zeros(grad_keyval_ref.shape[1:], jnp.float32)
        return carry

    def earlier(index, carry):
        one_piece(slot_of(index, place_ref), False)
        return carry

    lax.fori_loop(1, keyval_ref.shape[0], clear, 0)
    one_piece(0, True)
    lax.fori_loop(0, 2 * place_ref[0] + place_ref[1], earlier, 0)
    grad_query_ref[...] = grad_query_ref[...] * score_scale


def attend_back(group, place, queries, query_rows, grads, grad_rows, outs, logs, keyvals, keyval_cols):
    rows = queries.shape[1]
    flops = 10 * queries.size * rows * keyvals.shape[0] // KVHEADS
    return pl.pallas_call(
        partial(attend_back_kernel, group),
        out_shape=(
            jax.ShapeDtypeStruct((group_size * HEAD_DIM, rows), jnp.float32),
            jax.ShapeDtypeStruct((*keyvals.shape[:2], 2 * HEAD_DIM), jnp.float32),
        ),
        in_specs=[pl.BlockSpec(memory_space=pltpu.SMEM)] + in_vmem(8),
        out_specs=tuple(in_vmem(2)),
        scratch_shapes=[
            pltpu.VMEM((8, rows), jnp.float32),
            pltpu.VMEM((group_size, rows, 2 * HEAD_DIM), jnp.bfloat16),
            pltpu.VMEM((group_size, rows, 2 * HEAD_DIM), jnp.bfloat16),
        ],
        compiler_params=compiler_room,
        cost_estimate=pl.CostEstimate(
            flops=6 * flops, bytes_accessed=4 * keyvals.size, transcendentals=flops // 640
        ),
        name="attend_back_" + str(group),
    )(place, queries, query_rows, grads, grad_rows, outs, logs, keyvals, keyval_cols)


ssd_rows = 128


def two_parts(values):
    high = values.astype(jnp.bfloat16)
    rest = values - high.astype(jnp.float32)
    middle = rest.astype(jnp.bfloat16)
    low = (rest - middle.astype(jnp.float32)).astype(jnp.bfloat16)
    return jnp.concatenate([high, middle, low], axis=1)


def head_columns(heads, parts):
    shape = (heads * parts, heads * MHEAD_DIM)
    head = lax.broadcasted_iota(jnp.int32, shape, 0) % heads
    channel = lax.broadcasted_iota(jnp.int32, shape, 1) // MHEAD_DIM
    return jnp.where(head == channel, 1.0, 0.0).astype(jnp.bfloat16)


def widen(values, spread):
    return plain_dot(two_parts(values), spread)


def head_sums(values, spread):
    heads = spread.shape[0]
    high = values.astype(jnp.bfloat16)
    low = (values - high.astype(jnp.float32)).astype(jnp.bfloat16)
    total = nt_dot(high, spread) + nt_dot(low, spread)
    return total


def nt_dot(left, right):
    return lax.dot_general(
        left, right, (((1,), (1,)), ((), ())), preferred_element_type=jnp.float32
    )


def split_pair(pair, axis):
    lane = lax.broadcasted_iota(jnp.int32, pair.shape, 1)
    blank = jnp.zeros_like(pair)
    return jnp.concatenate(
        [jnp.where(lane < MHEAD_DIM, pair, blank), jnp.where(lane < MHEAD_DIM, blank, pair)],
        axis=axis,
    )


def bf(values):
    return values.astype(jnp.bfloat16)


def ssd_kernel(act_ref, cum_ref, cum_rows_ref, step_ref, spread_ref, y_ref, grown_ref, state_ref, tail_ref):
    chunks, rows, inner = y_ref.shape
    spread = spread_ref[...]
    state_ref[...] = jnp.zeros_like(state_ref)
    tail_ref[...] = jnp.zeros_like(tail_ref)
    late = lax.broadcasted_iota(jnp.int32, (rows, rows), 0) >= lax.broadcasted_iota(
        jnp.int32, (rows, rows), 1
    )

    def one_chunk(chunk, before):
        act = act_ref[chunk]
        cum = cum_ref[chunk]
        cum_rows = cum_rows_ref[chunk]
        scaled = act[:, :inner] * widen(step_ref[chunk], spread)
        input_mat = act[:, inner : inner + STATE]
        output_low = bf(act[:, inner + STATE :])
        last = cum[rows - 1 : rows, :]
        grown_ref[chunk] = widen(jnp.exp(cum + before), spread)
        mixing = nt_dot(output_low, bf(input_mat))
        state = state_ref[...]
        from_state = plain_dot(output_low, bf(state)) * widen(jnp.exp(cum), spread)
        scaled_low = bf(scaled)
        for pair in range(MHEADS // 2):
            kernels = []
            for head in (2 * pair, 2 * pair + 1):
                gap = cum[:, head : head + 1] - cum_rows[head : head + 1, :]
                kernels.append(bf(jnp.exp(jnp.where(late, gap, masked_score)) * mixing))
            span = slice(2 * pair * MHEAD_DIM, (2 * pair + 2) * MHEAD_DIM)
            y_ref[chunk, :, span] = from_state[:, span] + plain_dot(
                jnp.concatenate(kernels, axis=1), split_pair(scaled_low[:, span], 0)
            )
        weighted = scaled * widen(jnp.exp(last - cum), spread)
        fade = widen(jnp.exp(jnp.broadcast_to(last, (8, last.shape[1]))), spread)[:1]
        state_ref[...] = state * fade + plain_dot(bf(input_mat.T), bf(weighted))
        return before + last

    total = lax.fori_loop(0, chunks, one_chunk, jnp.zeros((1, cum_ref.shape[2]), jnp.float32))
    tail_ref[...] = widen(jnp.exp(jnp.broadcast_to(total, (8, total.shape[1]))), spread)


def by_chunks(values):
    return values.reshape(-1, math.gcd(values.shape[0], ssd_rows), values.shape[1])


def ssd_local(act, cum, step_size):
    act, cum, step_size = by_chunks(act), by_chunks(cum), by_chunks(step_size)
    chunks, rows, _ = act.shape
    inner = MHEADS * MHEAD_DIM
    return pl.pallas_call(
        ssd_kernel,
        out_shape=(
            jax.ShapeDtypeStruct((chunks, rows, inner), jnp.float32),
            jax.ShapeDtypeStruct((chunks, rows, inner), jnp.float32),
            jax.ShapeDtypeStruct((STATE, inner), jnp.float32),
            jax.ShapeDtypeStruct((8, inner), jnp.float32),
        ),
        in_specs=in_vmem(5),
        out_specs=tuple(in_vmem(4)),
        compiler_params=compiler_room,
        cost_estimate=pl.CostEstimate(
            flops=chunks * rows * inner * 10000, bytes_accessed=act.size * 16, transcendentals=0
        ),
        name="ssd",
    )(act, cum, jnp.swapaxes(cum, 1, 2), step_size, head_columns(MHEADS, 3))


def ssd_back_kernel(
    act_ref,
    cum_ref,
    cum_rows_ref,
    step_ref,
    grad_ref,
    carry_ref,
    grad_end_ref,
    skip_ref,
    spread_ref,
    grad_act_ref,
    grad_step_ref,
    grad_log_ref,
    grad_skip_ref,
    states_ref,
    grad_state_ref,
    sums_ref,
):
    chunks, rows, _ = act_ref.shape
    inner = grad_ref.shape[2]
    heads = cum_ref.shape[2]
    spread = spread_ref[...]
    one_spread = spread[:heads]
    at_row = lax.broadcasted_iota(jnp.int32, (rows, rows), 0)
    at_column = lax.broadcasted_iota(jnp.int32, (rows, rows), 1)

    def fade_of(last):
        return widen(jnp.exp(jnp.broadcast_to(last, (8, heads))), spread)[:1]

    states_ref[0] = carry_ref[...]
    for chunk in range(chunks - 1):
        cum = cum_ref[chunk]
        last = cum[rows - 1 : rows, :]
        act = act_ref[chunk]
        weighted = act[:, :inner] * widen(jnp.exp(last - cum) * step_ref[chunk], spread)
        states_ref[chunk + 1] = states_ref[chunk] * fade_of(last) + plain_dot(
            bf(act[:, inner : inner + STATE].T), bf(weighted)
        )
    grad_state_ref[...] = grad_end_ref[...]
    grad_skip_ref[...] = jnp.zeros_like(grad_skip_ref)
    sums_ref[...] = jnp.zeros_like(sums_ref)

    def one_chunk(turn, carried):
        chunk = chunks - 1 - turn
        act = act_ref[chunk]
        cum = cum_ref[chunk]
        cum_rows = cum_rows_ref[chunk]
        step = step_ref[chunk]
        grad_y = grad_ref[chunk]
        last = cum[rows - 1 : rows, :]
        inputs_x = act[:, :inner]
        step_wide = widen(step, spread)
        tail = jnp.exp(last - cum)
        tail_wide = widen(tail, spread)
        scaled = inputs_x * step_wide
        scaled_low = bf(scaled)
        grad_low = bf(grad_y)
        input_low = bf(act[:, inner : inner + STATE])
        output_mat = act[:, inner + STATE :]
        output_low = bf(output_mat)
        state = states_ref[chunk]
        state_low = bf(state)
        grad_state = grad_state_ref[...]
        grad_state_low = bf(grad_state)

        grown_grad = grad_y * widen(jnp.exp(cum), spread)
        grown_low = bf(grown_grad)
        from_row = head_sums(grown_grad * plain_dot(output_low, state_low), one_spread)
        grad_output = nt_dot(grown_low, state_low)
        back = plain_dot(input_low, grad_state_low)
        from_column = head_sums(scaled * back, one_spread) * tail
        grad_input = nt_dot(bf(scaled * tail_wide), grad_state_low)
        fade = fade_of(last)
        both = jnp.sum(grad_state * state, axis=0, keepdims=True) * fade
        from_last = head_sums(jnp.broadcast_to(both, (8, inner)), one_spread)[:1]
        grad_state_ref[...] = grad_state * fade + plain_dot(bf(output_mat.T), grown_low)

        mixing = nt_dot(input_low, output_low)
        grad_mixing = jnp.zeros((rows, rows), jnp.float32)
        column_sums = jnp.zeros((rows, rows), jnp.float32)
        grad_step = jnp.zeros((rows, rows), jnp.float32)
        for pair in range(heads // 2):
            span = slice(2 * pair * MHEAD_DIM, (2 * pair + 2) * MHEAD_DIM)
            apart = split_pair(grad_low[:, span], 0)
            grad_kernels = nt_dot(scaled_low[:, span], apart)
            kernels = []
            for side in range(2):
                head = 2 * pair + side
                gap = cum_rows[head : head + 1, :] - cum[:, head : head + 1]
                decay = jnp.exp(jnp.where(at_row <= at_column, gap, masked_score))
                part = grad_kernels[:, side * rows : (side + 1) * rows] * decay
                grad_mixing = grad_mixing + part
                moved = part * mixing
                sums_ref[head : head + 1, :] = jnp.sum(moved, axis=0, keepdims=True)
                column = jnp.sum(moved, axis=1, keepdims=True)
                column_sums = jnp.where(at_column == head, column, column_sums)
                kernels.append(bf(decay * mixing))
            grad_scaled = plain_dot(jnp.concatenate(kernels, axis=1), apart)
            grad_scaled = grad_scaled + back[:, span] * tail_wide[:, span]
            grad_act_ref[chunk, :, span] = (
                grad_scaled * step_wide[:, span] + skip_ref[:, span] * grad_y[:, span]
            )
            by_step = grad_scaled * inputs_x[:, span]
            lane = lax.broadcasted_iota(jnp.int32, by_step.shape, 1)
            for side in range(2):
                mine = jnp.where((lane < MHEAD_DIM) == (side == 0), by_step, 0.0)
                column = jnp.sum(mine, axis=1, keepdims=True)
                grad_step = jnp.where(at_column == 2 * pair + side, column, grad_step)
        grad_mixing_low = bf(grad_mixing)
        grad_act_ref[chunk, :, inner : inner + STATE] = grad_input + plain_dot(
            grad_mixing_low, output_low
        )
        grad_act_ref[chunk, :, inner + STATE :] = grad_output + plain_dot(
            bf(grad_mixing.T), input_low
        )
        grad_step_ref[chunk] = grad_step[:, :heads]
        row_sums = sums_ref[...].T[:, :heads]
        ahead = row_sums - column_sums[:, :heads] + from_row
        from_here = jnp.where(at_row <= at_column, 1.0, 0.0)
        before = jnp.where(at_row > at_column, 1.0, 0.0)
        grad_log_ref[chunk] = (
            jnp.dot(from_here, ahead, precision=highest_precision)
            + jnp.dot(before, from_column, precision=highest_precision)
            + from_last
        )
        grad_skip_ref[...] += jnp.sum(inputs_x * grad_y, axis=0, keepdims=True)
        return carried

    lax.fori_loop(0, chunks, one_chunk, 0)


def ssd_back(act, cum, step_size, grad_y, carry_state, grad_end, skip_row):
    shape = act.shape
    act, cum, step_size, grad_y = (by_chunks(a) for a in (act, cum, step_size, grad_y))
    chunks, rows, width = act.shape
    inner = MHEADS * MHEAD_DIM
    grad_act, grad_step, grad_log, grad_skip = pl.pallas_call(
        ssd_back_kernel,
        out_shape=(
            jax.ShapeDtypeStruct(act.shape, jnp.float32),
            jax.ShapeDtypeStruct(cum.shape, jnp.float32),
            jax.ShapeDtypeStruct(cum.shape, jnp.float32),
            jax.ShapeDtypeStruct((1, inner), jnp.float32),
        ),
        in_specs=in_vmem(9),
        out_specs=tuple(in_vmem(4)),
        scratch_shapes=[
            pltpu.VMEM((chunks, STATE, inner), jnp.float32),
            pltpu.VMEM((STATE, inner), jnp.float32),
            pltpu.VMEM((rows, rows), jnp.float32),
        ],
        compiler_params=compiler_room,
        cost_estimate=pl.CostEstimate(
            flops=chunks * rows * inner * 25000, bytes_accessed=act.size * 16, transcendentals=0
        ),
        name="ssd_back",
    )(
        act,
        cum,
        jnp.swapaxes(cum, 1, 2),
        step_size,
        grad_y,
        carry_state,
        grad_end,
        skip_row,
        head_columns(MHEADS, 3),
    )
    flat = (shape[0], MHEADS)
    return grad_act.reshape(shape), grad_step.reshape(flat), grad_log.reshape(flat), grad_skip


def shifted(block, axis, distance):
    count = lax.axis_size(axis)
    return lax.ppermute(block, axis, [(i, (i + distance) % count) for i in range(count)])


def moved_along(block, axis, distance):
    count = lax.axis_size(axis)
    route = [(i, i + distance) for i in range(count) if 0 <= i + distance < count]
    return lax.ppermute(block, axis, route)


def width_order(width):
    sizes = {axis: lax.axis_size(axis) for axis in every_axis}
    rows = width // math.prod(sizes.values())
    rest = lax.broadcasted_iota(jnp.int32, (width, width), 1)
    inside, rest = rest % rows, rest // rows
    owner = {}
    for axis in ("z", "x", "y", "core"):
        owner[axis] = (rest % sizes[axis] + lax.axis_index(axis)) % sizes[axis]
        rest = rest // sizes[axis]
    usual = owner["y"]
    for axis in ("core", "z", "x"):
        usual = usual * sizes[axis] + owner[axis]
    usual = usual * rows + inside
    return (lax.broadcasted_iota(jnp.int32, (width, width), 0) == usual).astype(jnp.bfloat16)


def after(values, *others):
    return lax.optimization_barrier((values, others))[0]


def gather_stages(shard):
    parts = [shard] + [shifted(shard, "z", -k) for k in range(1, lax.axis_size("z"))]
    block = jnp.concatenate(parts, axis=0)[None, None]
    middle = shard.shape[1] // 256 * 128
    halves = []
    for half, axes in ((block[..., :middle], "xy"), (block[..., middle:], "yx")):
        for axis in axes:
            parts = [half] + [shifted(half, axis, -k) for k in range(1, lax.axis_size(axis))]
            half = jnp.concatenate(parts, axis="yx".index(axis))
        halves.append(half.reshape(-1, half.shape[-1]))
    own = jnp.concatenate(halves, axis=1)
    return own, shifted(own, "core", 1)


def times_rows(values, pair):
    half = values.shape[1] // 2
    return plain_dot(values[:, :half], pair[0]) + plain_dot(values[:, half:], pair[1])


def times_rows_back(values, pair):
    return jnp.concatenate([back_product(values, pair[0]), back_product(values, pair[1])], axis=1)


def keep_own(total, axis, dim, received, hold=()):
    kept = lax.index_in_dim(total, 0, dim, False)
    for step in range(1, lax.axis_size(axis)):
        part = lax.index_in_dim(total, step, dim, False)
        got = shifted(part.astype(jnp.bfloat16), axis, step)
        received.append(got)
        if hold:
            got = after(got, *hold)
        kept = kept + got.astype(jnp.float32)
    return kept


def core_sum(left, right, received):
    half = left.shape[1] // 2
    sizes = [lax.axis_size(axis) for axis in ("y", "x", "z")]
    got = shifted(outer_product(left[:, half:], right).astype(jnp.bfloat16), "core", 1)
    received.append(got)
    total = outer_product(left[:, :half], right) + got.astype(jnp.float32)
    return total.reshape(*sizes, -1, right.shape[1])


def side_by_side(parts):
    return parts[0] if len(parts) == 1 else jnp.concatenate(parts, axis=-1)


def first_sums(by_x, by_y, received):
    by_x = side_by_side([keep_own(total, "x", 1, received) for total in by_x])
    by_y = side_by_side([keep_own(total, "y", 0, received) for total in by_y])
    return by_x, by_y


def layer_sums(by_x, by_y, received, hold=()):
    by_x = keep_own(by_x, "y", 0, received, hold)
    by_y = keep_own(by_y, "x", 0, received, hold)
    return jnp.concatenate([by_x, by_y], axis=-1)


def send_layers(total):
    parts = [total[step].astype(jnp.bfloat16) for step in range(1, total.shape[0])]
    return [total[0]] + [shifted(part, "z", step + 1) for step, part in enumerate(parts)]


def sum_layers(parts):
    return sum(part.astype(jnp.float32) for part in parts)


def sum_everywhere(values, holds):
    for axis in ("core", "x", "y", "z"):
        if axis in holds:
            values = after(values, *holds[axis])
        count = lax.axis_size(axis)
        step = 1
        while step < count:
            values = values + lax.ppermute(values, axis, [(i, i ^ step) for i in range(count)])
            step *= 2
    return values


def send_states(state, tail, direction):
    depth, width = state.shape
    half = width // 2
    at_x = lax.axis_index("x")
    is_second = (at_x == 1) if direction == 1 else (at_x == 0)
    packed = jnp.concatenate([state, tail], axis=0).astype(jnp.bfloat16)
    other = shifted(packed, "x", 1)
    own = packed.astype(jnp.float32)
    first = jnp.where(is_second, other.astype(jnp.float32), own)
    second = jnp.where(is_second, own, other.astype(jnp.float32))
    pair = jnp.concatenate(
        [
            second[depth : depth + 1] * first[:depth] + second[:depth],
            first[depth:] * second[depth:],
        ],
        axis=0,
    )
    mine = jnp.where(at_x == 0, pair[:, :half], pair[:, half:]).astype(jnp.bfloat16)
    steps = range(1, lax.axis_size("z"))
    passed = [moved_along(mine, "z", direction * step) for step in steps]
    return jnp.where(is_second, first, 0.0), other, passed


def carried(behind, passed, direction):
    depth, half = behind.shape[0] - 8, behind.shape[1] // 2
    at_x = lax.axis_index("x")
    is_second = (at_x == 1) if direction == 1 else (at_x == 0)
    total = jnp.zeros((depth, half), jnp.float32)
    fade = jnp.ones((1, half), jnp.float32)
    for got in passed:
        got = got.astype(jnp.float32)
        total = total + fade * got[:depth]
        fade = fade * got[depth : depth + 1]
    total = total.astype(jnp.bfloat16)
    rest = shifted(total, "x", 1)
    left, right = jnp.where(at_x == 0, total, rest), jnp.where(at_x == 0, rest, total)
    carry = jnp.concatenate([left, right], axis=1).astype(jnp.float32)
    return jnp.where(is_second, behind[depth : depth + 1], 1.0) * carry + behind[:depth]


def keys_behind(own):
    return [moved_along(own, "z", step) if step else own for step in range(lax.axis_size("z"))]


def all_slots(blocks):
    blocks = jnp.stack(blocks)
    slots = jnp.stack([blocks, shifted(blocks, "x", 1)], axis=1)
    return slots.reshape(-1, *blocks.shape[1:])


def swap_key_grads(slots):
    total = slots.reshape(-1, 2, *slots.shape[1:])
    swapped = shifted(total[:, 1].astype(jnp.bfloat16), "x", 1)
    return total[:, 0], swapped


def sum_key_grads(kept, swapped, received):
    kept = kept + swapped.astype(jnp.float32)
    own = kept[0]
    for step in range(1, kept.shape[0]):
        got = moved_along(kept[step].astype(jnp.bfloat16), "z", -step)
        received.append(got)
        own = own + got.astype(jnp.float32)
    return own


def on_device(
    tokens,
    gain_one,
    w_in,
    w_step,
    conv_weight,
    conv_bias,
    mamba_heads,
    skip_weight,
    w_query,
    w_keyval,
    w_attn_out,
    w_mix_out,
    gain_two,
    w_gate_up,
    w_down,
    cotangent,
):
    width = tokens.shape[2]
    row_count = tokens.shape[1]
    inner_width = MHEADS * MHEAD_DIM
    device_count = math.prod(lax.axis_size(axis) for axis in every_axis)
    channels = conv_weight.shape[1] * device_count
    key_width = KVHEADS * HEAD_DIM
    query_width = QHEADS * HEAD_DIM
    own_rows = gain_one.shape[0]
    at_z, at_x = lax.axis_index("z"), lax.axis_index("x")
    place = jnp.stack([at_z, at_x]).astype(jnp.int32)

    taps = jnp.concatenate([conv_weight, conv_bias[None]], axis=0)
    tap_columns = -(-taps.size // own_rows)
    tap_shard = jnp.pad(taps.reshape(-1), (0, tap_columns * own_rows - taps.size))
    query_at = channels + w_keyval.shape[1]
    step_at = query_at + query_width
    gain_at = step_at + w_step.shape[1]
    tap_at = gain_at + 2
    conv_shard = jnp.concatenate(
        [
            w_in[:, inner_width:],
            w_keyval,
            w_query,
            w_step,
            gain_one[:, None],
            gain_two[:, None],
            tap_shard.reshape(tap_columns, own_rows).T,
            jnp.zeros((own_rows, -(tap_at + tap_columns) % 128), jnp.bfloat16),
        ],
        axis=1,
    )
    late_shards = [w_in[:, :inner_width], w_mix_out.T, w_attn_out.T, w_gate_up, w_down.T]
    late = lax.all_gather(jnp.concatenate(late_shards, axis=1), every_axis, axis=0, tiled=True)
    out_at = inner_width
    ff_at = out_at + inner_width + query_width
    full_gate_z, full_out, full_gate, full_up, full_down = jnp.split(
        late, [out_at, ff_at, ff_at + FF, ff_at + 2 * FF], axis=1
    )
    conv_pair = gather_stages(conv_shard)

    order = lax.optimization_barrier(width_order(width))
    inputs = tokens[0].astype(jnp.float32)
    inputs_rows = plain_dot(tokens[0], order)
    grad_output = cotangent[0]
    small = jnp.concatenate([half[:, gain_at : tap_at + tap_columns] for half in conv_pair], axis=0)
    small_rows = lax.dot_general(
        small, order, (((0,), (1,)), ((), ())), preferred_element_type=jnp.float32
    )
    gain_one_float, gain_two_float = small_rows[0], small_rows[1]
    tap_all = small_rows[2:].reshape(tap_columns, device_count, own_rows)
    tap_all = jnp.swapaxes(tap_all, 0, 1).reshape(device_count, -1)[:, : taps.size]
    tap_all = jnp.swapaxes(tap_all.reshape(-1, *taps.shape), 0, 1).reshape(taps.shape[0], channels)

    normed = rms_norm(inputs_rows, small[:, 0].astype(jnp.float32)).astype(jnp.bfloat16)
    conv_projected = times_rows(normed, conv_pair)
    conv_input = conv_projected[:, :channels].astype(jnp.bfloat16)
    keyval_raw = conv_projected[:, channels:query_at]
    query_raw = conv_projected[:, query_at:step_at]
    step_raw = conv_projected[:, step_at:gain_at]
    positions = (at_z * lax.axis_size("x") + at_x) * row_count + jnp.arange(
        row_count, dtype=jnp.int32
    )
    cosine, sine = turn_columns(positions)
    keyval_cols = keyval_raw.T
    key_cols = turn_rows(keyval_cols[:key_width], cosine, sine)
    by_head = (KVHEADS, 1, HEAD_DIM, row_count)
    own_keyval = jnp.concatenate(
        [key_cols.reshape(by_head), keyval_cols[key_width:].reshape(by_head)], axis=1
    ).reshape(2 * key_width, row_count)
    key_blocks = keys_behind(own_keyval.T.astype(jnp.bfloat16))
    query_cols = turn_rows(query_raw.T, cosine, sine).astype(jnp.bfloat16)
    border = lax.ppermute(
        conv_input[row_count - (CONV - 1) :],
        seq_axes,
        [(i, i + 1) for i in range(lax.axis_size(seq_axes) - 1)],
    )
    extended = jnp.concatenate([border, conv_input], axis=0).astype(jnp.float32)
    act, pull_conv = jax.vjp(conv_act, extended, tap_all[:CONV], tap_all[CONV])
    step_size = jax.nn.softplus(step_raw + mamba_heads[1][None, :])
    log_decay = -jnp.exp(mamba_heads[0])[None, :] * step_size
    by_chunk = by_chunks(log_decay)
    chunk_rows = by_chunk.shape[1]
    lower = jnp.tril(jnp.ones((chunk_rows, chunk_rows), jnp.float32))
    cum = jnp.stack([jnp.dot(lower, c, precision=highest_precision) for c in by_chunk])
    cum = cum.reshape(log_decay.shape)
    y_local, grown, fresh_state, tail, *key_blocks = after(
        (*ssd_local(act, cum, step_size), *key_blocks)
    )
    all_keyval = all_slots(key_blocks)
    all_cols = jnp.swapaxes(all_keyval, 1, 2)
    y_local = y_local.reshape(row_count, inner_width)
    grown = grown.reshape(row_count, inner_width)
    behind, other_state, passed = send_states(fresh_state, tail, 1)
    attended_cols, logs = attend(place, after(query_cols, other_state), all_keyval, all_cols)
    attended_cols, logs, *passed = after((attended_cols, logs, *passed))
    carry_state = carried(behind, passed, 1)
    gate_z = plain_dot(back_product(normed, order).astype(jnp.bfloat16), full_gate_z)
    attention_rows = attended_cols.T.astype(jnp.bfloat16)

    skip_row = jnp.repeat(skip_weight, MHEAD_DIM)[None, :]
    output_low = act[:, inner_width + STATE :].astype(jnp.bfloat16)
    ssm_y = (
        y_local
        + grown * plain_dot(output_low, carry_state.astype(jnp.bfloat16))
        + skip_row * act[:, :inner_width]
    )
    gate_sigmoid = jax.nn.sigmoid(gate_z)
    mixer = (ssm_y * gate_z * gate_sigmoid).astype(jnp.bfloat16)
    branches = jnp.concatenate([mixer, attention_rows], axis=1)
    hidden = inputs + back_product(branches, full_out)
    normed_two = rms_norm(hidden, gain_two_float).astype(jnp.bfloat16)
    gate_part = plain_dot(normed_two, full_gate)
    up_part = plain_dot(normed_two, full_up)
    activated = (jax.nn.silu(gate_part) * up_part).astype(jnp.bfloat16)
    result = hidden + back_product(activated, full_down)
    output = result.astype(jnp.bfloat16)[None]

    def reordered(rows):
        return plain_dot(rows, order).astype(jnp.bfloat16)

    grad_activated = plain_dot(grad_output, full_down)
    core_got = []
    grad_output_rows = reordered(grad_output)
    down_half = FF // 2
    normed_two_rows = reordered(normed_two)
    ff_sigmoid = jax.nn.sigmoid(gate_part)
    grad_gate = grad_activated * up_part * ff_sigmoid * (1.0 + gate_part * (1.0 - ff_sigmoid))
    grad_gate = grad_gate.astype(jnp.bfloat16)
    grad_up = (grad_activated * gate_part * ff_sigmoid).astype(jnp.bfloat16)
    gate_total = core_sum(normed_two_rows, grad_gate, core_got)
    up_total = core_sum(normed_two_rows, grad_up, core_got)
    down_a = core_sum(grad_output_rows, activated[:, :down_half], [])
    down_b = core_sum(grad_output_rows, activated[:, down_half:], [])
    ff_got = []
    ff_later = []
    ff_parts = send_layers(
        layer_sums(*first_sums([gate_total, down_a], [up_total, down_b], ff_got), ff_later)
    )
    grad_normed_two = back_product(after(grad_gate, *core_got), full_gate) + back_product(grad_up, full_up)
    _, pull_two = jax.vjp(rms_norm, hidden, gain_two_float)
    grad_hidden_norm, grad_gain_two = pull_two(grad_normed_two)
    grad_hidden = grad_output.astype(jnp.float32) + grad_hidden_norm
    grad_branch = grad_hidden.astype(jnp.bfloat16)
    grad_branches = after(plain_dot(grad_branch, full_out), ff_got[1], ff_got[3])
    grad_mixer = grad_branches[:, :inner_width]
    grad_y = grad_mixer * gate_z * gate_sigmoid
    grad_gate_z = grad_mixer * ssm_y * gate_sigmoid * (1.0 + gate_z * (1.0 - gate_sigmoid))
    from_output = outer_product(output_low, (grown * grad_y).astype(jnp.bfloat16))
    behind, _, passed = send_states(from_output, tail, -1)

    grad_attention = grad_branches[:, inner_width:].astype(jnp.bfloat16)
    out_got = []
    out_total = core_sum(reordered(grad_branch), branches, out_got)
    grad_gate_low = grad_gate_z.astype(jnp.bfloat16)
    in_gate_total = core_sum(normed, grad_gate_low, out_got)
    grad_normed_part = back_product(grad_gate_low, full_gate_z)
    grad_cols = grad_attention.T
    query_rows = query_cols.T

    def one_group(group, grad_cols):
        return attend_back(
            group,
            place,
            query_cols,
            query_rows,
            grad_cols,
            grad_attention,
            attended_cols,
            logs,
            all_keyval,
            all_cols,
        )

    query_a, slots_a = one_group(0, after(grad_cols, gate_total, up_total))
    query_a, slots_a = after((query_a, slots_a), ff_got[0], ff_got[2])
    kept_a, swapped_a = swap_key_grads(slots_a)
    query_b, slots_b = one_group(1, after(grad_cols, ff_got[0], ff_got[2], *out_got))
    before_ssd = (query_b, *ff_later, swapped_a)
    query_b, slots_b, kept_a, swapped_a, *passed = after(
        (query_b, slots_b, kept_a, swapped_a, *passed), *before_ssd
    )
    grad_end = carried(behind, passed, -1)
    key_got = []
    own_a = sum_key_grads(kept_a, swapped_a, key_got)
    kept_b, swapped_b = swap_key_grads(slots_b)
    own_b = sum_key_grads(kept_b, swapped_b, key_got)
    own_grads = [own_a, own_b]
    grad_query_cols = jnp.concatenate([query_a, query_b], axis=0)
    mid_got = []
    mid_both = first_sums([in_gate_total], [out_total], mid_got)
    grad_query = turn_rows(grad_query_cols, cosine, -sine).T.astype(jnp.bfloat16)
    own_cols = jnp.concatenate(own_grads, axis=1).T.reshape(KVHEADS, 2, HEAD_DIM, row_count)
    grad_keys = turn_rows(own_cols[:, 0].reshape(key_width, row_count), cosine, -sine)
    grad_keyval = jnp.concatenate([grad_keys, own_cols[:, 1].reshape(key_width, row_count)], axis=0)
    grad_keyval = grad_keyval.T.astype(jnp.bfloat16)

    ssd_grad = after(
        grad_y, *before_ssd, swapped_b, *out_got, grad_normed_part
    )
    grad_act, grad_step_size, grad_log, grad_skip = ssd_back(
        act, cum, step_size, ssd_grad, carry_state, grad_end, skip_row
    )
    grad_act, grad_step_size, grad_log = after((grad_act, grad_step_size, grad_log), *key_got)
    grad_step_size = grad_step_size - grad_log * jnp.exp(mamba_heads[0])[None, :]
    grad_step_raw = grad_step_size * jax.nn.sigmoid(step_raw + mamba_heads[1][None, :])
    grad_heads = jnp.stack([jnp.sum(grad_log * log_decay, axis=0), jnp.sum(grad_step_raw, axis=0)])
    grad_extended, grad_conv_weight, grad_conv_bias = pull_conv(grad_act)
    grad_extended, *ff_parts = after((grad_extended, *ff_parts), *mid_got)
    ff_sums = sum_layers(ff_parts)
    rim_back = lax.ppermute(
        grad_extended[: CONV - 1],
        seq_axes,
        [(i + 1, i) for i in range(lax.axis_size(seq_axes) - 1)],
    )
    grad_conv_input = grad_extended[CONV - 1 :] + jnp.pad(
        rim_back, ((row_count - (CONV - 1), 0), (0, 0))
    )
    grad_step_low = jnp.pad(
        grad_step_raw.astype(jnp.bfloat16), ((0, 0), (0, conv_shard.shape[1] - gain_at))
    )
    grad_few = jnp.concatenate([grad_keyval, grad_query, grad_step_low], axis=1)
    few_core_got, last_core_got = [], []
    few_total = core_sum(normed, grad_few, few_core_got)
    grad_conv_low = after(grad_conv_input.astype(jnp.bfloat16), *few_core_got)
    conv_total = core_sum(normed, grad_conv_low, last_core_got)
    last_got, last_later = [], []
    mid_parts = send_layers(layer_sums(*mid_both, [], last_core_got))
    last_parts = send_layers(
        layer_sums(*first_sums([conv_total], [few_total], last_got), last_later)
    )
    last_parts, *mid_parts = after((tuple(last_parts), *mid_parts), *last_later)
    last_sums, mid_sums = sum_layers(last_parts), sum_layers(mid_parts)
    grad_normed = lax.dot_general(
        times_rows_back(jnp.concatenate([grad_conv_low, grad_few], axis=1), conv_pair),
        order.astype(jnp.float32),
        (((1,), (1,)), ((), ())),
        precision=lax.Precision.HIGH,
        preferred_element_type=jnp.float32,
    )
    _, pull_one = jax.vjp(rms_norm, inputs, gain_one_float)
    grad_input_norm, grad_gain_one = pull_one(grad_normed + grad_normed_part)
    input_grad = (grad_hidden + grad_input_norm)[None]

    def padded(row):
        return jnp.pad(row, ((0, 0), (0, channels - row.shape[1])))

    head_row = jnp.concatenate(
        [grad_heads[:1], grad_heads[1:], jnp.sum(grad_skip.reshape(MHEADS, -1), axis=1)[None]],
        axis=1,
    )
    summed = sum_everywhere(
        after(
            jnp.concatenate(
                [
                    grad_conv_weight,
                    grad_conv_bias[None],
                    padded(grad_gain_two[None]),
                    padded(grad_gain_one[None]),
                    padded(head_row),
                ],
                axis=0,
            ),
            *last_core_got,
        ),
        {"y": last_got, "z": last_later},
    )
    device = lax.axis_index(every_axis)
    own_channels = conv_weight.shape[1]
    own_taps = lax.dynamic_slice_in_dim(summed[: CONV + 1], device * own_channels, own_channels, 1)
    own_gain_two = lax.dynamic_slice_in_dim(summed[CONV + 1], device * own_rows, own_rows)
    own_gain_one = lax.dynamic_slice_in_dim(summed[CONV + 2], device * own_rows, own_rows)
    head_sums_row = summed[CONV + 3]
    return (
        output,
        input_grad,
        own_gain_one,
        jnp.concatenate([mid_sums[:, :inner_width], last_sums[:, :channels]], axis=1),
        last_sums[:, step_at:gain_at],
        own_taps[:CONV],
        own_taps[CONV],
        head_sums_row[: 2 * MHEADS].reshape(2, MHEADS),
        head_sums_row[2 * MHEADS : 3 * MHEADS],
        last_sums[:, query_at:step_at],
        last_sums[:, channels:query_at],
        mid_sums[:, 2 * inner_width :].T,
        mid_sums[:, inner_width : 2 * inner_width].T,
        own_gain_two,
        jnp.concatenate([ff_sums[:, :FF], ff_sums[:, FF + down_half : 2 * FF + down_half]], axis=1),
        jnp.concatenate(
            [ff_sums[:, FF : FF + down_half], ff_sums[:, 2 * FF + down_half :]], axis=1
        ).T,
    )


def solution(mesh):
    dp, seq = mesh.shape["dp"], mesh.shape["seq"]
    by_axis = Mesh(mesh.devices.reshape(dp // 2, 2, seq // 2, 2), every_axis)
    pieces = P(("y", "core"), seq_axes, None)
    rows = P(every_axis, None)
    columns = P(None, every_axis)
    vector = P(every_axis)
    weights = (rows, rows, columns, columns, vector, rows, columns)
    return jax.shard_map(
        on_device,
        mesh=by_axis,
        in_specs=(pieces, vector, rows, rows, columns, vector, P(), P(), *weights, pieces),
        out_specs=(pieces, pieces, vector, rows, rows, columns, vector, P(), P(), *weights),
        check_vma=False,
    )
```

```python
import math
from functools import partial

import jax
import jax.experimental.pallas as pl
import jax.experimental.pallas.tpu as pltpu
import jax.numpy as jnp
from jax import lax
from jax.sharding import Mesh
from jax.sharding import PartitionSpec as P

MHEADS = 24
MHEAD_DIM = 64
STATE = 128
CONV = 4
QHEADS = 8
KVHEADS = 2
HEAD_DIM = 64
FF = 2048


norm_epsilon = 1e-06
rope_base = 100000000000.0
masked_score = -1e30
highest_precision = lax.Precision.HIGHEST
seq_axes = ("z", "x")
every_axis = ("y", "core", "z", "x")


def rms_norm(values, gain_vector):
    return (
        values
        * lax.rsqrt(jnp.mean(values * values, axis=-1, keepdims=True) + norm_epsilon)
        * gain_vector
    )


def outer_product(left, right):
    return lax.dot_general(
        left, right, (((0,), (0,)), ((), ())), preferred_element_type=jnp.float32
    )


def back_product(grad_rows, weight_matrix):
    return lax.dot_general(
        grad_rows, weight_matrix, (((1,), (1,)), ((), ())), preferred_element_type=jnp.float32
    )


def turn_columns(positions):
    half = HEAD_DIM // 2
    exponents = jnp.arange(half).astype(jnp.float32) * (2.0 / HEAD_DIM)
    frequency = rope_base ** (-exponents)
    angles = frequency[:, None] * positions.astype(jnp.float32)[None, :]
    return (jnp.cos(angles), jnp.sin(angles))


def turn_rows(values, cosine, sine):
    half = HEAD_DIM // 2
    heads = values.reshape(-1, 2, half, values.shape[1])
    first, second = heads[:, 0], heads[:, 1]
    turned = [first * cosine - second * sine, second * cosine + first * sine]
    return jnp.stack(turned, axis=1).reshape(values.shape)


def conv_act(extended, conv_weight, conv_bias):
    row_count = extended.shape[0] - (CONV - 1)
    conv_sum = conv_bias[None, :] + conv_weight[0][None, :] * extended[0:row_count]
    for offset in range(1, CONV):
        conv_sum = conv_sum + conv_weight[offset][None, :] * extended[offset : offset + row_count]
    return jax.nn.silu(conv_sum)


log2_e = math.log2(math.e)
group_size = QHEADS // KVHEADS
score_scale = 1.0 / math.sqrt(HEAD_DIM)
compiler_room = pltpu.CompilerParams(vmem_limit_bytes=48 * 1024 * 1024)


def plain_dot(left, right):
    return jnp.dot(left, right, preferred_element_type=jnp.float32)


def head_span(head):
    return slice(head * HEAD_DIM, (head + 1) * HEAD_DIM)


def hidden_keys(rows):
    key_at = lax.broadcasted_iota(jnp.int32, (rows, rows), 0)
    query_at = lax.broadcasted_iota(jnp.int32, (rows, rows), 1)
    return key_at > query_at


def slot_of(index, place_ref):
    z, x = lax.shift_right_logical(index, 1), lax.bitwise_and(index, 1)
    return 2 * (place_ref[0] - z) + lax.bitwise_xor(x, place_ref[1])


def attend_kernel(place_ref, query_ref, keyval_ref, keyval_cols_ref, out_ref, log_ref, best_ref, sum_ref):
    rows = query_ref.shape[1]
    scale = log2_e * score_scale

    def scores_of(piece, head):
        group = head // group_size
        keys = keyval_ref[piece, :, 2 * group * HEAD_DIM : 2 * (group + 1) * HEAD_DIM]
        query = query_ref[head_span(head), :]
        return plain_dot(keys, jnp.concatenate([query, jnp.zeros_like(query)], axis=0)) * scale

    def values_of(piece, head):
        return keyval_cols_ref[piece, head_span(2 * (head // group_size) + 1), :]

    for head in range(QHEADS):
        scores = jnp.where(hidden_keys(rows), masked_score, scores_of(0, head))
        best = jnp.max(scores, axis=0, keepdims=True)
        weights = jnp.exp2(scores - best)
        best_ref[head : head + 1, :] = best
        sum_ref[head : head + 1, :] = jnp.sum(weights, axis=0, keepdims=True)
        out_ref[head_span(head), :] = plain_dot(values_of(0, head), weights.astype(jnp.bfloat16))

    def piece_step(index, carry):
        piece = slot_of(index, place_ref)
        for head in range(QHEADS):
            scores = scores_of(piece, head)
            old = best_ref[head : head + 1, :]
            best = jnp.maximum(old, jnp.max(scores, axis=0, keepdims=True))
            fade = jnp.exp2(old - best)
            weights = jnp.exp2(scores - best)
            best_ref[head : head + 1, :] = best
            sum_ref[head : head + 1, :] = sum_ref[head : head + 1, :] * fade + jnp.sum(
                weights, axis=0, keepdims=True
            )
            out_ref[head_span(head), :] = out_ref[head_span(head), :] * fade + plain_dot(
                values_of(piece, head), weights.astype(jnp.bfloat16)
            )
        return carry

    lax.fori_loop(0, 2 * place_ref[0] + place_ref[1], piece_step, 0)
    total = sum_ref[...]
    log_ref[...] = best_ref[...] + jnp.log2(total)
    for head in range(QHEADS):
        out_ref[head_span(head), :] = out_ref[head_span(head), :] / total[head : head + 1, :]


def in_vmem(count):
    return [pl.BlockSpec(memory_space=pltpu.VMEM)] * count


def attend(place, queries, keyvals, keyval_cols):
    rows = queries.shape[1]
    flops = 4 * queries.size * rows * keyvals.shape[0]
    return pl.pallas_call(
        attend_kernel,
        out_shape=(
            jax.ShapeDtypeStruct(queries.shape, jnp.float32),
            jax.ShapeDtypeStruct((QHEADS, rows), jnp.float32),
        ),
        in_specs=[pl.BlockSpec(memory_space=pltpu.SMEM)] + in_vmem(3),
        out_specs=tuple(in_vmem(2)),
        scratch_shapes=[pltpu.VMEM((QHEADS, rows), jnp.float32)] * 2,
        compiler_params=compiler_room,
        cost_estimate=pl.CostEstimate(
            flops=8 * flops, bytes_accessed=4 * keyvals.size, transcendentals=flops // 256
        ),
        name="attend",
    )(place, queries, keyvals, keyval_cols)


def attend_back_kernel(
    group,
    place_ref,
    query_ref,
    query_rows_ref,
    grad_ref,
    grad_rows_ref,
    out_ref,
    log_ref,
    keyval_ref,
    keyval_cols_ref,
    grad_query_ref,
    grad_own_ref,
    grad_other_ref,
    dots_ref,
    query_side_ref,
    grad_side_ref,
):
    rows = query_ref.shape[1]
    scale = log2_e * score_scale
    grad_query_ref[...] = jnp.zeros_like(grad_query_ref)
    for j in range(group_size):
        span = head_span(group * group_size + j)
        dots_ref[j : j + 1, :] = jnp.sum(
            grad_ref[span, :].astype(jnp.float32) * out_ref[span, :], axis=0, keepdims=True
        )
        query = (query_rows_ref[:, span].astype(jnp.float32) * score_scale).astype(jnp.bfloat16)
        grad = grad_rows_ref[:, span]
        query_side_ref[j] = jnp.concatenate([query, jnp.zeros_like(query)], axis=1)
        grad_side_ref[j] = jnp.concatenate([jnp.zeros_like(grad), grad], axis=1)

    def one_piece(piece, own):
        keyvals = keyval_ref[piece, :, 2 * group * HEAD_DIM : 2 * (group + 1) * HEAD_DIM]
        key_cols = keyval_cols_ref[piece, head_span(2 * group), :]
        total = jnp.zeros((rows, 2 * HEAD_DIM), jnp.float32)
        for j in range(group_size):
            head = group * group_size + j
            query, grad = query_ref[head_span(head), :], grad_ref[head_span(head), :]
            blank = jnp.zeros_like(query)
            scores = plain_dot(keyvals, jnp.concatenate([query, blank], axis=0)) * scale
            weights = jnp.exp2(scores - log_ref[head : head + 1, :])
            if own:
                weights = jnp.where(hidden_keys(rows), 0.0, weights)
            grad_weights = plain_dot(keyvals, jnp.concatenate([blank, grad], axis=0))
            grad_scores = (weights * (grad_weights - dots_ref[j : j + 1, :])).astype(jnp.bfloat16)
            grad_query_ref[head_span(j), :] += plain_dot(key_cols, grad_scores)
            total = total + plain_dot(grad_scores, query_side_ref[j])
            total = total + plain_dot(weights.astype(jnp.bfloat16), grad_side_ref[j])
        behind = lax.shift_right_logical(piece, 1) if not own else 0
        if own:
            grad_own_ref[0] = total
            return

        @pl.when(lax.bitwise_and(piece, 1) == 0)
        def _():
            grad_own_ref[behind] = total

        @pl.when(lax.bitwise_and(piece, 1) == 1)
        def _():
            grad_other_ref[behind] = total.astype(jnp.bfloat16)

    def clear(step, carry):
        grad_own_ref[step] = jnp.zeros(grad_own_ref.shape[1:], jnp.float32)
        grad_other_ref[step] = jnp.zeros(grad_other_ref.shape[1:], jnp.bfloat16)
        return carry

    def earlier(index, carry):
        one_piece(slot_of(index, place_ref), False)
        return carry

    lax.fori_loop(0, grad_own_ref.shape[0], clear, 0)
    one_piece(0, True)
    lax.fori_loop(0, 2 * place_ref[0] + place_ref[1], earlier, 0)
    grad_query_ref[...] = grad_query_ref[...] * score_scale


def attend_back(group, place, queries, query_rows, grads, grad_rows, outs, logs, keyvals, keyval_cols):
    rows = queries.shape[1]
    flops = 10 * queries.size * rows * keyvals.shape[0] // KVHEADS
    return pl.pallas_call(
        partial(attend_back_kernel, group),
        out_shape=(
            jax.ShapeDtypeStruct((group_size * HEAD_DIM, rows), jnp.float32),
            jax.ShapeDtypeStruct((keyvals.shape[0] // 2, rows, 2 * HEAD_DIM), jnp.float32),
            jax.ShapeDtypeStruct((keyvals.shape[0] // 2, rows, 2 * HEAD_DIM), jnp.bfloat16),
        ),
        in_specs=[pl.BlockSpec(memory_space=pltpu.SMEM)] + in_vmem(8),
        out_specs=tuple(in_vmem(3)),
        scratch_shapes=[
            pltpu.VMEM((8, rows), jnp.float32),
            pltpu.VMEM((group_size, rows, 2 * HEAD_DIM), jnp.bfloat16),
            pltpu.VMEM((group_size, rows, 2 * HEAD_DIM), jnp.bfloat16),
        ],
        compiler_params=compiler_room,
        cost_estimate=pl.CostEstimate(
            flops=6 * flops, bytes_accessed=4 * keyvals.size, transcendentals=flops // 640
        ),
        name="attend_back_" + str(group),
    )(place, queries, query_rows, grads, grad_rows, outs, logs, keyvals, keyval_cols)


ssd_rows = 128


def two_parts(values):
    high = values.astype(jnp.bfloat16)
    rest = values - high.astype(jnp.float32)
    middle = rest.astype(jnp.bfloat16)
    low = (rest - middle.astype(jnp.float32)).astype(jnp.bfloat16)
    return jnp.concatenate([high, middle, low], axis=1)


def head_columns(heads, parts):
    shape = (heads * parts, heads * MHEAD_DIM)
    head = lax.broadcasted_iota(jnp.int32, shape, 0) % heads
    channel = lax.broadcasted_iota(jnp.int32, shape, 1) // MHEAD_DIM
    return jnp.where(head == channel, 1.0, 0.0).astype(jnp.bfloat16)


def widen(values, spread):
    return plain_dot(two_parts(values), spread)


def head_sums(values, spread):
    heads = spread.shape[0]
    high = values.astype(jnp.bfloat16)
    low = (values - high.astype(jnp.float32)).astype(jnp.bfloat16)
    total = nt_dot(high, spread) + nt_dot(low, spread)
    return total


def nt_dot(left, right):
    return lax.dot_general(
        left, right, (((1,), (1,)), ((), ())), preferred_element_type=jnp.float32
    )


def split_pair(pair, axis):
    lane = lax.broadcasted_iota(jnp.int32, pair.shape, 1)
    blank = jnp.zeros_like(pair)
    return jnp.concatenate(
        [jnp.where(lane < MHEAD_DIM, pair, blank), jnp.where(lane < MHEAD_DIM, blank, pair)],
        axis=axis,
    )


def bf(values):
    return values.astype(jnp.bfloat16)


def ssd_kernel(act_ref, cum_ref, cum_rows_ref, step_ref, spread_ref, y_ref, grown_ref, state_ref, tail_ref):
    chunks, rows, inner = y_ref.shape
    spread = spread_ref[...]
    state_ref[...] = jnp.zeros_like(state_ref)
    tail_ref[...] = jnp.zeros_like(tail_ref)
    late = lax.broadcasted_iota(jnp.int32, (rows, rows), 0) >= lax.broadcasted_iota(
        jnp.int32, (rows, rows), 1
    )

    def one_chunk(chunk, before):
        act = act_ref[chunk]
        cum = cum_ref[chunk]
        cum_rows = cum_rows_ref[chunk]
        scaled = act[:, :inner] * widen(step_ref[chunk], spread)
        input_mat = act[:, inner : inner + STATE]
        output_low = bf(act[:, inner + STATE :])
        last = cum[rows - 1 : rows, :]
        grown_ref[chunk] = widen(jnp.exp(cum + before), spread)
        mixing = nt_dot(output_low, bf(input_mat))
        state = state_ref[...]
        from_state = plain_dot(output_low, bf(state)) * widen(jnp.exp(cum), spread)
        scaled_low = bf(scaled)
        for pair in range(MHEADS // 2):
            kernels = []
            for head in (2 * pair, 2 * pair + 1):
                gap = cum[:, head : head + 1] - cum_rows[head : head + 1, :]
                kernels.append(bf(jnp.exp(jnp.where(late, gap, masked_score)) * mixing))
            span = slice(2 * pair * MHEAD_DIM, (2 * pair + 2) * MHEAD_DIM)
            y_ref[chunk, :, span] = from_state[:, span] + plain_dot(
                jnp.concatenate(kernels, axis=1), split_pair(scaled_low[:, span], 0)
            )
        weighted = scaled * widen(jnp.exp(last - cum), spread)
        fade = widen(jnp.exp(jnp.broadcast_to(last, (8, last.shape[1]))), spread)[:1]
        state_ref[...] = state * fade + plain_dot(bf(input_mat.T), bf(weighted))
        return before + last

    total = lax.fori_loop(0, chunks, one_chunk, jnp.zeros((1, cum_ref.shape[2]), jnp.float32))
    tail_ref[...] = widen(jnp.exp(jnp.broadcast_to(total, (8, total.shape[1]))), spread)


def by_chunks(values):
    return values.reshape(-1, math.gcd(values.shape[0], ssd_rows), values.shape[1])


def ssd_local(act, cum, step_size):
    act, cum, step_size = by_chunks(act), by_chunks(cum), by_chunks(step_size)
    chunks, rows, _ = act.shape
    inner = MHEADS * MHEAD_DIM
    return pl.pallas_call(
        ssd_kernel,
        out_shape=(
            jax.ShapeDtypeStruct((chunks, rows, inner), jnp.float32),
            jax.ShapeDtypeStruct((chunks, rows, inner), jnp.float32),
            jax.ShapeDtypeStruct((STATE, inner), jnp.float32),
            jax.ShapeDtypeStruct((8, inner), jnp.float32),
        ),
        in_specs=in_vmem(5),
        out_specs=tuple(in_vmem(4)),
        compiler_params=compiler_room,
        cost_estimate=pl.CostEstimate(
            flops=chunks * rows * inner * 10000, bytes_accessed=act.size * 16, transcendentals=0
        ),
        name="ssd",
    )(act, cum, jnp.swapaxes(cum, 1, 2), step_size, head_columns(MHEADS, 3))


def ssd_back_kernel(
    act_ref,
    cum_ref,
    cum_rows_ref,
    step_ref,
    grad_ref,
    carry_ref,
    grad_end_ref,
    skip_ref,
    spread_ref,
    grad_act_ref,
    grad_step_ref,
    grad_log_ref,
    grad_skip_ref,
    states_ref,
    grad_state_ref,
    sums_ref,
):
    chunks, rows, _ = act_ref.shape
    inner = grad_ref.shape[2]
    heads = cum_ref.shape[2]
    spread = spread_ref[...]
    one_spread = spread[:heads]
    at_row = lax.broadcasted_iota(jnp.int32, (rows, rows), 0)
    at_column = lax.broadcasted_iota(jnp.int32, (rows, rows), 1)

    def fade_of(last):
        return widen(jnp.exp(jnp.broadcast_to(last, (8, heads))), spread)[:1]

    states_ref[0] = carry_ref[...]
    for chunk in range(chunks - 1):
        cum = cum_ref[chunk]
        last = cum[rows - 1 : rows, :]
        act = act_ref[chunk]
        weighted = act[:, :inner] * widen(jnp.exp(last - cum) * step_ref[chunk], spread)
        states_ref[chunk + 1] = states_ref[chunk] * fade_of(last) + plain_dot(
            bf(act[:, inner : inner + STATE].T), bf(weighted)
        )
    grad_state_ref[...] = grad_end_ref[...]
    grad_skip_ref[...] = jnp.zeros_like(grad_skip_ref)
    sums_ref[...] = jnp.zeros_like(sums_ref)

    def one_chunk(turn, carried):
        chunk = chunks - 1 - turn
        act = act_ref[chunk]
        cum = cum_ref[chunk]
        cum_rows = cum_rows_ref[chunk]
        step = step_ref[chunk]
        grad_y = grad_ref[chunk]
        last = cum[rows - 1 : rows, :]
        inputs_x = act[:, :inner]
        step_wide = widen(step, spread)
        tail = jnp.exp(last - cum)
        tail_wide = widen(tail, spread)
        scaled = inputs_x * step_wide
        scaled_low = bf(scaled)
        grad_low = bf(grad_y)
        input_low = bf(act[:, inner : inner + STATE])
        output_mat = act[:, inner + STATE :]
        output_low = bf(output_mat)
        state = states_ref[chunk]
        state_low = bf(state)
        grad_state = grad_state_ref[...]
        grad_state_low = bf(grad_state)

        grown_grad = grad_y * widen(jnp.exp(cum), spread)
        grown_low = bf(grown_grad)
        from_row = head_sums(grown_grad * plain_dot(output_low, state_low), one_spread)
        grad_output = nt_dot(grown_low, state_low)
        back = plain_dot(input_low, grad_state_low)
        from_column = head_sums(scaled * back, one_spread) * tail
        grad_input = nt_dot(bf(scaled * tail_wide), grad_state_low)
        fade = fade_of(last)
        both = jnp.sum(grad_state * state, axis=0, keepdims=True) * fade
        from_last = head_sums(jnp.broadcast_to(both, (8, inner)), one_spread)[:1]
        grad_state_ref[...] = grad_state * fade + plain_dot(bf(output_mat.T), grown_low)

        mixing = nt_dot(input_low, output_low)
        grad_mixing = jnp.zeros((rows, rows), jnp.float32)
        column_sums = jnp.zeros((rows, rows), jnp.float32)
        grad_step = jnp.zeros((rows, rows), jnp.float32)
        for pair in range(heads // 2):
            span = slice(2 * pair * MHEAD_DIM, (2 * pair + 2) * MHEAD_DIM)
            apart = split_pair(grad_low[:, span], 0)
            grad_kernels = nt_dot(scaled_low[:, span], apart)
            kernels = []
            for side in range(2):
                head = 2 * pair + side
                gap = cum_rows[head : head + 1, :] - cum[:, head : head + 1]
                decay = jnp.exp(jnp.where(at_row <= at_column, gap, masked_score))
                part = grad_kernels[:, side * rows : (side + 1) * rows] * decay
                grad_mixing = grad_mixing + part
                moved = part * mixing
                sums_ref[head : head + 1, :] = jnp.sum(moved, axis=0, keepdims=True)
                column = jnp.sum(moved, axis=1, keepdims=True)
                column_sums = jnp.where(at_column == head, column, column_sums)
                kernels.append(bf(decay * mixing))
            grad_scaled = plain_dot(jnp.concatenate(kernels, axis=1), apart)
            grad_scaled = grad_scaled + back[:, span] * tail_wide[:, span]
            grad_act_ref[chunk, :, span] = (
                grad_scaled * step_wide[:, span] + skip_ref[:, span] * grad_y[:, span]
            )
            by_step = grad_scaled * inputs_x[:, span]
            lane = lax.broadcasted_iota(jnp.int32, by_step.shape, 1)
            for side in range(2):
                mine = jnp.where((lane < MHEAD_DIM) == (side == 0), by_step, 0.0)
                column = jnp.sum(mine, axis=1, keepdims=True)
                grad_step = jnp.where(at_column == 2 * pair + side, column, grad_step)
        grad_mixing_low = bf(grad_mixing)
        grad_act_ref[chunk, :, inner : inner + STATE] = grad_input + plain_dot(
            grad_mixing_low, output_low
        )
        grad_act_ref[chunk, :, inner + STATE :] = grad_output + plain_dot(
            bf(grad_mixing.T), input_low
        )
        grad_step_ref[chunk] = grad_step[:, :heads]
        row_sums = sums_ref[...].T[:, :heads]
        ahead = row_sums - column_sums[:, :heads] + from_row
        from_here = jnp.where(at_row <= at_column, 1.0, 0.0)
        before = jnp.where(at_row > at_column, 1.0, 0.0)
        grad_log_ref[chunk] = (
            jnp.dot(from_here, ahead, precision=highest_precision)
            + jnp.dot(before, from_column, precision=highest_precision)
            + from_last
        )
        grad_skip_ref[...] += jnp.sum(inputs_x * grad_y, axis=0, keepdims=True)
        return carried

    lax.fori_loop(0, chunks, one_chunk, 0)


def ssd_back(act, cum, step_size, grad_y, carry_state, grad_end, skip_row):
    shape = act.shape
    act, cum, step_size, grad_y = (by_chunks(a) for a in (act, cum, step_size, grad_y))
    chunks, rows, width = act.shape
    inner = MHEADS * MHEAD_DIM
    grad_act, grad_step, grad_log, grad_skip = pl.pallas_call(
        ssd_back_kernel,
        out_shape=(
            jax.ShapeDtypeStruct(act.shape, jnp.float32),
            jax.ShapeDtypeStruct(cum.shape, jnp.float32),
            jax.ShapeDtypeStruct(cum.shape, jnp.float32),
            jax.ShapeDtypeStruct((1, inner), jnp.float32),
        ),
        in_specs=in_vmem(9),
        out_specs=tuple(in_vmem(4)),
        scratch_shapes=[
            pltpu.VMEM((chunks, STATE, inner), jnp.float32),
            pltpu.VMEM((STATE, inner), jnp.float32),
            pltpu.VMEM((rows, rows), jnp.float32),
        ],
        compiler_params=compiler_room,
        cost_estimate=pl.CostEstimate(
            flops=chunks * rows * inner * 25000, bytes_accessed=act.size * 16, transcendentals=0
        ),
        name="ssd_back",
    )(
        act,
        cum,
        jnp.swapaxes(cum, 1, 2),
        step_size,
        grad_y,
        carry_state,
        grad_end,
        skip_row,
        head_columns(MHEADS, 3),
    )
    flat = (shape[0], MHEADS)
    return grad_act.reshape(shape), grad_step.reshape(flat), grad_log.reshape(flat), grad_skip


def shifted(block, axis, distance):
    count = lax.axis_size(axis)
    return lax.ppermute(block, axis, [(i, (i + distance) % count) for i in range(count)])


def moved_along(block, axis, distance):
    count = lax.axis_size(axis)
    route = [(i, i + distance) for i in range(count) if 0 <= i + distance < count]
    return lax.ppermute(block, axis, route)


def own_half_first(values):
    cuts = 2 * lax.axis_size("y")
    width = values.shape[1] // cuts
    blocks = [values[:, i * width : (i + 1) * width] for i in range(cuts)]
    first = lax.axis_index("core") == 0
    own = [jnp.where(first, a, b) for a, b in zip(blocks[0::2], blocks[1::2])]
    other = [jnp.where(first, b, a) for a, b in zip(blocks[0::2], blocks[1::2])]
    return jnp.concatenate(own + other, axis=1)


def usual_order(values):
    cuts = 2 * lax.axis_size("y")
    width = values.shape[1] // cuts
    blocks = [values[:, i * width : (i + 1) * width] for i in range(cuts)]
    first = lax.axis_index("core") == 0
    merged = []
    for own, other in zip(blocks[: cuts // 2], blocks[cuts // 2 :]):
        merged += [jnp.where(first, own, other), jnp.where(first, other, own)]
    return jnp.concatenate(merged, axis=1)


def width_order(width, first):
    sizes = {axis: lax.axis_size(axis) for axis in every_axis}
    rows = width // math.prod(sizes.values())
    rest = lax.broadcasted_iota(jnp.int32, (width, width), 1)
    inside, rest = rest % rows, rest // rows
    owner = {}
    for axis in ("z", "xy".replace(first, ""), first):
        owner[axis] = (rest % sizes[axis] + lax.axis_index(axis)) % sizes[axis]
        rest = rest // sizes[axis]
    usual = rest
    for axis in ("y", "z", "x"):
        usual = usual * sizes[axis] + owner[axis]
    usual = usual * rows + inside
    return (lax.broadcasted_iota(jnp.int32, (width, width), 0) == usual).astype(jnp.bfloat16)


def after(values, *others):
    return lax.optimization_barrier((values, others))[0]


def gather_stages(shard, middle):
    parts = [shard] + [shifted(shard, "z", -k) for k in range(1, lax.axis_size("z"))]
    block = jnp.concatenate(parts, axis=0)
    halves = [block[:, :middle], block[:, middle:]]
    for axes in ("xy", "yx"):
        got = [
            [half] + [shifted(half, axis, -k) for k in range(1, lax.axis_size(axis))]
            for half, axis in zip(halves, axes)
        ]
        halves = [jnp.concatenate(parts, axis=0) for parts in lax.optimization_barrier(got)]
    return [(half, shifted(half, "core", 1)) for half in halves]


def times_rows(values, pair):
    half = values.shape[1] // 2
    return plain_dot(values[:, :half], pair[0]) + plain_dot(values[:, half:], pair[1])


def times_rows_back(values, pair):
    return jnp.concatenate([back_product(values, pair[0]), back_product(values, pair[1])], axis=1)


def keep_own(total, axis, received, hold=()):
    kept = total[0]
    for step in range(1, lax.axis_size(axis)):
        got = shifted(total[step].astype(jnp.bfloat16), axis, step)
        received.append(got)
        if hold:
            got = after(got, *hold)
        kept = kept + got.astype(jnp.float32)
    return kept


def core_sum(left, right, first, received):
    half = left.shape[1] // 2
    sizes = [lax.axis_size(axis) for axis in (first, "xy".replace(first, ""), "z")]
    got = shifted(outer_product(left[:, half:], right).astype(jnp.bfloat16), "core", 1)
    received.append(got)
    total = outer_product(left[:, :half], right) + got.astype(jnp.float32)
    return total.reshape(*sizes, -1, right.shape[1])


def side_by_side(parts):
    return parts[0] if len(parts) == 1 else jnp.concatenate(parts, axis=-1)


def first_sums(by_x, by_y, received):
    by_x = side_by_side([keep_own(total, "x", received) for total in by_x])
    by_y = side_by_side([keep_own(total, "y", received) for total in by_y])
    return by_x, by_y


def layer_sums(by_x, by_y, received, hold=()):
    by_x = keep_own(by_x, "y", received, hold)
    by_y = keep_own(by_y, "x", received, hold)
    return jnp.concatenate([by_x, by_y], axis=-1)


def send_layers(total):
    parts = [total[step].astype(jnp.bfloat16) for step in range(1, total.shape[0])]
    return [total[0]] + [shifted(part, "z", step + 1) for step, part in enumerate(parts)]


def sum_layers(parts):
    return sum(part.astype(jnp.float32) for part in parts)


def sum_everywhere(values, holds):
    for axis in ("core", "x", "y", "z"):
        if axis in holds:
            values = after(values, *holds[axis])
        count = lax.axis_size(axis)
        step = 1
        while step < count:
            values = values + lax.ppermute(values, axis, [(i, i ^ step) for i in range(count)])
            step *= 2
    return values


def send_states(state, tail, direction):
    depth, width = state.shape
    half = width // 2
    at_x = lax.axis_index("x")
    is_second = (at_x == 1) if direction == 1 else (at_x == 0)
    packed = jnp.concatenate([state, tail], axis=0).astype(jnp.bfloat16)
    other = shifted(packed, "x", 1)
    own = packed.astype(jnp.float32)
    first = jnp.where(is_second, other.astype(jnp.float32), own)
    second = jnp.where(is_second, own, other.astype(jnp.float32))
    pair = jnp.concatenate(
        [
            second[depth : depth + 1] * first[:depth] + second[:depth],
            first[depth:] * second[depth:],
        ],
        axis=0,
    )
    mine = jnp.where(at_x == 0, pair[:, :half], pair[:, half:]).astype(jnp.bfloat16)
    steps = range(1, lax.axis_size("z"))
    passed = [moved_along(mine, "z", direction * step) for step in steps]
    return jnp.where(is_second, first, 0.0), other, passed


def carried(behind, passed, direction):
    depth, half = behind.shape[0] - 8, behind.shape[1] // 2
    at_x = lax.axis_index("x")
    is_second = (at_x == 1) if direction == 1 else (at_x == 0)
    total = jnp.zeros((depth, half), jnp.float32)
    fade = jnp.ones((1, half), jnp.float32)
    for got in passed:
        total = total + fade * got[:depth].astype(jnp.float32)
        fade = fade * got[depth : depth + 1].astype(jnp.float32)
    total = total.astype(jnp.bfloat16)
    rest = shifted(total, "x", 1)
    left, right = jnp.where(at_x == 0, total, rest), jnp.where(at_x == 0, rest, total)
    carry = jnp.concatenate([left, right], axis=1).astype(jnp.float32)
    return jnp.where(is_second, behind[depth : depth + 1], 1.0) * carry + behind[:depth]


def keys_behind(own):
    return [moved_along(own, "z", step) if step else own for step in range(lax.axis_size("z"))]


def all_slots(blocks):
    blocks = jnp.stack(blocks)
    swapped = shifted(blocks, "x", 1)
    slots = jnp.stack([blocks, swapped], axis=1)
    return slots.reshape(-1, *blocks.shape[1:]), swapped


def sum_key_grads(kept, swapped, received):
    kept = kept + swapped.astype(jnp.float32)
    own = kept[0]
    for step in range(1, kept.shape[0]):
        got = moved_along(kept[step].astype(jnp.bfloat16), "z", -step)
        received.append(got)
        own = own + got.astype(jnp.float32)
    return own


def on_device(
    tokens,
    gain_one,
    w_in,
    w_step,
    conv_weight,
    conv_bias,
    mamba_heads,
    skip_weight,
    w_query,
    w_keyval,
    w_attn_out,
    w_mix_out,
    gain_two,
    w_gate_up,
    w_down,
    cotangent,
):
    width = tokens.shape[2]
    row_count = tokens.shape[1]
    inner_width = MHEADS * MHEAD_DIM
    device_count = math.prod(lax.axis_size(axis) for axis in every_axis)
    channels = conv_weight.shape[1] * device_count
    key_width = KVHEADS * HEAD_DIM
    query_width = QHEADS * HEAD_DIM
    own_rows = gain_one.shape[0]
    at_z, at_x = lax.axis_index("z"), lax.axis_index("x")
    place = jnp.stack([at_z, at_x]).astype(jnp.int32)

    taps = jnp.concatenate([conv_weight, conv_bias[None]], axis=0)
    tap_columns = -(-taps.size // own_rows)
    tap_shard = jnp.pad(taps.reshape(-1), (0, tap_columns * own_rows - taps.size))
    query_at = channels + w_keyval.shape[1]
    step_at = query_at + query_width
    gain_at = step_at + w_step.shape[1]
    tap_at = gain_at + 2
    conv_shard = jnp.concatenate(
        [
            w_in[:, inner_width:],
            w_keyval,
            w_query,
            w_step,
            gain_one[:, None],
            gain_two[:, None],
            tap_shard.reshape(tap_columns, own_rows).T,
            jnp.zeros((own_rows, -(tap_at + tap_columns) % 128), jnp.bfloat16),
        ],
        axis=1,
    )
    conv_shard = after(conv_shard)
    late_shards = [w_in[:, :inner_width], w_mix_out.T, w_attn_out.T, w_gate_up, after(w_down.T, conv_shard)]
    late = lax.all_gather(jnp.concatenate(late_shards, axis=1), ("y", "z", "x"), axis=0, tiled=True)
    middle = conv_shard.shape[1] // 256 * 128
    pair_a, pair_b = gather_stages(conv_shard, middle)
    out_at = inner_width
    ff_at = out_at + inner_width + query_width
    order_x, order_y = lax.optimization_barrier((width_order(width, "x"), width_order(width, "y")))
    inputs = own_half_first(tokens[0]).astype(jnp.float32)
    grad_output = own_half_first(cotangent[0])
    small = jnp.concatenate(
        [half[:, gain_at - middle : tap_at + tap_columns - middle] for half in pair_b], axis=0
    )
    small_rows = lax.dot_general(
        small, order_x, (((0,), (1,)), ((), ())), preferred_element_type=jnp.float32
    )
    gain_one_float, gain_two_float = small_rows[0], small_rows[1]
    tap_all = usual_order(small_rows[2:]).reshape(tap_columns, device_count, own_rows)
    tap_all = jnp.swapaxes(tap_all, 0, 1).reshape(device_count, -1)[:, : taps.size]
    tap_all = jnp.swapaxes(tap_all.reshape(-1, *taps.shape), 0, 1).reshape(taps.shape[0], channels)

    def reordered(rows, order):
        return plain_dot(rows, order).astype(jnp.bfloat16)

    normed = rms_norm(inputs, gain_one_float).astype(jnp.bfloat16)
    normed_x, normed_y = reordered(normed, order_x), reordered(normed, order_y)
    projected_a = times_rows(normed_y, pair_a)
    projected_b = times_rows(normed_x, pair_b)
    conv_input = jnp.concatenate(
        [
            projected_a.astype(jnp.bfloat16),
            projected_b[:, : channels - middle].astype(jnp.bfloat16),
        ],
        axis=1,
    )
    keyval_raw = projected_b[:, channels - middle : query_at - middle]
    query_raw = projected_b[:, query_at - middle : step_at - middle]
    step_raw = projected_b[:, step_at - middle : gain_at - middle]
    positions = (at_z * lax.axis_size("x") + at_x) * row_count + jnp.arange(
        row_count, dtype=jnp.int32
    )
    cosine, sine = turn_columns(positions)
    keyval_cols = keyval_raw.T
    key_cols = turn_rows(keyval_cols[:key_width], cosine, sine)
    by_head = (KVHEADS, 1, HEAD_DIM, row_count)
    own_keyval = jnp.concatenate(
        [key_cols.reshape(by_head), keyval_cols[key_width:].reshape(by_head)], axis=1
    ).reshape(2 * key_width, row_count)
    key_blocks = keys_behind(own_keyval.T.astype(jnp.bfloat16))
    query_cols = turn_rows(query_raw.T, cosine, sine).astype(jnp.bfloat16)
    border = lax.ppermute(
        conv_input[row_count - (CONV - 1) :],
        seq_axes,
        [(i, i + 1) for i in range(lax.axis_size(seq_axes) - 1)],
    )
    extended = jnp.concatenate([border, conv_input], axis=0).astype(jnp.float32)
    act, pull_conv = jax.vjp(conv_act, extended, tap_all[:CONV], tap_all[CONV])
    step_size = jax.nn.softplus(step_raw + mamba_heads[1][None, :])
    log_decay = -jnp.exp(mamba_heads[0])[None, :] * step_size
    by_chunk = by_chunks(log_decay)
    chunk_rows = by_chunk.shape[1]
    lower = jnp.tril(jnp.ones((chunk_rows, chunk_rows), jnp.float32))
    cum = jnp.stack([jnp.dot(lower, c, precision=highest_precision) for c in by_chunk])
    cum = cum.reshape(log_decay.shape)
    y_local, grown, fresh_state, tail, *key_blocks = after(
        (*ssd_local(act, cum, step_size), *key_blocks)
    )
    all_keyval, keys_swapped = all_slots(key_blocks)
    all_cols = jnp.swapaxes(all_keyval, 1, 2)
    y_local = y_local.reshape(row_count, inner_width)
    grown = grown.reshape(row_count, inner_width)
    behind, other_state, passed = send_states(fresh_state, tail, 1)
    late = after(late, keys_swapped)
    late = (late, shifted(late, "core", 1))
    cuts = (0, out_at, ff_at, ff_at + FF, ff_at + 2 * FF, late[0].shape[1])
    full_gate_z, full_out, full_gate, full_up, full_down = (
        tuple(half[:, low:high] for half in late) for low, high in zip(cuts[:-1], cuts[1:])
    )
    attended_cols, logs = attend(place, after(query_cols, other_state), all_keyval, all_cols)
    attended_cols, logs, *passed = after((attended_cols, logs, *passed))
    carry_state = carried(behind, passed, 1)
    gate_z = times_rows(normed, full_gate_z)
    attention_rows = attended_cols.T.astype(jnp.bfloat16)

    skip_row = jnp.repeat(skip_weight, MHEAD_DIM)[None, :]
    output_low = act[:, inner_width + STATE :].astype(jnp.bfloat16)
    ssm_y = (
        y_local
        + grown * plain_dot(output_low, carry_state.astype(jnp.bfloat16))
        + skip_row * act[:, :inner_width]
    )
    gate_sigmoid = jax.nn.sigmoid(gate_z)
    mixer = (ssm_y * gate_z * gate_sigmoid).astype(jnp.bfloat16)
    branches = jnp.concatenate([mixer, attention_rows], axis=1)
    hidden = inputs + times_rows_back(branches, full_out)
    normed_two = rms_norm(hidden, gain_two_float).astype(jnp.bfloat16)
    gate_part = times_rows(normed_two, full_gate)
    up_part = times_rows(normed_two, full_up)
    activated = (jax.nn.silu(gate_part) * up_part).astype(jnp.bfloat16)
    result = hidden + times_rows_back(activated, full_down)
    output = usual_order(result.astype(jnp.bfloat16))[None]

    grad_activated = times_rows(grad_output, full_down)
    core_got = []
    down_half = FF // 2
    ff_sigmoid = jax.nn.sigmoid(gate_part)
    grad_gate = grad_activated * up_part * ff_sigmoid * (1.0 + gate_part * (1.0 - ff_sigmoid))
    grad_gate = grad_gate.astype(jnp.bfloat16)
    grad_up = (grad_activated * gate_part * ff_sigmoid).astype(jnp.bfloat16)
    gate_total = core_sum(reordered(normed_two, order_x), grad_gate, "x", core_got)
    up_total = core_sum(reordered(normed_two, order_y), grad_up, "y", core_got)
    down_a = core_sum(reordered(grad_output, order_x), activated[:, :down_half], "x", [])
    down_b = core_sum(reordered(grad_output, order_y), activated[:, down_half:], "y", [])
    ff_got = []
    ff_later = []
    ff_parts = send_layers(
        layer_sums(*first_sums([gate_total, down_a], [up_total, down_b], ff_got), ff_later)
    )
    grad_normed_two = times_rows_back(after(grad_gate, *core_got), full_gate) + times_rows_back(
        grad_up, full_up
    )
    _, pull_two = jax.vjp(rms_norm, hidden, gain_two_float)
    grad_hidden_norm, grad_gain_two = pull_two(grad_normed_two)
    grad_hidden = grad_output.astype(jnp.float32) + grad_hidden_norm
    grad_branch = grad_hidden.astype(jnp.bfloat16)
    grad_branches = after(times_rows(grad_branch, full_out), ff_got[1], ff_got[3])
    grad_mixer = grad_branches[:, :inner_width]
    grad_y = grad_mixer * gate_z * gate_sigmoid
    grad_gate_z = grad_mixer * ssm_y * gate_sigmoid * (1.0 + gate_z * (1.0 - gate_sigmoid))
    from_output = outer_product(output_low, (grown * grad_y).astype(jnp.bfloat16))
    behind, _, passed = send_states(from_output, tail, -1)

    grad_attention = grad_branches[:, inner_width:].astype(jnp.bfloat16)
    out_got = []
    out_total = core_sum(reordered(grad_branch, order_y), branches, "y", out_got)
    grad_gate_low = grad_gate_z.astype(jnp.bfloat16)
    in_gate_total = core_sum(normed_x, grad_gate_low, "x", out_got)
    grad_normed_part = times_rows_back(grad_gate_low, full_gate_z)
    grad_cols = grad_attention.T
    query_rows = query_cols.T

    def one_group(group, place):
        return attend_back(
            group,
            place,
            query_cols,
            query_rows,
            grad_cols,
            grad_attention,
            attended_cols,
            logs,
            all_keyval,
            all_cols,
        )

    query_a, kept_a, other_a = one_group(0, after(place, gate_total, up_total))
    query_a, kept_a, other_a = after((query_a, kept_a, other_a), ff_got[0], ff_got[2])
    swapped_a = shifted(other_a, "x", 1)
    query_b, kept_b, other_b = one_group(1, after(place, ff_got[0], ff_got[2], *out_got))
    before_ssd = (query_b, *ff_later, swapped_a)
    query_b, kept_b, other_b, kept_a, swapped_a, *passed = after(
        (query_b, kept_b, other_b, kept_a, swapped_a, *passed), *before_ssd
    )
    grad_end = carried(behind, passed, -1)
    key_got = []
    own_a = sum_key_grads(kept_a, swapped_a, key_got)
    swapped_b = shifted(other_b, "x", 1)
    own_b = sum_key_grads(kept_b, swapped_b, key_got)
    own_grads = [own_a, own_b]
    grad_query_cols = jnp.concatenate([query_a, query_b], axis=0)
    mid_got = []
    mid_both = first_sums([in_gate_total], [out_total], mid_got)
    grad_query = turn_rows(grad_query_cols, cosine, -sine).T.astype(jnp.bfloat16)
    own_cols = jnp.concatenate(own_grads, axis=1).T.reshape(KVHEADS, 2, HEAD_DIM, row_count)
    grad_keys = turn_rows(own_cols[:, 0].reshape(key_width, row_count), cosine, -sine)
    grad_keyval = jnp.concatenate([grad_keys, own_cols[:, 1].reshape(key_width, row_count)], axis=0)
    grad_keyval = grad_keyval.T.astype(jnp.bfloat16)

    ssd_skip = after(
        skip_row, *before_ssd, swapped_b, *out_got, grad_normed_part
    )
    grad_act, grad_step_size, grad_log, grad_skip = ssd_back(
        act, cum, step_size, grad_y, carry_state, grad_end, ssd_skip
    )
    grad_act, grad_step_size, grad_log = after((grad_act, grad_step_size, grad_log), *key_got)
    grad_step_size = grad_step_size - grad_log * jnp.exp(mamba_heads[0])[None, :]
    grad_step_raw = grad_step_size * jax.nn.sigmoid(step_raw + mamba_heads[1][None, :])
    grad_heads = jnp.stack([jnp.sum(grad_log * log_decay, axis=0), jnp.sum(grad_step_raw, axis=0)])
    grad_extended, grad_conv_weight, grad_conv_bias = pull_conv(grad_act)
    grad_extended, *ff_parts = after((grad_extended, *ff_parts), *mid_got)
    ff_sums = sum_layers(ff_parts)
    rim_back = lax.ppermute(
        grad_extended[: CONV - 1],
        seq_axes,
        [(i + 1, i) for i in range(lax.axis_size(seq_axes) - 1)],
    )
    grad_conv_input = grad_extended[CONV - 1 :] + jnp.pad(
        rim_back, ((row_count - (CONV - 1), 0), (0, 0))
    )
    grad_step_low = jnp.pad(
        grad_step_raw.astype(jnp.bfloat16), ((0, 0), (0, conv_shard.shape[1] - gain_at))
    )
    grad_few = jnp.concatenate([grad_keyval, grad_query, grad_step_low], axis=1)
    few_core_got, last_core_got = [], []
    few_total = core_sum(normed_y, grad_few, "y", few_core_got)
    grad_conv_low = after(grad_conv_input.astype(jnp.bfloat16), *few_core_got)
    conv_total = core_sum(normed_x, grad_conv_low, "x", last_core_got)
    last_got, last_later = [], []
    mid_parts = send_layers(layer_sums(*mid_both, [], last_core_got))
    last_parts = send_layers(
        layer_sums(*first_sums([conv_total], [few_total], last_got), last_later)
    )
    last_parts, *mid_parts = after((tuple(last_parts), *mid_parts), *last_later)
    last_sums, mid_sums = sum_layers(last_parts), sum_layers(mid_parts)
    grad_normed = lax.dot_general(
        jnp.concatenate(
            [
                times_rows_back(grad_conv_low[:, :middle], pair_a),
                times_rows_back(
                    jnp.concatenate([grad_conv_low[:, middle:], grad_few], axis=1), pair_b
                ),
            ],
            axis=1,
        ),
        jnp.concatenate([order_y, order_x], axis=1).astype(jnp.float32),
        (((1,), (1,)), ((), ())),
        precision=lax.Precision.HIGH,
        preferred_element_type=jnp.float32,
    )
    _, pull_one = jax.vjp(rms_norm, inputs, gain_one_float)
    grad_input_norm, grad_gain_one = pull_one(grad_normed + grad_normed_part)
    input_grad = usual_order(grad_hidden + grad_input_norm)[None]
    gain_grads = usual_order(jnp.stack([grad_gain_two, grad_gain_one]))

    def padded(row):
        return jnp.pad(row, ((0, 0), (0, channels - row.shape[1])))

    head_row = jnp.concatenate(
        [grad_heads[:1], grad_heads[1:], jnp.sum(grad_skip.reshape(MHEADS, -1), axis=1)[None]],
        axis=1,
    )
    summed = sum_everywhere(
        after(
            jnp.concatenate(
                [
                    grad_conv_weight,
                    grad_conv_bias[None],
                    padded(gain_grads),
                    padded(head_row),
                ],
                axis=0,
            ),
            *last_core_got,
        ),
        {"y": last_got, "z": last_later},
    )
    device = lax.axis_index(every_axis)
    own_channels = conv_weight.shape[1]
    own_taps = lax.dynamic_slice_in_dim(summed[: CONV + 1], device * own_channels, own_channels, 1)
    own_gain_two = lax.dynamic_slice_in_dim(summed[CONV + 1], device * own_rows, own_rows)
    own_gain_one = lax.dynamic_slice_in_dim(summed[CONV + 2], device * own_rows, own_rows)
    head_sums_row = summed[CONV + 3]
    return (
        output,
        input_grad,
        own_gain_one,
        jnp.concatenate([mid_sums[:, :inner_width], last_sums[:, :channels]], axis=1),
        last_sums[:, step_at:gain_at],
        own_taps[:CONV],
        own_taps[CONV],
        head_sums_row[: 2 * MHEADS].reshape(2, MHEADS),
        head_sums_row[2 * MHEADS : 3 * MHEADS],
        last_sums[:, query_at:step_at],
        last_sums[:, channels:query_at],
        mid_sums[:, 2 * inner_width :].T,
        mid_sums[:, inner_width : 2 * inner_width].T,
        own_gain_two,
        jnp.concatenate([ff_sums[:, :FF], ff_sums[:, FF + down_half : 2 * FF + down_half]], axis=1),
        jnp.concatenate(
            [ff_sums[:, FF : FF + down_half], ff_sums[:, 2 * FF + down_half :]], axis=1
        ).T,
    )


def solution(mesh):
    dp, seq = mesh.shape["dp"], mesh.shape["seq"]
    by_axis = Mesh(mesh.devices.reshape(dp // 2, 2, seq // 2, 2), every_axis)
    pieces = P(("y", "core"), seq_axes, None)
    rows = P(every_axis, None)
    columns = P(None, every_axis)
    vector = P(every_axis)
    weights = (rows, rows, columns, columns, vector, rows, columns)
    return jax.shard_map(
        on_device,
        mesh=by_axis,
        in_specs=(pieces, vector, rows, rows, columns, vector, P(), P(), *weights, pieces),
        out_specs=(pieces, pieces, vector, rows, rows, columns, vector, P(), P(), *weights),
        check_vma=False,
    )
```

```python
import math
from functools import partial

import jax
import jax.experimental.pallas as pl
import jax.experimental.pallas.tpu as pltpu
import jax.numpy as jnp
from jax import lax
from jax.sharding import Mesh
from jax.sharding import PartitionSpec as P

MHEADS = 24
MHEAD_DIM = 64
STATE = 128
CONV = 4
QHEADS = 8
KVHEADS = 2
HEAD_DIM = 64
FF = 2048


norm_epsilon = 1e-06
rope_base = 100000000000.0
masked_score = -1e30
highest_precision = lax.Precision.HIGHEST
seq_axes = ("z", "x")
every_axis = ("y", "core", "z", "x")


def rms_norm(values, gain_vector):
    return (
        values
        * lax.rsqrt(jnp.mean(values * values, axis=-1, keepdims=True) + norm_epsilon)
        * gain_vector
    )


def outer_product(left, right):
    return lax.dot_general(
        left, right, (((0,), (0,)), ((), ())), preferred_element_type=jnp.float32
    )


def back_product(grad_rows, weight_matrix):
    return lax.dot_general(
        grad_rows, weight_matrix, (((1,), (1,)), ((), ())), preferred_element_type=jnp.float32
    )


def turn_columns(positions):
    half = HEAD_DIM // 2
    exponents = jnp.arange(half).astype(jnp.float32) * (2.0 / HEAD_DIM)
    frequency = rope_base ** (-exponents)
    angles = frequency[:, None] * positions.astype(jnp.float32)[None, :]
    return (jnp.cos(angles), jnp.sin(angles))


def turn_rows(values, cosine, sine):
    half = HEAD_DIM // 2
    heads = values.reshape(-1, 2, half, values.shape[1])
    first, second = heads[:, 0], heads[:, 1]
    turned = [first * cosine - second * sine, second * cosine + first * sine]
    return jnp.stack(turned, axis=1).reshape(values.shape)


def conv_act(extended, conv_weight, conv_bias):
    row_count = extended.shape[0] - (CONV - 1)
    conv_sum = conv_bias[None, :] + conv_weight[0][None, :] * extended[0:row_count]
    for offset in range(1, CONV):
        conv_sum = conv_sum + conv_weight[offset][None, :] * extended[offset : offset + row_count]
    return jax.nn.silu(conv_sum)


log2_e = math.log2(math.e)
group_size = QHEADS // KVHEADS
score_scale = 1.0 / math.sqrt(HEAD_DIM)
compiler_room = pltpu.CompilerParams(vmem_limit_bytes=48 * 1024 * 1024)


def plain_dot(left, right):
    return jnp.dot(left, right, preferred_element_type=jnp.float32)


def head_span(head):
    return slice(head * HEAD_DIM, (head + 1) * HEAD_DIM)


def hidden_keys(rows):
    key_at = lax.broadcasted_iota(jnp.int32, (rows, rows), 0)
    query_at = lax.broadcasted_iota(jnp.int32, (rows, rows), 1)
    return key_at > query_at


def slot_of(index, place_ref):
    z, x = lax.shift_right_logical(index, 1), lax.bitwise_and(index, 1)
    return 2 * (place_ref[0] - z) + lax.bitwise_xor(x, place_ref[1])


def attend_kernel(place_ref, query_ref, keyval_ref, keyval_cols_ref, out_ref, log_ref, best_ref, sum_ref):
    rows = query_ref.shape[1]
    scale = log2_e * score_scale

    def scores_of(piece, head):
        group = head // group_size
        keys = keyval_ref[piece, :, 2 * group * HEAD_DIM : 2 * (group + 1) * HEAD_DIM]
        query = query_ref[head_span(head), :]
        return plain_dot(keys, jnp.concatenate([query, jnp.zeros_like(query)], axis=0)) * scale

    def values_of(piece, head):
        return keyval_cols_ref[piece, head_span(2 * (head // group_size) + 1), :]

    for head in range(QHEADS):
        scores = jnp.where(hidden_keys(rows), masked_score, scores_of(0, head))
        best = jnp.max(scores, axis=0, keepdims=True)
        weights = jnp.exp2(scores - best)
        best_ref[head : head + 1, :] = best
        sum_ref[head : head + 1, :] = jnp.sum(weights, axis=0, keepdims=True)
        out_ref[head_span(head), :] = plain_dot(values_of(0, head), weights.astype(jnp.bfloat16))

    def piece_step(index, carry):
        piece = slot_of(index, place_ref)
        for head in range(QHEADS):
            scores = scores_of(piece, head)
            old = best_ref[head : head + 1, :]
            best = jnp.maximum(old, jnp.max(scores, axis=0, keepdims=True))
            fade = jnp.exp2(old - best)
            weights = jnp.exp2(scores - best)
            best_ref[head : head + 1, :] = best
            sum_ref[head : head + 1, :] = sum_ref[head : head + 1, :] * fade + jnp.sum(
                weights, axis=0, keepdims=True
            )
            out_ref[head_span(head), :] = out_ref[head_span(head), :] * fade + plain_dot(
                values_of(piece, head), weights.astype(jnp.bfloat16)
            )
        return carry

    lax.fori_loop(0, 2 * place_ref[0] + place_ref[1], piece_step, 0)
    total = sum_ref[...]
    log_ref[...] = best_ref[...] + jnp.log2(total)
    for head in range(QHEADS):
        out_ref[head_span(head), :] = out_ref[head_span(head), :] / total[head : head + 1, :]


def in_vmem(count):
    return [pl.BlockSpec(memory_space=pltpu.VMEM)] * count


def attend(place, queries, keyvals, keyval_cols):
    rows = queries.shape[1]
    flops = 4 * queries.size * rows * keyvals.shape[0]
    return pl.pallas_call(
        attend_kernel,
        out_shape=(
            jax.ShapeDtypeStruct(queries.shape, jnp.float32),
            jax.ShapeDtypeStruct((QHEADS, rows), jnp.float32),
        ),
        in_specs=[pl.BlockSpec(memory_space=pltpu.SMEM)] + in_vmem(3),
        out_specs=tuple(in_vmem(2)),
        scratch_shapes=[pltpu.VMEM((QHEADS, rows), jnp.float32)] * 2,
        compiler_params=compiler_room,
        cost_estimate=pl.CostEstimate(
            flops=8 * flops, bytes_accessed=4 * keyvals.size, transcendentals=flops // 256
        ),
        name="attend",
    )(place, queries, keyvals, keyval_cols)


def attend_back_kernel(
    place_ref,
    query_ref,
    query_rows_ref,
    grad_ref,
    grad_rows_ref,
    out_ref,
    log_ref,
    keyval_ref,
    keyval_cols_ref,
    grad_query_ref,
    grad_own_ref,
    grad_other_ref,
    dots_ref,
    query_side_ref,
    grad_side_ref,
):
    rows = query_ref.shape[1]
    scale = log2_e * score_scale
    grad_query_ref[...] = jnp.zeros_like(grad_query_ref)
    for head in range(QHEADS):
        span = head_span(head)
        dots_ref[head : head + 1, :] = jnp.sum(
            grad_ref[span, :].astype(jnp.float32) * out_ref[span, :], axis=0, keepdims=True
        )
        query = (query_rows_ref[:, span].astype(jnp.float32) * score_scale).astype(jnp.bfloat16)
        grad = grad_rows_ref[:, span]
        query_side_ref[head] = jnp.concatenate([query, jnp.zeros_like(query)], axis=1)
        grad_side_ref[head] = jnp.concatenate([jnp.zeros_like(grad), grad], axis=1)

    def one_piece(piece, own):
        for group in range(KVHEADS):
            both = slice(2 * group * HEAD_DIM, 2 * (group + 1) * HEAD_DIM)
            keyvals = keyval_ref[piece, :, both]
            key_cols = keyval_cols_ref[piece, head_span(2 * group), :]
            total = jnp.zeros((rows, 2 * HEAD_DIM), jnp.float32)
            for head in range(group * group_size, (group + 1) * group_size):
                query, grad = query_ref[head_span(head), :], grad_ref[head_span(head), :]
                blank = jnp.zeros_like(query)
                scores = plain_dot(keyvals, jnp.concatenate([query, blank], axis=0)) * scale
                weights = jnp.exp2(scores - log_ref[head : head + 1, :])
                if own:
                    weights = jnp.where(hidden_keys(rows), 0.0, weights)
                grad_weights = plain_dot(keyvals, jnp.concatenate([blank, grad], axis=0))
                grad_scores = weights * (grad_weights - dots_ref[head : head + 1, :])
                grad_scores = grad_scores.astype(jnp.bfloat16)
                grad_query_ref[head_span(head), :] += plain_dot(key_cols, grad_scores)
                total = total + plain_dot(grad_scores, query_side_ref[head])
                total = total + plain_dot(weights.astype(jnp.bfloat16), grad_side_ref[head])
            if own:
                grad_own_ref[0, :, both] = total
            else:
                put_piece(piece, both, total)

    def put_piece(piece, both, total):
        behind = lax.shift_right_logical(piece, 1)

        @pl.when(lax.bitwise_and(piece, 1) == 0)
        def _():
            grad_own_ref[behind, :, both] = total

        @pl.when(lax.bitwise_and(piece, 1) == 1)
        def _():
            grad_other_ref[behind, :, both] = total.astype(jnp.bfloat16)

    def clear(step, carry):
        grad_own_ref[step] = jnp.zeros(grad_own_ref.shape[1:], jnp.float32)
        grad_other_ref[step] = jnp.zeros(grad_other_ref.shape[1:], jnp.bfloat16)
        return carry

    def earlier(index, carry):
        one_piece(slot_of(index, place_ref), False)
        return carry

    lax.fori_loop(0, grad_own_ref.shape[0], clear, 0)
    one_piece(0, True)
    lax.fori_loop(0, 2 * place_ref[0] + place_ref[1], earlier, 0)
    grad_query_ref[...] = grad_query_ref[...] * score_scale


def attend_back(place, queries, query_rows, grads, grad_rows, outs, logs, keyvals, keyval_cols):
    slots, rows, width = keyvals.shape
    flops = 10 * queries.size * rows * slots
    return pl.pallas_call(
        attend_back_kernel,
        out_shape=(
            jax.ShapeDtypeStruct(queries.shape, jnp.float32),
            jax.ShapeDtypeStruct((slots // 2, rows, width), jnp.float32),
            jax.ShapeDtypeStruct((slots // 2, rows, width), jnp.bfloat16),
        ),
        in_specs=[pl.BlockSpec(memory_space=pltpu.SMEM)] + in_vmem(8),
        out_specs=tuple(in_vmem(3)),
        scratch_shapes=[
            pltpu.VMEM((QHEADS, rows), jnp.float32),
            pltpu.VMEM((QHEADS, rows, 2 * HEAD_DIM), jnp.bfloat16),
            pltpu.VMEM((QHEADS, rows, 2 * HEAD_DIM), jnp.bfloat16),
        ],
        compiler_params=compiler_room,
        cost_estimate=pl.CostEstimate(
            flops=6 * flops, bytes_accessed=4 * keyvals.size, transcendentals=flops // 640
        ),
        name="attend_back",
    )(place, queries, query_rows, grads, grad_rows, outs, logs, keyvals, keyval_cols)


ssd_rows = 128


def two_parts(values):
    high = values.astype(jnp.bfloat16)
    rest = values - high.astype(jnp.float32)
    middle = rest.astype(jnp.bfloat16)
    low = (rest - middle.astype(jnp.float32)).astype(jnp.bfloat16)
    return jnp.concatenate([high, middle, low], axis=1)


def head_columns(heads, parts):
    shape = (heads * parts, heads * MHEAD_DIM)
    head = lax.broadcasted_iota(jnp.int32, shape, 0) % heads
    channel = lax.broadcasted_iota(jnp.int32, shape, 1) // MHEAD_DIM
    return jnp.where(head == channel, 1.0, 0.0).astype(jnp.bfloat16)


def widen(values, spread):
    return plain_dot(two_parts(values), spread)


def head_sums(values, spread):
    heads = spread.shape[0]
    high = values.astype(jnp.bfloat16)
    low = (values - high.astype(jnp.float32)).astype(jnp.bfloat16)
    total = nt_dot(high, spread) + nt_dot(low, spread)
    return total


def nt_dot(left, right):
    return lax.dot_general(
        left, right, (((1,), (1,)), ((), ())), preferred_element_type=jnp.float32
    )


def split_pair(pair, axis):
    lane = lax.broadcasted_iota(jnp.int32, pair.shape, 1)
    blank = jnp.zeros_like(pair)
    return jnp.concatenate(
        [jnp.where(lane < MHEAD_DIM, pair, blank), jnp.where(lane < MHEAD_DIM, blank, pair)],
        axis=axis,
    )


def bf(values):
    return values.astype(jnp.bfloat16)


def ssd_kernel(act_ref, cum_ref, cum_rows_ref, step_ref, spread_ref, y_ref, grown_ref, state_ref, tail_ref):
    chunks, rows, inner = y_ref.shape
    spread = spread_ref[...]
    state_ref[...] = jnp.zeros_like(state_ref)
    tail_ref[...] = jnp.zeros_like(tail_ref)
    late = lax.broadcasted_iota(jnp.int32, (rows, rows), 0) >= lax.broadcasted_iota(
        jnp.int32, (rows, rows), 1
    )

    def one_chunk(chunk, before):
        act = act_ref[chunk]
        cum = cum_ref[chunk]
        cum_rows = cum_rows_ref[chunk]
        scaled = act[:, :inner] * widen(step_ref[chunk], spread)
        input_mat = act[:, inner : inner + STATE]
        output_low = bf(act[:, inner + STATE :])
        last = cum[rows - 1 : rows, :]
        grown_ref[chunk] = widen(jnp.exp(cum + before), spread)
        mixing = nt_dot(output_low, bf(input_mat))
        state = state_ref[...]
        from_state = plain_dot(output_low, bf(state)) * widen(jnp.exp(cum), spread)
        scaled_low = bf(scaled)
        for pair in range(MHEADS // 2):
            kernels = []
            for head in (2 * pair, 2 * pair + 1):
                gap = cum[:, head : head + 1] - cum_rows[head : head + 1, :]
                kernels.append(bf(jnp.exp(jnp.where(late, gap, masked_score)) * mixing))
            span = slice(2 * pair * MHEAD_DIM, (2 * pair + 2) * MHEAD_DIM)
            y_ref[chunk, :, span] = from_state[:, span] + plain_dot(
                jnp.concatenate(kernels, axis=1), split_pair(scaled_low[:, span], 0)
            )
        weighted = scaled * widen(jnp.exp(last - cum), spread)
        fade = widen(jnp.exp(jnp.broadcast_to(last, (8, last.shape[1]))), spread)[:1]
        state_ref[...] = state * fade + plain_dot(bf(input_mat.T), bf(weighted))
        return before + last

    total = lax.fori_loop(0, chunks, one_chunk, jnp.zeros((1, cum_ref.shape[2]), jnp.float32))
    tail_ref[...] = widen(jnp.exp(jnp.broadcast_to(total, (8, total.shape[1]))), spread)


def by_chunks(values):
    return values.reshape(-1, math.gcd(values.shape[0], ssd_rows), values.shape[1])


def ssd_local(act, cum, step_size):
    act, cum, step_size = by_chunks(act), by_chunks(cum), by_chunks(step_size)
    chunks, rows, _ = act.shape
    inner = MHEADS * MHEAD_DIM
    return pl.pallas_call(
        ssd_kernel,
        out_shape=(
            jax.ShapeDtypeStruct((chunks, rows, inner), jnp.float32),
            jax.ShapeDtypeStruct((chunks, rows, inner), jnp.float32),
            jax.ShapeDtypeStruct((STATE, inner), jnp.float32),
            jax.ShapeDtypeStruct((8, inner), jnp.float32),
        ),
        in_specs=in_vmem(5),
        out_specs=tuple(in_vmem(4)),
        compiler_params=compiler_room,
        cost_estimate=pl.CostEstimate(
            flops=chunks * rows * inner * 10000, bytes_accessed=act.size * 16, transcendentals=0
        ),
        name="ssd",
    )(act, cum, jnp.swapaxes(cum, 1, 2), step_size, head_columns(MHEADS, 3))


def ssd_back_kernel(
    act_ref,
    cum_ref,
    cum_rows_ref,
    step_ref,
    grad_ref,
    carry_ref,
    grad_end_ref,
    skip_ref,
    spread_ref,
    grad_act_ref,
    grad_step_ref,
    grad_log_ref,
    grad_skip_ref,
    states_ref,
    grad_state_ref,
    sums_ref,
):
    chunks, rows, _ = act_ref.shape
    inner = grad_ref.shape[2]
    heads = cum_ref.shape[2]
    spread = spread_ref[...]
    one_spread = spread[:heads]
    at_row = lax.broadcasted_iota(jnp.int32, (rows, rows), 0)
    at_column = lax.broadcasted_iota(jnp.int32, (rows, rows), 1)

    def fade_of(last):
        return widen(jnp.exp(jnp.broadcast_to(last, (8, heads))), spread)[:1]

    states_ref[0] = carry_ref[...]
    for chunk in range(chunks - 1):
        cum = cum_ref[chunk]
        last = cum[rows - 1 : rows, :]
        act = act_ref[chunk]
        weighted = act[:, :inner] * widen(jnp.exp(last - cum) * step_ref[chunk], spread)
        states_ref[chunk + 1] = states_ref[chunk] * fade_of(last) + plain_dot(
            bf(act[:, inner : inner + STATE].T), bf(weighted)
        )
    grad_state_ref[...] = grad_end_ref[...]
    grad_skip_ref[...] = jnp.zeros_like(grad_skip_ref)
    sums_ref[...] = jnp.zeros_like(sums_ref)

    def one_chunk(turn, carried):
        chunk = chunks - 1 - turn
        act = act_ref[chunk]
        cum = cum_ref[chunk]
        cum_rows = cum_rows_ref[chunk]
        step = step_ref[chunk]
        grad_y = grad_ref[chunk]
        last = cum[rows - 1 : rows, :]
        inputs_x = act[:, :inner]
        step_wide = widen(step, spread)
        tail = jnp.exp(last - cum)
        tail_wide = widen(tail, spread)
        scaled = inputs_x * step_wide
        scaled_low = bf(scaled)
        grad_low = bf(grad_y)
        input_low = bf(act[:, inner : inner + STATE])
        output_mat = act[:, inner + STATE :]
        output_low = bf(output_mat)
        state = states_ref[chunk]
        state_low = bf(state)
        grad_state = grad_state_ref[...]
        grad_state_low = bf(grad_state)

        grown_grad = grad_y * widen(jnp.exp(cum), spread)
        grown_low = bf(grown_grad)
        from_row = head_sums(grown_grad * plain_dot(output_low, state_low), one_spread)
        grad_output = nt_dot(grown_low, state_low)
        back = plain_dot(input_low, grad_state_low)
        from_column = head_sums(scaled * back, one_spread) * tail
        grad_input = nt_dot(bf(scaled * tail_wide), grad_state_low)
        fade = fade_of(last)
        both = jnp.sum(grad_state * state, axis=0, keepdims=True) * fade
        from_last = head_sums(jnp.broadcast_to(both, (8, inner)), one_spread)[:1]
        grad_state_ref[...] = grad_state * fade + plain_dot(bf(output_mat.T), grown_low)

        mixing = nt_dot(input_low, output_low)
        grad_mixing = jnp.zeros((rows, rows), jnp.float32)
        column_sums = jnp.zeros((rows, rows), jnp.float32)
        grad_step = jnp.zeros((rows, rows), jnp.float32)
        for pair in range(heads // 2):
            span = slice(2 * pair * MHEAD_DIM, (2 * pair + 2) * MHEAD_DIM)
            apart = split_pair(grad_low[:, span], 0)
            grad_kernels = nt_dot(scaled_low[:, span], apart)
            kernels = []
            for side in range(2):
                head = 2 * pair + side
                gap = cum_rows[head : head + 1, :] - cum[:, head : head + 1]
                decay = jnp.exp(jnp.where(at_row <= at_column, gap, masked_score))
                part = grad_kernels[:, side * rows : (side + 1) * rows] * decay
                grad_mixing = grad_mixing + part
                moved = part * mixing
                sums_ref[head : head + 1, :] = jnp.sum(moved, axis=0, keepdims=True)
                column = jnp.sum(moved, axis=1, keepdims=True)
                column_sums = jnp.where(at_column == head, column, column_sums)
                kernels.append(bf(decay * mixing))
            grad_scaled = plain_dot(jnp.concatenate(kernels, axis=1), apart)
            grad_scaled = grad_scaled + back[:, span] * tail_wide[:, span]
            grad_act_ref[chunk, :, span] = (
                grad_scaled * step_wide[:, span] + skip_ref[:, span] * grad_y[:, span]
            )
            by_step = grad_scaled * inputs_x[:, span]
            lane = lax.broadcasted_iota(jnp.int32, by_step.shape, 1)
            for side in range(2):
                mine = jnp.where((lane < MHEAD_DIM) == (side == 0), by_step, 0.0)
                column = jnp.sum(mine, axis=1, keepdims=True)
                grad_step = jnp.where(at_column == 2 * pair + side, column, grad_step)
        grad_mixing_low = bf(grad_mixing)
        grad_act_ref[chunk, :, inner : inner + STATE] = grad_input + plain_dot(
            grad_mixing_low, output_low
        )
        grad_act_ref[chunk, :, inner + STATE :] = grad_output + plain_dot(
            bf(grad_mixing.T), input_low
        )
        grad_step_ref[chunk] = grad_step[:, :heads]
        row_sums = sums_ref[...].T[:, :heads]
        ahead = row_sums - column_sums[:, :heads] + from_row
        from_here = jnp.where(at_row <= at_column, 1.0, 0.0)
        before = jnp.where(at_row > at_column, 1.0, 0.0)
        grad_log_ref[chunk] = (
            jnp.dot(from_here, ahead, precision=highest_precision)
            + jnp.dot(before, from_column, precision=highest_precision)
            + from_last
        )
        grad_skip_ref[...] += jnp.sum(inputs_x * grad_y, axis=0, keepdims=True)
        return carried

    lax.fori_loop(0, chunks, one_chunk, 0)


def ssd_back(act, cum, step_size, grad_y, carry_state, grad_end, skip_row):
    shape = act.shape
    act, cum, step_size, grad_y = (by_chunks(a) for a in (act, cum, step_size, grad_y))
    chunks, rows, width = act.shape
    inner = MHEADS * MHEAD_DIM
    grad_act, grad_step, grad_log, grad_skip = pl.pallas_call(
        ssd_back_kernel,
        out_shape=(
            jax.ShapeDtypeStruct(act.shape, jnp.float32),
            jax.ShapeDtypeStruct(cum.shape, jnp.float32),
            jax.ShapeDtypeStruct(cum.shape, jnp.float32),
            jax.ShapeDtypeStruct((1, inner), jnp.float32),
        ),
        in_specs=in_vmem(9),
        out_specs=tuple(in_vmem(4)),
        scratch_shapes=[
            pltpu.VMEM((chunks, STATE, inner), jnp.float32),
            pltpu.VMEM((STATE, inner), jnp.float32),
            pltpu.VMEM((rows, rows), jnp.float32),
        ],
        compiler_params=compiler_room,
        cost_estimate=pl.CostEstimate(
            flops=chunks * rows * inner * 25000, bytes_accessed=act.size * 16, transcendentals=0
        ),
        name="ssd_back",
    )(
        act,
        cum,
        jnp.swapaxes(cum, 1, 2),
        step_size,
        grad_y,
        carry_state,
        grad_end,
        skip_row,
        head_columns(MHEADS, 3),
    )
    flat = (shape[0], MHEADS)
    return grad_act.reshape(shape), grad_step.reshape(flat), grad_log.reshape(flat), grad_skip


def shifted(block, axis, distance):
    count = lax.axis_size(axis)
    return lax.ppermute(block, axis, [(i, (i + distance) % count) for i in range(count)])


def moved_along(block, axis, distance):
    count = lax.axis_size(axis)
    route = [(i, i + distance) for i in range(count) if 0 <= i + distance < count]
    return lax.ppermute(block, axis, route)


def width_order(width, first):
    sizes = {axis: lax.axis_size(axis) for axis in every_axis}
    rows = width // math.prod(sizes.values())
    rest = lax.broadcasted_iota(jnp.int32, (width, width), 1)
    inside, rest = rest % rows, rest // rows
    owner = {}
    for axis in ("z", "xy".replace(first, ""), first, "core"):
        owner[axis] = (rest % sizes[axis] + lax.axis_index(axis)) % sizes[axis]
        rest = rest // sizes[axis]
    usual = owner["y"]
    for axis in ("core", "z", "x"):
        usual = usual * sizes[axis] + owner[axis]
    usual = usual * rows + inside
    return (lax.broadcasted_iota(jnp.int32, (width, width), 0) == usual).astype(jnp.bfloat16)


def after(values, *others):
    return lax.optimization_barrier((values, others))[0]


def gather_stages(shard, middle):
    parts = [shard] + [shifted(shard, "z", -k) for k in range(1, lax.axis_size("z"))]
    block = jnp.concatenate(parts, axis=0)
    halves = [block[:, :middle], block[:, middle:]]
    arrived = []
    for axes in ("xy", "yx"):
        got = [
            [half] + [shifted(half, axis, -k) for k in range(1, lax.axis_size(axis))]
            for half, axis in zip(halves, axes)
        ]
        arrived += [parts[1] for parts in got]
        halves = [jnp.concatenate(parts, axis=0) for parts in lax.optimization_barrier(got)]
    return [(half, shifted(half, "core", 1)) for half in halves], arrived[:2]


def times_rows(values, pair):
    half = values.shape[1] // 2
    return plain_dot(values[:, :half], pair[0]) + plain_dot(values[:, half:], pair[1])


def times_rows_back(values, pair):
    return jnp.concatenate([back_product(values, pair[0]), back_product(values, pair[1])], axis=1)


def keep_own(total, axis, received, hold=()):
    kept = total[0]
    for step in range(1, lax.axis_size(axis)):
        got = shifted(total[step].astype(jnp.bfloat16), axis, step)
        received.append(got)
        if hold:
            got = after(got, *hold)
        kept = kept + got.astype(jnp.float32)
    return kept


def core_sum(left, right, first, received):
    half = left.shape[1] // 2
    sizes = [lax.axis_size(axis) for axis in (first, "xy".replace(first, ""), "z")]
    got = shifted(outer_product(left[:, half:], right).astype(jnp.bfloat16), "core", 1)
    received.append(got)
    total = outer_product(left[:, :half], right) + got.astype(jnp.float32)
    return total.reshape(*sizes, -1, right.shape[1])


def side_by_side(parts):
    return parts[0] if len(parts) == 1 else jnp.concatenate(parts, axis=-1)


def first_sums(by_x, by_y, received):
    by_x = side_by_side([keep_own(total, "x", received) for total in by_x])
    by_y = side_by_side([keep_own(total, "y", received) for total in by_y])
    return by_x, by_y


def layer_sums(by_x, by_y, received, hold=()):
    by_x = keep_own(by_x, "y", received, hold)
    by_y = keep_own(by_y, "x", received, hold)
    return jnp.concatenate([by_x, by_y], axis=-1)


def send_layers(total):
    parts = [total[step].astype(jnp.bfloat16) for step in range(1, total.shape[0])]
    return [total[0]] + [shifted(part, "z", step + 1) for step, part in enumerate(parts)]


def sum_layers(parts):
    return sum(part.astype(jnp.float32) for part in parts)


def sum_everywhere(values, holds):
    for axis in ("core", "x", "y", "z"):
        if axis in holds:
            values = after(values, *holds[axis])
        count = lax.axis_size(axis)
        step = 1
        while step < count:
            values = values + lax.ppermute(values, axis, [(i, i ^ step) for i in range(count)])
            step *= 2
    return values


def send_states(state, tail, direction):
    depth, width = state.shape
    half = width // 2
    at_x = lax.axis_index("x")
    is_second = (at_x == 1) if direction == 1 else (at_x == 0)
    packed = jnp.concatenate([state, tail], axis=0).astype(jnp.bfloat16)
    other = shifted(packed, "x", 1)
    own = packed.astype(jnp.float32)
    first = jnp.where(is_second, other.astype(jnp.float32), own)
    second = jnp.where(is_second, own, other.astype(jnp.float32))
    pair = jnp.concatenate(
        [
            second[depth : depth + 1] * first[:depth] + second[:depth],
            first[depth:] * second[depth:],
        ],
        axis=0,
    )
    mine = jnp.where(at_x == 0, pair[:, :half], pair[:, half:]).astype(jnp.bfloat16)
    steps = range(1, lax.axis_size("z"))
    passed = [moved_along(mine, "z", direction * step) for step in steps]
    return jnp.where(is_second, first, 0.0), other, passed


def carried(behind, passed, direction):
    depth, half = behind.shape[0] - 8, behind.shape[1] // 2
    at_x = lax.axis_index("x")
    is_second = (at_x == 1) if direction == 1 else (at_x == 0)
    total = jnp.zeros((depth, half), jnp.float32)
    fade = jnp.ones((1, half), jnp.float32)
    for got in passed:
        total = total + fade * got[:depth].astype(jnp.float32)
        fade = fade * got[depth : depth + 1].astype(jnp.float32)
    total = total.astype(jnp.bfloat16)
    rest = shifted(total, "x", 1)
    left, right = jnp.where(at_x == 0, total, rest), jnp.where(at_x == 0, rest, total)
    carry = jnp.concatenate([left, right], axis=1).astype(jnp.float32)
    return jnp.where(is_second, behind[depth : depth + 1], 1.0) * carry + behind[:depth]


def keys_behind(own):
    return [moved_along(own, "z", step) if step else own for step in range(lax.axis_size("z"))]


def all_slots(blocks):
    blocks = jnp.stack(blocks)
    slots = jnp.stack([blocks, shifted(blocks, "x", 1)], axis=1)
    return slots.reshape(-1, *blocks.shape[1:])


def sum_key_grads(kept, swapped, received):
    kept = kept + swapped.astype(jnp.float32)
    own = kept[0]
    for step in range(1, kept.shape[0]):
        got = moved_along(kept[step].astype(jnp.bfloat16), "z", -step)
        received.append(got)
        own = own + got.astype(jnp.float32)
    return own


def on_device(
    tokens,
    gain_one,
    w_in,
    w_step,
    conv_weight,
    conv_bias,
    mamba_heads,
    skip_weight,
    w_query,
    w_keyval,
    w_attn_out,
    w_mix_out,
    gain_two,
    w_gate_up,
    w_down,
    cotangent,
):
    width = tokens.shape[2]
    row_count = tokens.shape[1]
    inner_width = MHEADS * MHEAD_DIM
    device_count = math.prod(lax.axis_size(axis) for axis in every_axis)
    channels = conv_weight.shape[1] * device_count
    key_width = KVHEADS * HEAD_DIM
    query_width = QHEADS * HEAD_DIM
    own_rows = gain_one.shape[0]
    at_z, at_x = lax.axis_index("z"), lax.axis_index("x")
    place = jnp.stack([at_z, at_x]).astype(jnp.int32)

    taps = jnp.concatenate([conv_weight, conv_bias[None]], axis=0)
    tap_columns = -(-taps.size // own_rows)
    tap_shard = jnp.pad(taps.reshape(-1), (0, tap_columns * own_rows - taps.size))
    query_at = channels + w_keyval.shape[1]
    step_at = query_at + query_width
    gain_at = step_at + w_step.shape[1]
    tap_at = gain_at + 2
    conv_shard = jnp.concatenate(
        [
            w_in[:, inner_width:],
            w_keyval,
            w_query,
            w_step,
            gain_one[:, None],
            gain_two[:, None],
            tap_shard.reshape(tap_columns, own_rows).T,
            jnp.zeros((own_rows, -(tap_at + tap_columns) % 128), jnp.bfloat16),
        ],
        axis=1,
    )
    middle = conv_shard.shape[1] // 256 * 128
    (pair_a, pair_b), arrived = gather_stages(conv_shard, middle)
    late_shards = [w_in[:, :inner_width], w_mix_out.T, w_attn_out.T, w_gate_up, w_down.T]
    late_shard = after(jnp.concatenate(late_shards, axis=1), *arrived)
    late = lax.all_gather(late_shard, every_axis, axis=0, tiled=True)
    out_at = inner_width
    ff_at = out_at + inner_width + query_width
    full_gate_z, full_out, full_gate, full_up, full_down = jnp.split(
        late, [out_at, ff_at, ff_at + FF, ff_at + 2 * FF], axis=1
    )

    order_x, order_y = lax.optimization_barrier((width_order(width, "x"), width_order(width, "y")))
    inputs = tokens[0].astype(jnp.float32)
    grad_output = cotangent[0]
    small = jnp.concatenate(
        [half[:, gain_at - middle : tap_at + tap_columns - middle] for half in pair_b], axis=0
    )
    small_rows = lax.dot_general(
        small, order_x, (((0,), (1,)), ((), ())), preferred_element_type=jnp.float32
    )
    gain_one_float, gain_two_float = small_rows[0], small_rows[1]
    tap_all = small_rows[2:].reshape(tap_columns, device_count, own_rows)
    tap_all = jnp.swapaxes(tap_all, 0, 1).reshape(device_count, -1)[:, : taps.size]
    tap_all = jnp.swapaxes(tap_all.reshape(-1, *taps.shape), 0, 1).reshape(taps.shape[0], channels)

    def reordered(rows, order):
        return plain_dot(rows, order).astype(jnp.bfloat16)

    normed = rms_norm(inputs, gain_one_float).astype(jnp.bfloat16)
    normed_x, normed_y = reordered(normed, order_x), reordered(normed, order_y)
    projected_a = times_rows(normed_y, pair_a)
    projected_b = times_rows(normed_x, pair_b)
    conv_input = jnp.concatenate(
        [
            projected_a.astype(jnp.bfloat16),
            projected_b[:, : channels - middle].astype(jnp.bfloat16),
        ],
        axis=1,
    )
    keyval_raw = projected_b[:, channels - middle : query_at - middle]
    query_raw = projected_b[:, query_at - middle : step_at - middle]
    step_raw = projected_b[:, step_at - middle : gain_at - middle]
    positions = (at_z * lax.axis_size("x") + at_x) * row_count + jnp.arange(
        row_count, dtype=jnp.int32
    )
    cosine, sine = turn_columns(positions)
    keyval_cols = keyval_raw.T
    key_cols = turn_rows(keyval_cols[:key_width], cosine, sine)
    by_head = (KVHEADS, 1, HEAD_DIM, row_count)
    own_keyval = jnp.concatenate(
        [key_cols.reshape(by_head), keyval_cols[key_width:].reshape(by_head)], axis=1
    ).reshape(2 * key_width, row_count)
    key_blocks = keys_behind(own_keyval.T.astype(jnp.bfloat16))
    query_cols = turn_rows(query_raw.T, cosine, sine).astype(jnp.bfloat16)
    border = lax.ppermute(
        conv_input[row_count - (CONV - 1) :],
        seq_axes,
        [(i, i + 1) for i in range(lax.axis_size(seq_axes) - 1)],
    )
    extended = jnp.concatenate([border, conv_input], axis=0).astype(jnp.float32)
    act, pull_conv = jax.vjp(conv_act, extended, tap_all[:CONV], tap_all[CONV])
    step_size = jax.nn.softplus(step_raw + mamba_heads[1][None, :])
    log_decay = -jnp.exp(mamba_heads[0])[None, :] * step_size
    by_chunk = by_chunks(log_decay)
    chunk_rows = by_chunk.shape[1]
    lower = jnp.tril(jnp.ones((chunk_rows, chunk_rows), jnp.float32))
    cum = jnp.stack([jnp.dot(lower, c, precision=highest_precision) for c in by_chunk])
    cum = cum.reshape(log_decay.shape)
    y_local, grown, fresh_state, tail, *key_blocks = after(
        (*ssd_local(act, cum, step_size), *key_blocks)
    )
    all_keyval = all_slots(key_blocks)
    all_cols = jnp.swapaxes(all_keyval, 1, 2)
    y_local = y_local.reshape(row_count, inner_width)
    grown = grown.reshape(row_count, inner_width)
    behind, other_state, passed = send_states(fresh_state, tail, 1)
    attended_cols, logs = attend(place, after(query_cols, other_state), all_keyval, all_cols)
    attended_cols, logs, *passed = after((attended_cols, logs, *passed))
    carry_state = carried(behind, passed, 1)
    gate_z = plain_dot(normed, full_gate_z)
    attention_rows = attended_cols.T.astype(jnp.bfloat16)

    skip_row = jnp.repeat(skip_weight, MHEAD_DIM)[None, :]
    output_low = act[:, inner_width + STATE :].astype(jnp.bfloat16)
    ssm_y = (
        y_local
        + grown * plain_dot(output_low, carry_state.astype(jnp.bfloat16))
        + skip_row * act[:, :inner_width]
    )
    gate_sigmoid = jax.nn.sigmoid(gate_z)
    mixer = (ssm_y * gate_z * gate_sigmoid).astype(jnp.bfloat16)
    branches = jnp.concatenate([mixer, attention_rows], axis=1)
    hidden = inputs + back_product(branches, full_out)
    normed_two = rms_norm(hidden, gain_two_float).astype(jnp.bfloat16)
    gate_part = plain_dot(normed_two, full_gate)
    up_part = plain_dot(normed_two, full_up)
    activated = (jax.nn.silu(gate_part) * up_part).astype(jnp.bfloat16)
    result = hidden + back_product(activated, full_down)
    output = result.astype(jnp.bfloat16)[None]

    grad_activated = plain_dot(grad_output, full_down)
    core_got = []
    down_half = FF // 2
    ff_sigmoid = jax.nn.sigmoid(gate_part)
    grad_gate = grad_activated * up_part * ff_sigmoid * (1.0 + gate_part * (1.0 - ff_sigmoid))
    grad_gate = grad_gate.astype(jnp.bfloat16)
    grad_up = (grad_activated * gate_part * ff_sigmoid).astype(jnp.bfloat16)
    gate_total = core_sum(reordered(normed_two, order_x), grad_gate, "x", core_got)
    up_total = core_sum(reordered(normed_two, order_y), grad_up, "y", core_got)
    down_a = core_sum(reordered(grad_output, order_x), activated[:, :down_half], "x", [])
    down_b = core_sum(reordered(grad_output, order_y), activated[:, down_half:], "y", [])
    ff_got = []
    ff_later = []
    ff_parts = send_layers(
        layer_sums(*first_sums([gate_total, down_a], [up_total, down_b], ff_got), ff_later)
    )
    grad_normed_two = back_product(after(grad_gate, *core_got), full_gate) + back_product(
        grad_up, full_up
    )
    _, pull_two = jax.vjp(rms_norm, hidden, gain_two_float)
    grad_hidden_norm, grad_gain_two = pull_two(grad_normed_two)
    grad_hidden = grad_output.astype(jnp.float32) + grad_hidden_norm
    grad_branch = grad_hidden.astype(jnp.bfloat16)
    grad_branches = after(plain_dot(grad_branch, full_out), ff_got[1], ff_got[3])
    grad_mixer = grad_branches[:, :inner_width]
    grad_y = grad_mixer * gate_z * gate_sigmoid
    grad_gate_z = grad_mixer * ssm_y * gate_sigmoid * (1.0 + gate_z * (1.0 - gate_sigmoid))
    from_output = outer_product(output_low, (grown * grad_y).astype(jnp.bfloat16))
    behind, other_state, passed = send_states(from_output, tail, -1)

    grad_attention = grad_branches[:, inner_width:].astype(jnp.bfloat16)
    out_got = []
    out_total = core_sum(reordered(grad_branch, order_y), branches, "y", out_got)
    grad_gate_low = grad_gate_z.astype(jnp.bfloat16)
    in_gate_total = core_sum(normed_x, grad_gate_low, "x", out_got)
    grad_normed_part = back_product(grad_gate_low, full_gate_z)
    grad_cols = grad_attention.T
    query_rows = query_cols.T

    grad_query_cols, kept, other = attend_back(
        after(place, gate_total, up_total, other_state),
        query_cols,
        query_rows,
        grad_cols,
        grad_attention,
        attended_cols,
        logs,
        all_keyval,
        all_cols,
    )
    grad_query_cols, kept, other, *passed = after(
        (grad_query_cols, kept, other, *passed), ff_got[0], ff_got[2], *out_got
    )
    grad_end = carried(behind, passed, -1)
    swapped = shifted(other, "x", 1)
    key_got = []
    own_grads = sum_key_grads(kept, swapped, key_got)
    mid_got = []
    mid_both = first_sums([in_gate_total], [out_total], mid_got)
    grad_query = turn_rows(grad_query_cols, cosine, -sine).T.astype(jnp.bfloat16)
    own_cols = own_grads.T.reshape(KVHEADS, 2, HEAD_DIM, row_count)
    grad_keys = turn_rows(own_cols[:, 0].reshape(key_width, row_count), cosine, -sine)
    grad_keyval = jnp.concatenate([grad_keys, own_cols[:, 1].reshape(key_width, row_count)], axis=0)
    grad_keyval = grad_keyval.T.astype(jnp.bfloat16)

    ssd_skip = after(
        skip_row, grad_normed_part
    )
    grad_act, grad_step_size, grad_log, grad_skip = ssd_back(
        act, cum, step_size, grad_y, carry_state, grad_end, ssd_skip
    )
    grad_act, grad_step_size, grad_log = after(
        (grad_act, grad_step_size, grad_log), *ff_later, *mid_got, swapped
    )
    grad_step_size = grad_step_size - grad_log * jnp.exp(mamba_heads[0])[None, :]
    grad_step_raw = grad_step_size * jax.nn.sigmoid(step_raw + mamba_heads[1][None, :])
    grad_heads = jnp.stack([jnp.sum(grad_log * log_decay, axis=0), jnp.sum(grad_step_raw, axis=0)])
    grad_extended, grad_conv_weight, grad_conv_bias = pull_conv(grad_act)
    grad_extended, *ff_parts = after((grad_extended, *ff_parts), *key_got)
    ff_sums = sum_layers(ff_parts)
    rim_back = lax.ppermute(
        grad_extended[: CONV - 1],
        seq_axes,
        [(i + 1, i) for i in range(lax.axis_size(seq_axes) - 1)],
    )
    grad_conv_input = grad_extended[CONV - 1 :] + jnp.pad(
        rim_back, ((row_count - (CONV - 1), 0), (0, 0))
    )
    grad_step_low = jnp.pad(
        grad_step_raw.astype(jnp.bfloat16), ((0, 0), (0, conv_shard.shape[1] - gain_at))
    )
    grad_few = jnp.concatenate([grad_keyval, grad_query, grad_step_low], axis=1)
    few_core_got, last_core_got = [], []
    few_total = core_sum(normed_y, grad_few, "y", few_core_got)
    grad_conv_low = after(grad_conv_input.astype(jnp.bfloat16), *few_core_got)
    conv_total = core_sum(normed_x, grad_conv_low, "x", last_core_got)
    last_got, last_later = [], []
    mid_parts = send_layers(layer_sums(*mid_both, [], last_core_got))
    last_parts = send_layers(
        layer_sums(*first_sums([conv_total], [few_total], last_got), last_later)
    )
    last_parts, *mid_parts = after((tuple(last_parts), *mid_parts), *last_later)
    last_sums, mid_sums = sum_layers(last_parts), sum_layers(mid_parts)
    grad_normed = lax.dot_general(
        jnp.concatenate(
            [
                times_rows_back(grad_conv_low[:, :middle], pair_a),
                times_rows_back(
                    jnp.concatenate([grad_conv_low[:, middle:], grad_few], axis=1), pair_b
                ),
            ],
            axis=1,
        ),
        jnp.concatenate([order_y, order_x], axis=1).astype(jnp.float32),
        (((1,), (1,)), ((), ())),
        precision=lax.Precision.HIGH,
        preferred_element_type=jnp.float32,
    )
    _, pull_one = jax.vjp(rms_norm, inputs, gain_one_float)
    grad_input_norm, grad_gain_one = pull_one(grad_normed + grad_normed_part)
    input_grad = (grad_hidden + grad_input_norm)[None]
    gain_grads = jnp.stack([grad_gain_two, grad_gain_one])

    def padded(row):
        return jnp.pad(row, ((0, 0), (0, channels - row.shape[1])))

    head_row = jnp.concatenate(
        [grad_heads[:1], grad_heads[1:], jnp.sum(grad_skip.reshape(MHEADS, -1), axis=1)[None]],
        axis=1,
    )
    summed = sum_everywhere(
        after(
            jnp.concatenate(
                [
                    grad_conv_weight,
                    grad_conv_bias[None],
                    padded(gain_grads),
                    padded(head_row),
                ],
                axis=0,
            ),
            *last_core_got,
        ),
        {"y": last_got, "z": last_later},
    )
    device = lax.axis_index(every_axis)
    own_channels = conv_weight.shape[1]
    own_taps = lax.dynamic_slice_in_dim(summed[: CONV + 1], device * own_channels, own_channels, 1)
    own_gain_two = lax.dynamic_slice_in_dim(summed[CONV + 1], device * own_rows, own_rows)
    own_gain_one = lax.dynamic_slice_in_dim(summed[CONV + 2], device * own_rows, own_rows)
    head_sums_row = summed[CONV + 3]
    return (
        output,
        input_grad,
        own_gain_one,
        jnp.concatenate([mid_sums[:, :inner_width], last_sums[:, :channels]], axis=1),
        last_sums[:, step_at:gain_at],
        own_taps[:CONV],
        own_taps[CONV],
        head_sums_row[: 2 * MHEADS].reshape(2, MHEADS),
        head_sums_row[2 * MHEADS : 3 * MHEADS],
        last_sums[:, query_at:step_at],
        last_sums[:, channels:query_at],
        mid_sums[:, 2 * inner_width :].T,
        mid_sums[:, inner_width : 2 * inner_width].T,
        own_gain_two,
        jnp.concatenate([ff_sums[:, :FF], ff_sums[:, FF + down_half : 2 * FF + down_half]], axis=1),
        jnp.concatenate(
            [ff_sums[:, FF : FF + down_half], ff_sums[:, 2 * FF + down_half :]], axis=1
        ).T,
    )


def solution(mesh):
    dp, seq = mesh.shape["dp"], mesh.shape["seq"]
    by_axis = Mesh(mesh.devices.reshape(dp // 2, 2, seq // 2, 2), every_axis)
    pieces = P(("y", "core"), seq_axes, None)
    rows = P(every_axis, None)
    columns = P(None, every_axis)
    vector = P(every_axis)
    weights = (rows, rows, columns, columns, vector, rows, columns)
    return jax.shard_map(
        on_device,
        mesh=by_axis,
        in_specs=(pieces, vector, rows, rows, columns, vector, P(), P(), *weights, pieces),
        out_specs=(pieces, pieces, vector, rows, rows, columns, vector, P(), P(), *weights),
        check_vma=False,
    )
```

```python
import math
from functools import partial

import jax
import jax.experimental.pallas as pl
import jax.experimental.pallas.tpu as pltpu
import jax.numpy as jnp
from jax import lax
from jax.sharding import Mesh
from jax.sharding import PartitionSpec as P

MHEADS = 24
MHEAD_DIM = 64
STATE = 128
CONV = 4
QHEADS = 8
KVHEADS = 2
HEAD_DIM = 64
FF = 2048


norm_epsilon = 1e-06
rope_base = 100000000000.0
masked_score = -1e30
highest_precision = lax.Precision.HIGHEST
seq_axes = ("z", "x")
every_axis = ("y", "core", "z", "x")


def rms_norm(values, gain_vector):
    return (
        values
        * lax.rsqrt(jnp.mean(values * values, axis=-1, keepdims=True) + norm_epsilon)
        * gain_vector
    )


def outer_product(left, right):
    return lax.dot_general(
        left, right, (((0,), (0,)), ((), ())), preferred_element_type=jnp.float32
    )


def back_product(grad_rows, weight_matrix):
    return lax.dot_general(
        grad_rows, weight_matrix, (((1,), (1,)), ((), ())), preferred_element_type=jnp.float32
    )


def turn_columns(positions):
    half = HEAD_DIM // 2
    exponents = jnp.arange(half).astype(jnp.float32) * (2.0 / HEAD_DIM)
    frequency = rope_base ** (-exponents)
    angles = frequency[:, None] * positions.astype(jnp.float32)[None, :]
    return (jnp.cos(angles), jnp.sin(angles))


def turn_rows(values, cosine, sine):
    half = HEAD_DIM // 2
    heads = values.reshape(-1, 2, half, values.shape[1])
    first, second = heads[:, 0], heads[:, 1]
    turned = [first * cosine - second * sine, second * cosine + first * sine]
    return jnp.stack(turned, axis=1).reshape(values.shape)


def conv_act(extended, conv_weight, conv_bias):
    row_count = extended.shape[0] - (CONV - 1)
    conv_sum = conv_bias[None, :] + conv_weight[0][None, :] * extended[0:row_count]
    for offset in range(1, CONV):
        conv_sum = conv_sum + conv_weight[offset][None, :] * extended[offset : offset + row_count]
    return jax.nn.silu(conv_sum)


log2_e = math.log2(math.e)
group_size = QHEADS // KVHEADS
score_scale = 1.0 / math.sqrt(HEAD_DIM)
compiler_room = pltpu.CompilerParams(vmem_limit_bytes=48 * 1024 * 1024)


def plain_dot(left, right):
    return jnp.dot(left, right, preferred_element_type=jnp.float32)


def head_span(head):
    return slice(head * HEAD_DIM, (head + 1) * HEAD_DIM)


def hidden_keys(rows):
    key_at = lax.broadcasted_iota(jnp.int32, (rows, rows), 0)
    query_at = lax.broadcasted_iota(jnp.int32, (rows, rows), 1)
    return key_at > query_at


def slot_of(index, place_ref):
    z, x = lax.shift_right_logical(index, 1), lax.bitwise_and(index, 1)
    return 2 * (place_ref[0] - z) + lax.bitwise_xor(x, place_ref[1])


def attend_kernel(place_ref, query_ref, keyval_ref, keyval_cols_ref, out_ref, log_ref, best_ref, sum_ref):
    rows = query_ref.shape[1]
    scale = log2_e * score_scale

    def scores_of(piece, head):
        group = head // group_size
        keys = keyval_ref[piece, :, 2 * group * HEAD_DIM : 2 * (group + 1) * HEAD_DIM]
        query = query_ref[head_span(head), :]
        return plain_dot(keys, jnp.concatenate([query, jnp.zeros_like(query)], axis=0)) * scale

    def values_of(piece, head):
        return keyval_cols_ref[piece, head_span(2 * (head // group_size) + 1), :]

    for head in range(QHEADS):
        scores = jnp.where(hidden_keys(rows), masked_score, scores_of(0, head))
        best = jnp.max(scores, axis=0, keepdims=True)
        weights = jnp.exp2(scores - best)
        best_ref[head : head + 1, :] = best
        sum_ref[head : head + 1, :] = jnp.sum(weights, axis=0, keepdims=True)
        out_ref[head_span(head), :] = plain_dot(values_of(0, head), weights.astype(jnp.bfloat16))

    def piece_step(index, carry):
        piece = slot_of(index, place_ref)
        for head in range(QHEADS):
            scores = scores_of(piece, head)
            old = best_ref[head : head + 1, :]
            best = jnp.maximum(old, jnp.max(scores, axis=0, keepdims=True))
            fade = jnp.exp2(old - best)
            weights = jnp.exp2(scores - best)
            best_ref[head : head + 1, :] = best
            sum_ref[head : head + 1, :] = sum_ref[head : head + 1, :] * fade + jnp.sum(
                weights, axis=0, keepdims=True
            )
            out_ref[head_span(head), :] = out_ref[head_span(head), :] * fade + plain_dot(
                values_of(piece, head), weights.astype(jnp.bfloat16)
            )
        return carry

    lax.fori_loop(0, 2 * place_ref[0] + place_ref[1], piece_step, 0)
    total = sum_ref[...]
    log_ref[...] = best_ref[...] + jnp.log2(total)
    for head in range(QHEADS):
        out_ref[head_span(head), :] = out_ref[head_span(head), :] / total[head : head + 1, :]


def in_vmem(count):
    return [pl.BlockSpec(memory_space=pltpu.VMEM)] * count


def attend(place, queries, keyvals, keyval_cols):
    rows = queries.shape[1]
    flops = 4 * queries.size * rows * keyvals.shape[0]
    return pl.pallas_call(
        attend_kernel,
        out_shape=(
            jax.ShapeDtypeStruct(queries.shape, jnp.float32),
            jax.ShapeDtypeStruct((QHEADS, rows), jnp.float32),
        ),
        in_specs=[pl.BlockSpec(memory_space=pltpu.SMEM)] + in_vmem(3),
        out_specs=tuple(in_vmem(2)),
        scratch_shapes=[pltpu.VMEM((QHEADS, rows), jnp.float32)] * 2,
        compiler_params=compiler_room,
        cost_estimate=pl.CostEstimate(
            flops=8 * flops, bytes_accessed=4 * keyvals.size, transcendentals=flops // 256
        ),
        name="attend",
    )(place, queries, keyvals, keyval_cols)


def attend_back_kernel(
    place_ref,
    query_ref,
    query_rows_ref,
    grad_ref,
    grad_rows_ref,
    out_ref,
    log_ref,
    keyval_ref,
    keyval_cols_ref,
    grad_query_ref,
    grad_own_ref,
    grad_other_ref,
    dots_ref,
    query_side_ref,
    grad_side_ref,
):
    rows = query_ref.shape[1]
    scale = log2_e * score_scale
    grad_query_ref[...] = jnp.zeros_like(grad_query_ref)
    for head in range(QHEADS):
        span = head_span(head)
        dots_ref[head : head + 1, :] = jnp.sum(
            grad_ref[span, :].astype(jnp.float32) * out_ref[span, :], axis=0, keepdims=True
        )
        query = (query_rows_ref[:, span].astype(jnp.float32) * score_scale).astype(jnp.bfloat16)
        grad = grad_rows_ref[:, span]
        query_side_ref[head] = jnp.concatenate([query, jnp.zeros_like(query)], axis=1)
        grad_side_ref[head] = jnp.concatenate([jnp.zeros_like(grad), grad], axis=1)

    def one_piece(piece, own):
        for group in range(KVHEADS):
            both = slice(2 * group * HEAD_DIM, 2 * (group + 1) * HEAD_DIM)
            keyvals = keyval_ref[piece, :, both]
            key_cols = keyval_cols_ref[piece, head_span(2 * group), :]
            total = jnp.zeros((rows, 2 * HEAD_DIM), jnp.float32)
            for head in range(group * group_size, (group + 1) * group_size):
                query, grad = query_ref[head_span(head), :], grad_ref[head_span(head), :]
                blank = jnp.zeros_like(query)
                scores = plain_dot(keyvals, jnp.concatenate([query, blank], axis=0)) * scale
                weights = jnp.exp2(scores - log_ref[head : head + 1, :])
                if own:
                    weights = jnp.where(hidden_keys(rows), 0.0, weights)
                grad_weights = plain_dot(keyvals, jnp.concatenate([blank, grad], axis=0))
                grad_scores = weights * (grad_weights - dots_ref[head : head + 1, :])
                grad_scores = grad_scores.astype(jnp.bfloat16)
                grad_query_ref[head_span(head), :] += plain_dot(key_cols, grad_scores)
                total = total + plain_dot(grad_scores, query_side_ref[head])
                total = total + plain_dot(weights.astype(jnp.bfloat16), grad_side_ref[head])
            if own:
                grad_own_ref[0, :, both] = total
            else:
                put_piece(piece, both, total)

    def put_piece(piece, both, total):
        behind = lax.shift_right_logical(piece, 1)

        @pl.when(lax.bitwise_and(piece, 1) == 0)
        def _():
            grad_own_ref[behind, :, both] = total

        @pl.when(lax.bitwise_and(piece, 1) == 1)
        def _():
            grad_other_ref[behind, :, both] = total.astype(jnp.bfloat16)

    def clear(step, carry):
        grad_own_ref[step] = jnp.zeros(grad_own_ref.shape[1:], jnp.float32)
        grad_other_ref[step] = jnp.zeros(grad_other_ref.shape[1:], jnp.bfloat16)
        return carry

    def earlier(index, carry):
        one_piece(slot_of(index, place_ref), False)
        return carry

    lax.fori_loop(0, grad_own_ref.shape[0], clear, 0)
    one_piece(0, True)
    lax.fori_loop(0, 2 * place_ref[0] + place_ref[1], earlier, 0)
    grad_query_ref[...] = grad_query_ref[...] * score_scale


def attend_back(place, queries, query_rows, grads, grad_rows, outs, logs, keyvals, keyval_cols):
    slots, rows, width = keyvals.shape
    flops = 10 * queries.size * rows * slots
    return pl.pallas_call(
        attend_back_kernel,
        out_shape=(
            jax.ShapeDtypeStruct(queries.shape, jnp.float32),
            jax.ShapeDtypeStruct((slots // 2, rows, width), jnp.float32),
            jax.ShapeDtypeStruct((slots // 2, rows, width), jnp.bfloat16),
        ),
        in_specs=[pl.BlockSpec(memory_space=pltpu.SMEM)] + in_vmem(8),
        out_specs=tuple(in_vmem(3)),
        scratch_shapes=[
            pltpu.VMEM((QHEADS, rows), jnp.float32),
            pltpu.VMEM((QHEADS, rows, 2 * HEAD_DIM), jnp.bfloat16),
            pltpu.VMEM((QHEADS, rows, 2 * HEAD_DIM), jnp.bfloat16),
        ],
        compiler_params=compiler_room,
        cost_estimate=pl.CostEstimate(
            flops=6 * flops, bytes_accessed=4 * keyvals.size, transcendentals=flops // 640
        ),
        name="attend_back",
    )(place, queries, query_rows, grads, grad_rows, outs, logs, keyvals, keyval_cols)


ssd_rows = 128


def two_parts(values):
    high = values.astype(jnp.bfloat16)
    rest = values - high.astype(jnp.float32)
    middle = rest.astype(jnp.bfloat16)
    low = (rest - middle.astype(jnp.float32)).astype(jnp.bfloat16)
    return jnp.concatenate([high, middle, low], axis=1)


def head_columns(heads, parts):
    shape = (heads * parts, heads * MHEAD_DIM)
    head = lax.broadcasted_iota(jnp.int32, shape, 0) % heads
    channel = lax.broadcasted_iota(jnp.int32, shape, 1) // MHEAD_DIM
    return jnp.where(head == channel, 1.0, 0.0).astype(jnp.bfloat16)


def widen(values, spread):
    return plain_dot(two_parts(values), spread)


def head_sums(values, spread):
    heads = spread.shape[0]
    high = values.astype(jnp.bfloat16)
    low = (values - high.astype(jnp.float32)).astype(jnp.bfloat16)
    total = nt_dot(high, spread) + nt_dot(low, spread)
    return total


def nt_dot(left, right):
    return lax.dot_general(
        left, right, (((1,), (1,)), ((), ())), preferred_element_type=jnp.float32
    )


def split_pair(pair, axis):
    lane = lax.broadcasted_iota(jnp.int32, pair.shape, 1)
    blank = jnp.zeros_like(pair)
    return jnp.concatenate(
        [jnp.where(lane < MHEAD_DIM, pair, blank), jnp.where(lane < MHEAD_DIM, blank, pair)],
        axis=axis,
    )


def bf(values):
    return values.astype(jnp.bfloat16)


def ssd_kernel(act_ref, cum_ref, cum_rows_ref, step_ref, spread_ref, y_ref, grown_ref, state_ref, tail_ref):
    chunks, rows, inner = y_ref.shape
    spread = spread_ref[...]
    state_ref[...] = jnp.zeros_like(state_ref)
    tail_ref[...] = jnp.zeros_like(tail_ref)
    late = lax.broadcasted_iota(jnp.int32, (rows, rows), 0) >= lax.broadcasted_iota(
        jnp.int32, (rows, rows), 1
    )

    def one_chunk(chunk, before):
        act = act_ref[chunk]
        cum = cum_ref[chunk]
        cum_rows = cum_rows_ref[chunk]
        scaled = act[:, :inner] * widen(step_ref[chunk], spread)
        input_mat = act[:, inner : inner + STATE]
        output_low = bf(act[:, inner + STATE :])
        last = cum[rows - 1 : rows, :]
        grown_ref[chunk] = widen(jnp.exp(cum + before), spread)
        mixing = nt_dot(output_low, bf(input_mat))
        state = state_ref[...]
        from_state = plain_dot(output_low, bf(state)) * widen(jnp.exp(cum), spread)
        scaled_low = bf(scaled)
        for pair in range(MHEADS // 2):
            kernels = []
            for head in (2 * pair, 2 * pair + 1):
                gap = cum[:, head : head + 1] - cum_rows[head : head + 1, :]
                kernels.append(bf(jnp.exp(jnp.where(late, gap, masked_score)) * mixing))
            span = slice(2 * pair * MHEAD_DIM, (2 * pair + 2) * MHEAD_DIM)
            y_ref[chunk, :, span] = from_state[:, span] + plain_dot(
                jnp.concatenate(kernels, axis=1), split_pair(scaled_low[:, span], 0)
            )
        weighted = scaled * widen(jnp.exp(last - cum), spread)
        fade = widen(jnp.exp(jnp.broadcast_to(last, (8, last.shape[1]))), spread)[:1]
        state_ref[...] = state * fade + plain_dot(bf(input_mat.T), bf(weighted))
        return before + last

    total = lax.fori_loop(0, chunks, one_chunk, jnp.zeros((1, cum_ref.shape[2]), jnp.float32))
    tail_ref[...] = widen(jnp.exp(jnp.broadcast_to(total, (8, total.shape[1]))), spread)


def by_chunks(values):
    return values.reshape(-1, math.gcd(values.shape[0], ssd_rows), values.shape[1])


def ssd_local(act, cum, step_size):
    act, cum, step_size = by_chunks(act), by_chunks(cum), by_chunks(step_size)
    chunks, rows, _ = act.shape
    inner = MHEADS * MHEAD_DIM
    return pl.pallas_call(
        ssd_kernel,
        out_shape=(
            jax.ShapeDtypeStruct((chunks, rows, inner), jnp.float32),
            jax.ShapeDtypeStruct((chunks, rows, inner), jnp.float32),
            jax.ShapeDtypeStruct((STATE, inner), jnp.float32),
            jax.ShapeDtypeStruct((8, inner), jnp.float32),
        ),
        in_specs=in_vmem(5),
        out_specs=tuple(in_vmem(4)),
        compiler_params=compiler_room,
        cost_estimate=pl.CostEstimate(
            flops=chunks * rows * inner * 10000, bytes_accessed=act.size * 16, transcendentals=0
        ),
        name="ssd",
    )(act, cum, jnp.swapaxes(cum, 1, 2), step_size, head_columns(MHEADS, 3))


def ssd_back_kernel(
    act_ref,
    cum_ref,
    cum_rows_ref,
    step_ref,
    grad_ref,
    carry_ref,
    grad_end_ref,
    skip_ref,
    spread_ref,
    grad_act_ref,
    grad_step_ref,
    grad_log_ref,
    grad_skip_ref,
    states_ref,
    grad_state_ref,
    sums_ref,
):
    chunks, rows, _ = act_ref.shape
    inner = grad_ref.shape[2]
    heads = cum_ref.shape[2]
    spread = spread_ref[...]
    one_spread = spread[:heads]
    at_row = lax.broadcasted_iota(jnp.int32, (rows, rows), 0)
    at_column = lax.broadcasted_iota(jnp.int32, (rows, rows), 1)

    def fade_of(last):
        return widen(jnp.exp(jnp.broadcast_to(last, (8, heads))), spread)[:1]

    states_ref[0] = carry_ref[...]
    for chunk in range(chunks - 1):
        cum = cum_ref[chunk]
        last = cum[rows - 1 : rows, :]
        act = act_ref[chunk]
        weighted = act[:, :inner] * widen(jnp.exp(last - cum) * step_ref[chunk], spread)
        states_ref[chunk + 1] = states_ref[chunk] * fade_of(last) + plain_dot(
            bf(act[:, inner : inner + STATE].T), bf(weighted)
        )
    grad_state_ref[...] = grad_end_ref[...]
    grad_skip_ref[...] = jnp.zeros_like(grad_skip_ref)
    sums_ref[...] = jnp.zeros_like(sums_ref)

    def one_chunk(turn, carried):
        chunk = chunks - 1 - turn
        act = act_ref[chunk]
        cum = cum_ref[chunk]
        cum_rows = cum_rows_ref[chunk]
        step = step_ref[chunk]
        grad_y = grad_ref[chunk]
        last = cum[rows - 1 : rows, :]
        inputs_x = act[:, :inner]
        step_wide = widen(step, spread)
        tail = jnp.exp(last - cum)
        tail_wide = widen(tail, spread)
        scaled = inputs_x * step_wide
        scaled_low = bf(scaled)
        grad_low = bf(grad_y)
        input_low = bf(act[:, inner : inner + STATE])
        output_mat = act[:, inner + STATE :]
        output_low = bf(output_mat)
        state = states_ref[chunk]
        state_low = bf(state)
        grad_state = grad_state_ref[...]
        grad_state_low = bf(grad_state)

        grown_grad = grad_y * widen(jnp.exp(cum), spread)
        grown_low = bf(grown_grad)
        from_row = head_sums(grown_grad * plain_dot(output_low, state_low), one_spread)
        grad_output = nt_dot(grown_low, state_low)
        back = plain_dot(input_low, grad_state_low)
        from_column = head_sums(scaled * back, one_spread) * tail
        grad_input = nt_dot(bf(scaled * tail_wide), grad_state_low)
        fade = fade_of(last)
        both = jnp.sum(grad_state * state, axis=0, keepdims=True) * fade
        from_last = head_sums(jnp.broadcast_to(both, (8, inner)), one_spread)[:1]
        grad_state_ref[...] = grad_state * fade + plain_dot(bf(output_mat.T), grown_low)

        mixing = nt_dot(input_low, output_low)
        grad_mixing = jnp.zeros((rows, rows), jnp.float32)
        column_sums = jnp.zeros((rows, rows), jnp.float32)
        grad_step = jnp.zeros((rows, rows), jnp.float32)
        for pair in range(heads // 2):
            span = slice(2 * pair * MHEAD_DIM, (2 * pair + 2) * MHEAD_DIM)
            apart = split_pair(grad_low[:, span], 0)
            grad_kernels = nt_dot(scaled_low[:, span], apart)
            kernels = []
            for side in range(2):
                head = 2 * pair + side
                gap = cum_rows[head : head + 1, :] - cum[:, head : head + 1]
                decay = jnp.exp(jnp.where(at_row <= at_column, gap, masked_score))
                part = grad_kernels[:, side * rows : (side + 1) * rows] * decay
                grad_mixing = grad_mixing + part
                moved = part * mixing
                sums_ref[head : head + 1, :] = jnp.sum(moved, axis=0, keepdims=True)
                column = jnp.sum(moved, axis=1, keepdims=True)
                column_sums = jnp.where(at_column == head, column, column_sums)
                kernels.append(bf(decay * mixing))
            grad_scaled = plain_dot(jnp.concatenate(kernels, axis=1), apart)
            grad_scaled = grad_scaled + back[:, span] * tail_wide[:, span]
            grad_act_ref[chunk, :, span] = (
                grad_scaled * step_wide[:, span] + skip_ref[:, span] * grad_y[:, span]
            )
            by_step = grad_scaled * inputs_x[:, span]
            lane = lax.broadcasted_iota(jnp.int32, by_step.shape, 1)
            for side in range(2):
                mine = jnp.where((lane < MHEAD_DIM) == (side == 0), by_step, 0.0)
                column = jnp.sum(mine, axis=1, keepdims=True)
                grad_step = jnp.where(at_column == 2 * pair + side, column, grad_step)
        grad_mixing_low = bf(grad_mixing)
        grad_act_ref[chunk, :, inner : inner + STATE] = grad_input + plain_dot(
            grad_mixing_low, output_low
        )
        grad_act_ref[chunk, :, inner + STATE :] = grad_output + plain_dot(
            bf(grad_mixing.T), input_low
        )
        grad_step_ref[chunk] = grad_step[:, :heads]
        row_sums = sums_ref[...].T[:, :heads]
        ahead = row_sums - column_sums[:, :heads] + from_row
        from_here = jnp.where(at_row <= at_column, 1.0, 0.0)
        before = jnp.where(at_row > at_column, 1.0, 0.0)
        grad_log_ref[chunk] = (
            jnp.dot(from_here, ahead, precision=highest_precision)
            + jnp.dot(before, from_column, precision=highest_precision)
            + from_last
        )
        grad_skip_ref[...] += jnp.sum(inputs_x * grad_y, axis=0, keepdims=True)
        return carried

    lax.fori_loop(0, chunks, one_chunk, 0)


def ssd_back(act, cum, step_size, grad_y, carry_state, grad_end, skip_row):
    shape = act.shape
    act, cum, step_size, grad_y = (by_chunks(a) for a in (act, cum, step_size, grad_y))
    chunks, rows, width = act.shape
    inner = MHEADS * MHEAD_DIM
    grad_act, grad_step, grad_log, grad_skip = pl.pallas_call(
        ssd_back_kernel,
        out_shape=(
            jax.ShapeDtypeStruct(act.shape, jnp.float32),
            jax.ShapeDtypeStruct(cum.shape, jnp.float32),
            jax.ShapeDtypeStruct(cum.shape, jnp.float32),
            jax.ShapeDtypeStruct((1, inner), jnp.float32),
        ),
        in_specs=in_vmem(9),
        out_specs=tuple(in_vmem(4)),
        scratch_shapes=[
            pltpu.VMEM((chunks, STATE, inner), jnp.float32),
            pltpu.VMEM((STATE, inner), jnp.float32),
            pltpu.VMEM((rows, rows), jnp.float32),
        ],
        compiler_params=compiler_room,
        cost_estimate=pl.CostEstimate(
            flops=chunks * rows * inner * 25000, bytes_accessed=act.size * 16, transcendentals=0
        ),
        name="ssd_back",
    )(
        act,
        cum,
        jnp.swapaxes(cum, 1, 2),
        step_size,
        grad_y,
        carry_state,
        grad_end,
        skip_row,
        head_columns(MHEADS, 3),
    )
    flat = (shape[0], MHEADS)
    return grad_act.reshape(shape), grad_step.reshape(flat), grad_log.reshape(flat), grad_skip


def shifted(block, axis, distance):
    count = lax.axis_size(axis)
    return lax.ppermute(block, axis, [(i, (i + distance) % count) for i in range(count)])


def moved_along(block, axis, distance):
    count = lax.axis_size(axis)
    route = [(i, i + distance) for i in range(count) if 0 <= i + distance < count]
    return lax.ppermute(block, axis, route)


def width_order(width, first):
    sizes = {axis: lax.axis_size(axis) for axis in every_axis}
    rows = width // math.prod(sizes.values())
    rest = lax.broadcasted_iota(jnp.int32, (width, width), 1)
    inside, rest = rest % rows, rest // rows
    owner = {}
    for axis in ("z", "xy".replace(first, ""), first, "core"):
        owner[axis] = (rest % sizes[axis] + lax.axis_index(axis)) % sizes[axis]
        rest = rest // sizes[axis]
    usual = owner["y"]
    for axis in ("core", "z", "x"):
        usual = usual * sizes[axis] + owner[axis]
    usual = usual * rows + inside
    return (lax.broadcasted_iota(jnp.int32, (width, width), 0) == usual).astype(jnp.bfloat16)


def after(values, *others):
    return lax.optimization_barrier((values, others))[0]


def gather_stages(shard, middle):
    parts = [shard] + [shifted(shard, "z", -k) for k in range(1, lax.axis_size("z"))]
    block = jnp.concatenate(parts, axis=0)
    halves = [block[:, :middle], block[:, middle:]]
    arrived = []
    for axes in ("xy", "yx"):
        got = [
            [half] + [shifted(half, axis, -k) for k in range(1, lax.axis_size(axis))]
            for half, axis in zip(halves, axes)
        ]
        arrived += [parts[1] for parts in got]
        halves = [jnp.concatenate(parts, axis=0) for parts in lax.optimization_barrier(got)]
    return [(half, shifted(half, "core", 1)) for half in halves], arrived[:2]


def times_rows(values, pair):
    half = values.shape[1] // 2
    return plain_dot(values[:, :half], pair[0]) + plain_dot(values[:, half:], pair[1])


def times_rows_back(values, pair):
    return jnp.concatenate([back_product(values, pair[0]), back_product(values, pair[1])], axis=1)


def keep_own(total, axis, received):
    kept = total[0]
    for step in range(1, lax.axis_size(axis)):
        got = shifted(total[step].astype(jnp.bfloat16), axis, step)
        received.append(got)
        kept = kept + got.astype(jnp.float32)
    return kept


def core_sum(left, right, first, received):
    half = left.shape[1] // 2
    sizes = [lax.axis_size(axis) for axis in (first, "xy".replace(first, ""), "z")]
    got = shifted(outer_product(left[:, half:], right).astype(jnp.bfloat16), "core", 1)
    received.append(got)
    total = outer_product(left[:, :half], right) + got.astype(jnp.float32)
    return total.reshape(*sizes, -1, right.shape[1])


def side_by_side(parts):
    return parts[0] if len(parts) == 1 else jnp.concatenate(parts, axis=-1)


def first_sums(by_x, by_y, received):
    by_x = side_by_side([keep_own(total, "x", received) for total in by_x])
    by_y = side_by_side([keep_own(total, "y", received) for total in by_y])
    return by_x, by_y


def layer_sums(by_x, by_y, received):
    by_x = keep_own(by_x, "y", received)
    by_y = keep_own(by_y, "x", received)
    return jnp.concatenate([by_x, by_y], axis=-1)


def send_layers(total):
    parts = [total[step].astype(jnp.bfloat16) for step in range(1, total.shape[0])]
    return [total[0]] + [shifted(part, "z", step + 1) for step, part in enumerate(parts)]


def sum_layers(parts):
    return sum(part.astype(jnp.float32) for part in parts)


def sum_everywhere(values, holds):
    for axis in ("core", "y", "x", "z"):
        if axis in holds:
            values = after(values, *holds[axis])
        count = lax.axis_size(axis)
        step = 1
        while step < count:
            values = values + lax.ppermute(values, axis, [(i, i ^ step) for i in range(count)])
            step *= 2
    return values


def send_states(state, tail, direction):
    depth, width = state.shape
    half = width // 2
    at_x = lax.axis_index("x")
    is_second = (at_x == 1) if direction == 1 else (at_x == 0)
    packed = jnp.concatenate([state, tail], axis=0).astype(jnp.bfloat16)
    other = shifted(packed, "x", 1)
    own = packed.astype(jnp.float32)
    first = jnp.where(is_second, other.astype(jnp.float32), own)
    second = jnp.where(is_second, own, other.astype(jnp.float32))
    pair = jnp.concatenate(
        [
            second[depth : depth + 1] * first[:depth] + second[:depth],
            first[depth:] * second[depth:],
        ],
        axis=0,
    )
    mine = jnp.where(at_x == 0, pair[:, :half], pair[:, half:]).astype(jnp.bfloat16)
    steps = range(1, lax.axis_size("z"))
    passed = [moved_along(mine, "z", direction * step) for step in steps]
    return jnp.where(is_second, first, 0.0), other, passed


def carried(behind, passed, direction, received):
    depth, half = behind.shape[0] - 8, behind.shape[1] // 2
    at_x = lax.axis_index("x")
    is_second = (at_x == 1) if direction == 1 else (at_x == 0)
    total = jnp.zeros((depth, half), jnp.float32)
    fade = jnp.ones((1, half), jnp.float32)
    for got in passed:
        total = total + fade * got[:depth].astype(jnp.float32)
        fade = fade * got[depth : depth + 1].astype(jnp.float32)
    total = total.astype(jnp.bfloat16)
    rest = shifted(total, "x", 1)
    received.append(rest)
    left, right = jnp.where(at_x == 0, total, rest), jnp.where(at_x == 0, rest, total)
    carry = jnp.concatenate([left, right], axis=1).astype(jnp.float32)
    return jnp.where(is_second, behind[depth : depth + 1], 1.0) * carry + behind[:depth]


def keys_behind(own):
    return [moved_along(own, "z", step) if step else own for step in range(lax.axis_size("z"))]


def all_slots(blocks):
    blocks = jnp.stack(blocks)
    slots = jnp.stack([blocks, shifted(blocks, "x", 1)], axis=1)
    return slots.reshape(-1, *blocks.shape[1:])


def sum_key_grads(kept, swapped, received):
    kept = kept + swapped.astype(jnp.float32)
    own = kept[0]
    for step in range(1, kept.shape[0]):
        got = moved_along(kept[step].astype(jnp.bfloat16), "z", -step)
        received.append(got)
        own = own + got.astype(jnp.float32)
    return own


def on_device(
    tokens,
    gain_one,
    w_in,
    w_step,
    conv_weight,
    conv_bias,
    mamba_heads,
    skip_weight,
    w_query,
    w_keyval,
    w_attn_out,
    w_mix_out,
    gain_two,
    w_gate_up,
    w_down,
    cotangent,
):
    width = tokens.shape[2]
    row_count = tokens.shape[1]
    inner_width = MHEADS * MHEAD_DIM
    device_count = math.prod(lax.axis_size(axis) for axis in every_axis)
    channels = conv_weight.shape[1] * device_count
    key_width = KVHEADS * HEAD_DIM
    query_width = QHEADS * HEAD_DIM
    own_rows = gain_one.shape[0]
    at_z, at_x = lax.axis_index("z"), lax.axis_index("x")
    place = jnp.stack([at_z, at_x]).astype(jnp.int32)

    taps = jnp.concatenate([conv_weight, conv_bias[None]], axis=0)
    tap_columns = -(-taps.size // own_rows)
    tap_shard = jnp.pad(taps.reshape(-1), (0, tap_columns * own_rows - taps.size))
    query_at = channels + w_keyval.shape[1]
    step_at = query_at + query_width
    gain_at = step_at + w_step.shape[1]
    tap_at = gain_at + 2
    conv_shard = jnp.concatenate(
        [
            w_in[:, inner_width:],
            w_keyval,
            w_query,
            w_step,
            gain_one[:, None],
            gain_two[:, None],
            tap_shard.reshape(tap_columns, own_rows).T,
            jnp.zeros((own_rows, -(tap_at + tap_columns) % 128), jnp.bfloat16),
        ],
        axis=1,
    )
    middle = conv_shard.shape[1] // 256 * 128
    (pair_a, pair_b), arrived = gather_stages(conv_shard, middle)
    late_shards = [w_in[:, :inner_width], w_mix_out.T, w_attn_out.T, w_gate_up, w_down.T]
    late_shard = after(jnp.concatenate(late_shards, axis=1), *arrived)
    late = lax.all_gather(late_shard, every_axis, axis=0, tiled=True)
    out_at = inner_width
    ff_at = out_at + inner_width + query_width
    full_gate_z, full_out, full_gate, full_up, full_down = jnp.split(
        late, [out_at, ff_at, ff_at + FF, ff_at + 2 * FF], axis=1
    )

    order_x, order_y = lax.optimization_barrier((width_order(width, "x"), width_order(width, "y")))
    inputs = tokens[0].astype(jnp.float32)
    grad_output = cotangent[0]
    small = jnp.concatenate(
        [half[:, gain_at - middle : tap_at + tap_columns - middle] for half in pair_b], axis=0
    )
    small_rows = lax.dot_general(
        small, order_x, (((0,), (1,)), ((), ())), preferred_element_type=jnp.float32
    )
    gain_one_float, gain_two_float = small_rows[0], small_rows[1]
    tap_all = small_rows[2:].reshape(tap_columns, device_count, own_rows)
    tap_all = jnp.swapaxes(tap_all, 0, 1).reshape(device_count, -1)[:, : taps.size]
    tap_all = jnp.swapaxes(tap_all.reshape(-1, *taps.shape), 0, 1).reshape(taps.shape[0], channels)

    def reordered(rows, order):
        return plain_dot(rows, order).astype(jnp.bfloat16)

    normed = rms_norm(inputs, gain_one_float).astype(jnp.bfloat16)
    normed_x, normed_y = reordered(normed, order_x), reordered(normed, order_y)
    projected_a = times_rows(normed_y, pair_a)
    projected_b = times_rows(normed_x, pair_b)
    conv_input = jnp.concatenate(
        [
            projected_a.astype(jnp.bfloat16),
            projected_b[:, : channels - middle].astype(jnp.bfloat16),
        ],
        axis=1,
    )
    keyval_raw = projected_b[:, channels - middle : query_at - middle]
    query_raw = projected_b[:, query_at - middle : step_at - middle]
    step_raw = projected_b[:, step_at - middle : gain_at - middle]
    positions = (at_z * lax.axis_size("x") + at_x) * row_count + jnp.arange(
        row_count, dtype=jnp.int32
    )
    cosine, sine = turn_columns(positions)
    keyval_cols = keyval_raw.T
    key_cols = turn_rows(keyval_cols[:key_width], cosine, sine)
    by_head = (KVHEADS, 1, HEAD_DIM, row_count)
    own_keyval = jnp.concatenate(
        [key_cols.reshape(by_head), keyval_cols[key_width:].reshape(by_head)], axis=1
    ).reshape(2 * key_width, row_count)
    key_blocks = keys_behind(own_keyval.T.astype(jnp.bfloat16))
    query_cols = turn_rows(query_raw.T, cosine, sine).astype(jnp.bfloat16)
    border = lax.ppermute(
        conv_input[row_count - (CONV - 1) :],
        seq_axes,
        [(i, i + 1) for i in range(lax.axis_size(seq_axes) - 1)],
    )
    extended = jnp.concatenate([border, conv_input], axis=0).astype(jnp.float32)
    act, pull_conv = jax.vjp(conv_act, extended, tap_all[:CONV], tap_all[CONV])
    step_size = jax.nn.softplus(step_raw + mamba_heads[1][None, :])
    log_decay = -jnp.exp(mamba_heads[0])[None, :] * step_size
    by_chunk = by_chunks(log_decay)
    chunk_rows = by_chunk.shape[1]
    lower = jnp.tril(jnp.ones((chunk_rows, chunk_rows), jnp.float32))
    cum = jnp.stack([jnp.dot(lower, c, precision=highest_precision) for c in by_chunk])
    cum = cum.reshape(log_decay.shape)
    y_local, grown, fresh_state, tail, *key_blocks = after(
        (*ssd_local(act, cum, step_size), *key_blocks)
    )
    all_keyval = all_slots(key_blocks)
    all_cols = jnp.swapaxes(all_keyval, 1, 2)
    y_local = y_local.reshape(row_count, inner_width)
    grown = grown.reshape(row_count, inner_width)
    behind, other_state, passed = send_states(fresh_state, tail, 1)
    attended_cols, logs = attend(place, after(query_cols, other_state), all_keyval, all_cols)
    attended_cols, logs, *passed = after((attended_cols, logs, *passed))
    carry_state = carried(behind, passed, 1, [])
    gate_z = plain_dot(normed, full_gate_z)
    attention_rows = attended_cols.T.astype(jnp.bfloat16)

    skip_row = jnp.repeat(skip_weight, MHEAD_DIM)[None, :]
    output_low = act[:, inner_width + STATE :].astype(jnp.bfloat16)
    ssm_y = (
        y_local
        + grown * plain_dot(output_low, carry_state.astype(jnp.bfloat16))
        + skip_row * act[:, :inner_width]
    )
    gate_sigmoid = jax.nn.sigmoid(gate_z)
    mixer = (ssm_y * gate_z * gate_sigmoid).astype(jnp.bfloat16)
    branches = jnp.concatenate([mixer, attention_rows], axis=1)
    hidden = inputs + back_product(branches, full_out)
    normed_two = rms_norm(hidden, gain_two_float).astype(jnp.bfloat16)
    gate_part = plain_dot(normed_two, full_gate)
    up_part = plain_dot(normed_two, full_up)
    activated = (jax.nn.silu(gate_part) * up_part).astype(jnp.bfloat16)
    result = hidden + back_product(activated, full_down)
    output = result.astype(jnp.bfloat16)[None]

    grad_activated = plain_dot(grad_output, full_down)
    core_got = []
    down_half = FF // 2
    ff_sigmoid = jax.nn.sigmoid(gate_part)
    grad_gate = grad_activated * up_part * ff_sigmoid * (1.0 + gate_part * (1.0 - ff_sigmoid))
    grad_gate = grad_gate.astype(jnp.bfloat16)
    grad_up = (grad_activated * gate_part * ff_sigmoid).astype(jnp.bfloat16)
    gate_total = core_sum(reordered(normed_two, order_x), grad_gate, "x", core_got)
    up_total = core_sum(reordered(normed_two, order_y), grad_up, "y", core_got)
    down_a = core_sum(reordered(grad_output, order_x), activated[:, :down_half], "x", [])
    down_b = core_sum(reordered(grad_output, order_y), activated[:, down_half:], "y", [])
    ff_got = []
    ff_later = []
    ff_parts = send_layers(
        layer_sums(*first_sums([gate_total, down_a], [up_total, down_b], ff_got), ff_later)
    )
    grad_normed_two = back_product(after(grad_gate, *core_got), full_gate) + back_product(
        grad_up, full_up
    )
    _, pull_two = jax.vjp(rms_norm, hidden, gain_two_float)
    grad_hidden_norm, grad_gain_two = pull_two(grad_normed_two)
    grad_hidden = grad_output.astype(jnp.float32) + grad_hidden_norm
    grad_branch = grad_hidden.astype(jnp.bfloat16)
    grad_branches = after(plain_dot(grad_branch, full_out), ff_got[1], ff_got[3])
    grad_mixer = grad_branches[:, :inner_width]
    grad_y = grad_mixer * gate_z * gate_sigmoid
    grad_gate_z = grad_mixer * ssm_y * gate_sigmoid * (1.0 + gate_z * (1.0 - gate_sigmoid))
    from_output = outer_product(output_low, (grown * grad_y).astype(jnp.bfloat16))
    behind, other_state, passed = send_states(from_output, tail, -1)

    grad_attention = grad_branches[:, inner_width:].astype(jnp.bfloat16)
    out_got = []
    out_total = core_sum(reordered(grad_branch, order_y), branches, "y", out_got)
    grad_gate_low = grad_gate_z.astype(jnp.bfloat16)
    in_gate_total = core_sum(normed_x, grad_gate_low, "x", out_got)
    grad_normed_part = back_product(grad_gate_low, full_gate_z)
    grad_cols = grad_attention.T
    query_rows = query_cols.T

    grad_query_cols, kept, other = attend_back(
        after(place, gate_total, up_total, other_state),
        query_cols,
        query_rows,
        grad_cols,
        grad_attention,
        attended_cols,
        logs,
        all_keyval,
        all_cols,
    )
    grad_query_cols, kept, other, *passed = after(
        (grad_query_cols, kept, other, *passed), ff_got[0], ff_got[2], *out_got
    )
    rested = []
    grad_end = carried(behind, passed, -1, rested)
    swapped = shifted(other, "x", 1)
    key_got = []
    own_grads = sum_key_grads(kept, swapped, key_got)
    mid_got = []
    mid_both = first_sums(
        [after(in_gate_total, *rested)], [after(out_total, *rested)], mid_got
    )
    mid_later = []
    mid_parts = send_layers(layer_sums(*mid_both, mid_later))
    grad_query = turn_rows(grad_query_cols, cosine, -sine).T.astype(jnp.bfloat16)
    own_cols = own_grads.T.reshape(KVHEADS, 2, HEAD_DIM, row_count)
    grad_keys = turn_rows(own_cols[:, 0].reshape(key_width, row_count), cosine, -sine)
    grad_keyval = jnp.concatenate([grad_keys, own_cols[:, 1].reshape(key_width, row_count)], axis=0)
    grad_keyval = grad_keyval.T.astype(jnp.bfloat16)

    ssd_skip = after(
        skip_row, grad_normed_part
    )
    grad_act, grad_step_size, grad_log, grad_skip = ssd_back(
        act, cum, step_size, grad_y, carry_state, grad_end, ssd_skip
    )
    grad_act, grad_step_size, grad_log = after(
        (grad_act, grad_step_size, grad_log), *ff_later, swapped
    )
    grad_step_size = grad_step_size - grad_log * jnp.exp(mamba_heads[0])[None, :]
    grad_step_raw = grad_step_size * jax.nn.sigmoid(step_raw + mamba_heads[1][None, :])
    grad_heads = jnp.stack([jnp.sum(grad_log * log_decay, axis=0), jnp.sum(grad_step_raw, axis=0)])
    grad_extended, grad_conv_weight, grad_conv_bias = pull_conv(grad_act)
    grad_extended, *ff_parts = after((grad_extended, *ff_parts), *key_got, *mid_got)
    ff_sums = sum_layers(ff_parts)
    rim_back = lax.ppermute(
        grad_extended[: CONV - 1],
        seq_axes,
        [(i + 1, i) for i in range(lax.axis_size(seq_axes) - 1)],
    )
    grad_conv_input = grad_extended[CONV - 1 :] + jnp.pad(
        rim_back, ((row_count - (CONV - 1), 0), (0, 0))
    )
    grad_step_low = jnp.pad(
        grad_step_raw.astype(jnp.bfloat16), ((0, 0), (0, conv_shard.shape[1] - gain_at))
    )
    grad_few = jnp.concatenate([grad_keyval, grad_query, grad_step_low], axis=1)
    few_core_got, last_core_got = [], []
    few_total = core_sum(normed_y, grad_few, "y", few_core_got)
    grad_conv_low = after(
        grad_conv_input.astype(jnp.bfloat16), *few_core_got, *mid_later
    )
    conv_total = core_sum(normed_x, grad_conv_low, "x", last_core_got)
    last_got, last_later = [], []
    last_both = after(first_sums([conv_total], [few_total], last_got), *last_got)
    last_parts = send_layers(layer_sums(*last_both, last_later))
    last_parts, *mid_parts = after((tuple(last_parts), *mid_parts), *last_later)
    last_sums, mid_sums = sum_layers(last_parts), sum_layers(mid_parts)
    grad_normed = lax.dot_general(
        jnp.concatenate(
            [
                times_rows_back(grad_conv_low[:, :middle], pair_a),
                times_rows_back(
                    jnp.concatenate([grad_conv_low[:, middle:], grad_few], axis=1), pair_b
                ),
            ],
            axis=1,
        ),
        jnp.concatenate([order_y, order_x], axis=1).astype(jnp.float32),
        (((1,), (1,)), ((), ())),
        precision=lax.Precision.HIGH,
        preferred_element_type=jnp.float32,
    )
    _, pull_one = jax.vjp(rms_norm, inputs, gain_one_float)
    grad_input_norm, grad_gain_one = pull_one(grad_normed + grad_normed_part)
    input_grad = (grad_hidden + grad_input_norm)[None]
    gain_grads = jnp.stack([grad_gain_two, grad_gain_one])

    def padded(row):
        return jnp.pad(row, ((0, 0), (0, channels - row.shape[1])))

    head_row = jnp.concatenate(
        [grad_heads[:1], grad_heads[1:], jnp.sum(grad_skip.reshape(MHEADS, -1), axis=1)[None]],
        axis=1,
    )
    summed = sum_everywhere(
        after(
            jnp.concatenate(
                [
                    grad_conv_weight,
                    grad_conv_bias[None],
                    padded(gain_grads),
                    padded(head_row),
                ],
                axis=0,
            ),
            *last_core_got,
        ),
        {"x": last_got, "z": last_later},
    )
    device = lax.axis_index(every_axis)
    own_channels = conv_weight.shape[1]
    own_taps = lax.dynamic_slice_in_dim(summed[: CONV + 1], device * own_channels, own_channels, 1)
    own_gain_two = lax.dynamic_slice_in_dim(summed[CONV + 1], device * own_rows, own_rows)
    own_gain_one = lax.dynamic_slice_in_dim(summed[CONV + 2], device * own_rows, own_rows)
    head_sums_row = summed[CONV + 3]
    return (
        output,
        input_grad,
        own_gain_one,
        jnp.concatenate([mid_sums[:, :inner_width], last_sums[:, :channels]], axis=1),
        last_sums[:, step_at:gain_at],
        own_taps[:CONV],
        own_taps[CONV],
        head_sums_row[: 2 * MHEADS].reshape(2, MHEADS),
        head_sums_row[2 * MHEADS : 3 * MHEADS],
        last_sums[:, query_at:step_at],
        last_sums[:, channels:query_at],
        mid_sums[:, 2 * inner_width :].T,
        mid_sums[:, inner_width : 2 * inner_width].T,
        own_gain_two,
        jnp.concatenate([ff_sums[:, :FF], ff_sums[:, FF + down_half : 2 * FF + down_half]], axis=1),
        jnp.concatenate(
            [ff_sums[:, FF : FF + down_half], ff_sums[:, 2 * FF + down_half :]], axis=1
        ).T,
    )


def solution(mesh):
    dp, seq = mesh.shape["dp"], mesh.shape["seq"]
    by_axis = Mesh(mesh.devices.reshape(dp // 2, 2, seq // 2, 2), every_axis)
    pieces = P(("y", "core"), seq_axes, None)
    rows = P(every_axis, None)
    columns = P(None, every_axis)
    vector = P(every_axis)
    weights = (rows, rows, columns, columns, vector, rows, columns)
    return jax.shard_map(
        on_device,
        mesh=by_axis,
        in_specs=(pieces, vector, rows, rows, columns, vector, P(), P(), *weights, pieces),
        out_specs=(pieces, pieces, vector, rows, rows, columns, vector, P(), P(), *weights),
        check_vma=False,
    )
```

```python
import math
from functools import partial

import jax
import jax.experimental.pallas as pl
import jax.experimental.pallas.tpu as pltpu
import jax.numpy as jnp
from jax import lax
from jax.sharding import Mesh
from jax.sharding import PartitionSpec as P

MHEADS = 24
MHEAD_DIM = 64
STATE = 128
CONV = 4
QHEADS = 8
KVHEADS = 2
HEAD_DIM = 64
FF = 2048


norm_epsilon = 1e-06
rope_base = 100000000000.0
masked_score = -1e30
highest_precision = lax.Precision.HIGHEST
seq_axes = ("z", "x")
every_axis = ("y", "core", "z", "x")


def rms_norm(values, gain_vector):
    return (
        values
        * lax.rsqrt(jnp.mean(values * values, axis=-1, keepdims=True) + norm_epsilon)
        * gain_vector
    )


def outer_product(left, right):
    return lax.dot_general(
        left, right, (((0,), (0,)), ((), ())), preferred_element_type=jnp.float32
    )


def back_product(grad_rows, weight_matrix):
    return lax.dot_general(
        grad_rows, weight_matrix, (((1,), (1,)), ((), ())), preferred_element_type=jnp.float32
    )


def turn_columns(positions):
    half = HEAD_DIM // 2
    exponents = jnp.arange(half).astype(jnp.float32) * (2.0 / HEAD_DIM)
    frequency = rope_base ** (-exponents)
    angles = frequency[:, None] * positions.astype(jnp.float32)[None, :]
    return (jnp.cos(angles), jnp.sin(angles))


def turn_rows(values, cosine, sine):
    half = HEAD_DIM // 2
    heads = values.reshape(-1, 2, half, values.shape[1])
    first, second = heads[:, 0], heads[:, 1]
    turned = [first * cosine - second * sine, second * cosine + first * sine]
    return jnp.stack(turned, axis=1).reshape(values.shape)


def conv_act(extended, conv_weight, conv_bias):
    row_count = extended.shape[0] - (CONV - 1)
    conv_sum = conv_bias[None, :] + conv_weight[0][None, :] * extended[0:row_count]
    for offset in range(1, CONV):
        conv_sum = conv_sum + conv_weight[offset][None, :] * extended[offset : offset + row_count]
    return jax.nn.silu(conv_sum)


log2_e = math.log2(math.e)
group_size = QHEADS // KVHEADS
score_scale = 1.0 / math.sqrt(HEAD_DIM)
compiler_room = pltpu.CompilerParams(vmem_limit_bytes=48 * 1024 * 1024)


def plain_dot(left, right):
    return jnp.dot(left, right, preferred_element_type=jnp.float32)


def head_span(head):
    return slice(head * HEAD_DIM, (head + 1) * HEAD_DIM)


def hidden_keys(rows):
    key_at = lax.broadcasted_iota(jnp.int32, (rows, rows), 0)
    query_at = lax.broadcasted_iota(jnp.int32, (rows, rows), 1)
    return key_at > query_at


def slot_of(index, place_ref):
    z, x = lax.shift_right_logical(index, 1), lax.bitwise_and(index, 1)
    return 2 * (place_ref[0] - z) + lax.bitwise_xor(x, place_ref[1])


def attend_kernel(place_ref, query_ref, keyval_ref, keyval_cols_ref, out_ref, log_ref, best_ref, sum_ref):
    rows = query_ref.shape[1]
    scale = log2_e * score_scale

    def scores_of(piece, head):
        group = head // group_size
        keys = keyval_ref[piece, :, 2 * group * HEAD_DIM : 2 * (group + 1) * HEAD_DIM]
        query = query_ref[head_span(head), :]
        return plain_dot(keys, jnp.concatenate([query, jnp.zeros_like(query)], axis=0)) * scale

    def values_of(piece, head):
        return keyval_cols_ref[piece, head_span(2 * (head // group_size) + 1), :]

    for head in range(QHEADS):
        scores = jnp.where(hidden_keys(rows), masked_score, scores_of(0, head))
        best = jnp.max(scores, axis=0, keepdims=True)
        weights = jnp.exp2(scores - best)
        best_ref[head : head + 1, :] = best
        sum_ref[head : head + 1, :] = jnp.sum(weights, axis=0, keepdims=True)
        out_ref[head_span(head), :] = plain_dot(values_of(0, head), weights.astype(jnp.bfloat16))

    def piece_step(index, carry):
        piece = slot_of(index, place_ref)
        for head in range(QHEADS):
            scores = scores_of(piece, head)
            old = best_ref[head : head + 1, :]
            best = jnp.maximum(old, jnp.max(scores, axis=0, keepdims=True))
            fade = jnp.exp2(old - best)
            weights = jnp.exp2(scores - best)
            best_ref[head : head + 1, :] = best
            sum_ref[head : head + 1, :] = sum_ref[head : head + 1, :] * fade + jnp.sum(
                weights, axis=0, keepdims=True
            )
            out_ref[head_span(head), :] = out_ref[head_span(head), :] * fade + plain_dot(
                values_of(piece, head), weights.astype(jnp.bfloat16)
            )
        return carry

    lax.fori_loop(0, 2 * place_ref[0] + place_ref[1], piece_step, 0)
    total = sum_ref[...]
    log_ref[...] = best_ref[...] + jnp.log2(total)
    for head in range(QHEADS):
        out_ref[head_span(head), :] = out_ref[head_span(head), :] / total[head : head + 1, :]


def in_vmem(count):
    return [pl.BlockSpec(memory_space=pltpu.VMEM)] * count


def attend(place, queries, keyvals, keyval_cols):
    rows = queries.shape[1]
    flops = 4 * queries.size * rows * keyvals.shape[0]
    return pl.pallas_call(
        attend_kernel,
        out_shape=(
            jax.ShapeDtypeStruct(queries.shape, jnp.float32),
            jax.ShapeDtypeStruct((QHEADS, rows), jnp.float32),
        ),
        in_specs=[pl.BlockSpec(memory_space=pltpu.SMEM)] + in_vmem(3),
        out_specs=tuple(in_vmem(2)),
        scratch_shapes=[pltpu.VMEM((QHEADS, rows), jnp.float32)] * 2,
        compiler_params=compiler_room,
        cost_estimate=pl.CostEstimate(
            flops=8 * flops, bytes_accessed=4 * keyvals.size, transcendentals=flops // 256
        ),
        name="attend",
    )(place, queries, keyvals, keyval_cols)


def attend_back_kernel(
    place_ref,
    query_ref,
    query_rows_ref,
    grad_ref,
    grad_rows_ref,
    out_ref,
    log_ref,
    keyval_ref,
    keyval_cols_ref,
    grad_query_ref,
    grad_own_ref,
    grad_other_ref,
    dots_ref,
    query_side_ref,
    grad_side_ref,
):
    rows = query_ref.shape[1]
    scale = log2_e * score_scale
    grad_query_ref[...] = jnp.zeros_like(grad_query_ref)
    for head in range(QHEADS):
        span = head_span(head)
        dots_ref[head : head + 1, :] = jnp.sum(
            grad_ref[span, :].astype(jnp.float32) * out_ref[span, :], axis=0, keepdims=True
        )
        query = (query_rows_ref[:, span].astype(jnp.float32) * score_scale).astype(jnp.bfloat16)
        grad = grad_rows_ref[:, span]
        query_side_ref[head] = jnp.concatenate([query, jnp.zeros_like(query)], axis=1)
        grad_side_ref[head] = jnp.concatenate([jnp.zeros_like(grad), grad], axis=1)

    def one_piece(piece, own):
        for group in range(KVHEADS):
            both = slice(2 * group * HEAD_DIM, 2 * (group + 1) * HEAD_DIM)
            keyvals = keyval_ref[piece, :, both]
            key_cols = keyval_cols_ref[piece, head_span(2 * group), :]
            total = jnp.zeros((rows, 2 * HEAD_DIM), jnp.float32)
            for head in range(group * group_size, (group + 1) * group_size):
                query, grad = query_ref[head_span(head), :], grad_ref[head_span(head), :]
                blank = jnp.zeros_like(query)
                scores = plain_dot(keyvals, jnp.concatenate([query, blank], axis=0)) * scale
                weights = jnp.exp2(scores - log_ref[head : head + 1, :])
                if own:
                    weights = jnp.where(hidden_keys(rows), 0.0, weights)
                grad_weights = plain_dot(keyvals, jnp.concatenate([blank, grad], axis=0))
                grad_scores = weights * (grad_weights - dots_ref[head : head + 1, :])
                grad_scores = grad_scores.astype(jnp.bfloat16)
                grad_query_ref[head_span(head), :] += plain_dot(key_cols, grad_scores)
                total = total + plain_dot(grad_scores, query_side_ref[head])
                total = total + plain_dot(weights.astype(jnp.bfloat16), grad_side_ref[head])
            if own:
                grad_own_ref[0, :, both] = total
            else:
                put_piece(piece, both, total)

    def put_piece(piece, both, total):
        behind = lax.shift_right_logical(piece, 1)

        @pl.when(lax.bitwise_and(piece, 1) == 0)
        def _():
            grad_own_ref[behind, :, both] = total

        @pl.when(lax.bitwise_and(piece, 1) == 1)
        def _():
            grad_other_ref[behind, :, both] = total.astype(jnp.bfloat16)

    def clear(step, carry):
        grad_own_ref[step] = jnp.zeros(grad_own_ref.shape[1:], jnp.float32)
        grad_other_ref[step] = jnp.zeros(grad_other_ref.shape[1:], jnp.bfloat16)
        return carry

    def earlier(index, carry):
        one_piece(slot_of(index, place_ref), False)
        return carry

    lax.fori_loop(0, grad_own_ref.shape[0], clear, 0)
    one_piece(0, True)
    lax.fori_loop(0, 2 * place_ref[0] + place_ref[1], earlier, 0)
    grad_query_ref[...] = grad_query_ref[...] * score_scale


def attend_back(place, queries, query_rows, grads, grad_rows, outs, logs, keyvals, keyval_cols):
    slots, rows, width = keyvals.shape
    flops = 10 * queries.size * rows * slots
    return pl.pallas_call(
        attend_back_kernel,
        out_shape=(
            jax.ShapeDtypeStruct(queries.shape, jnp.float32),
            jax.ShapeDtypeStruct((slots // 2, rows, width), jnp.float32),
            jax.ShapeDtypeStruct((slots // 2, rows, width), jnp.bfloat16),
        ),
        in_specs=[pl.BlockSpec(memory_space=pltpu.SMEM)] + in_vmem(8),
        out_specs=tuple(in_vmem(3)),
        scratch_shapes=[
            pltpu.VMEM((QHEADS, rows), jnp.float32),
            pltpu.VMEM((QHEADS, rows, 2 * HEAD_DIM), jnp.bfloat16),
            pltpu.VMEM((QHEADS, rows, 2 * HEAD_DIM), jnp.bfloat16),
        ],
        compiler_params=compiler_room,
        cost_estimate=pl.CostEstimate(
            flops=6 * flops, bytes_accessed=4 * keyvals.size, transcendentals=flops // 640
        ),
        name="attend_back",
    )(place, queries, query_rows, grads, grad_rows, outs, logs, keyvals, keyval_cols)


ssd_rows = 128


def two_parts(values):
    high = values.astype(jnp.bfloat16)
    rest = values - high.astype(jnp.float32)
    middle = rest.astype(jnp.bfloat16)
    low = (rest - middle.astype(jnp.float32)).astype(jnp.bfloat16)
    return jnp.concatenate([high, middle, low], axis=1)


def head_columns(heads, parts):
    shape = (heads * parts, heads * MHEAD_DIM)
    head = lax.broadcasted_iota(jnp.int32, shape, 0) % heads
    channel = lax.broadcasted_iota(jnp.int32, shape, 1) // MHEAD_DIM
    return jnp.where(head == channel, 1.0, 0.0).astype(jnp.bfloat16)


def widen(values, spread):
    return plain_dot(two_parts(values), spread)


def head_sums(values, spread):
    heads = spread.shape[0]
    high = values.astype(jnp.bfloat16)
    low = (values - high.astype(jnp.float32)).astype(jnp.bfloat16)
    total = nt_dot(high, spread) + nt_dot(low, spread)
    return total


def nt_dot(left, right):
    return lax.dot_general(
        left, right, (((1,), (1,)), ((), ())), preferred_element_type=jnp.float32
    )


def split_pair(pair, axis):
    lane = lax.broadcasted_iota(jnp.int32, pair.shape, 1)
    blank = jnp.zeros_like(pair)
    return jnp.concatenate(
        [jnp.where(lane < MHEAD_DIM, pair, blank), jnp.where(lane < MHEAD_DIM, blank, pair)],
        axis=axis,
    )


def bf(values):
    return values.astype(jnp.bfloat16)


def ssd_kernel(act_ref, cum_ref, cum_rows_ref, step_ref, spread_ref, y_ref, grown_ref, state_ref, tail_ref):
    chunks, rows, inner = y_ref.shape
    spread = spread_ref[...]
    state_ref[...] = jnp.zeros_like(state_ref)
    tail_ref[...] = jnp.zeros_like(tail_ref)
    late = lax.broadcasted_iota(jnp.int32, (rows, rows), 0) >= lax.broadcasted_iota(
        jnp.int32, (rows, rows), 1
    )

    def one_chunk(chunk, before):
        act = act_ref[chunk]
        cum = cum_ref[chunk]
        cum_rows = cum_rows_ref[chunk]
        scaled = act[:, :inner] * widen(step_ref[chunk], spread)
        input_mat = act[:, inner : inner + STATE]
        output_low = bf(act[:, inner + STATE :])
        last = cum[rows - 1 : rows, :]
        grown_ref[chunk] = widen(jnp.exp(cum + before), spread)
        mixing = nt_dot(output_low, bf(input_mat))
        state = state_ref[...]
        from_state = plain_dot(output_low, bf(state)) * widen(jnp.exp(cum), spread)
        scaled_low = bf(scaled)
        for pair in range(MHEADS // 2):
            kernels = []
            for head in (2 * pair, 2 * pair + 1):
                gap = cum[:, head : head + 1] - cum_rows[head : head + 1, :]
                kernels.append(bf(jnp.exp(jnp.where(late, gap, masked_score)) * mixing))
            span = slice(2 * pair * MHEAD_DIM, (2 * pair + 2) * MHEAD_DIM)
            y_ref[chunk, :, span] = from_state[:, span] + plain_dot(
                jnp.concatenate(kernels, axis=1), split_pair(scaled_low[:, span], 0)
            )
        weighted = scaled * widen(jnp.exp(last - cum), spread)
        fade = widen(jnp.exp(jnp.broadcast_to(last, (8, last.shape[1]))), spread)[:1]
        state_ref[...] = state * fade + plain_dot(bf(input_mat.T), bf(weighted))
        return before + last

    total = lax.fori_loop(0, chunks, one_chunk, jnp.zeros((1, cum_ref.shape[2]), jnp.float32))
    tail_ref[...] = widen(jnp.exp(jnp.broadcast_to(total, (8, total.shape[1]))), spread)


def by_chunks(values):
    return values.reshape(-1, math.gcd(values.shape[0], ssd_rows), values.shape[1])


def ssd_local(act, cum, step_size):
    act, cum, step_size = by_chunks(act), by_chunks(cum), by_chunks(step_size)
    chunks, rows, _ = act.shape
    inner = MHEADS * MHEAD_DIM
    return pl.pallas_call(
        ssd_kernel,
        out_shape=(
            jax.ShapeDtypeStruct((chunks, rows, inner), jnp.float32),
            jax.ShapeDtypeStruct((chunks, rows, inner), jnp.float32),
            jax.ShapeDtypeStruct((STATE, inner), jnp.float32),
            jax.ShapeDtypeStruct((8, inner), jnp.float32),
        ),
        in_specs=in_vmem(5),
        out_specs=tuple(in_vmem(4)),
        compiler_params=compiler_room,
        cost_estimate=pl.CostEstimate(
            flops=chunks * rows * inner * 10000, bytes_accessed=act.size * 16, transcendentals=0
        ),
        name="ssd",
    )(act, cum, jnp.swapaxes(cum, 1, 2), step_size, head_columns(MHEADS, 3))


def ssd_back_kernel(
    act_ref,
    cum_ref,
    cum_rows_ref,
    step_ref,
    grad_ref,
    carry_ref,
    grad_end_ref,
    skip_ref,
    spread_ref,
    grad_act_ref,
    grad_step_ref,
    grad_log_ref,
    grad_skip_ref,
    states_ref,
    grad_state_ref,
    sums_ref,
):
    chunks, rows, _ = act_ref.shape
    inner = grad_ref.shape[2]
    heads = cum_ref.shape[2]
    spread = spread_ref[...]
    one_spread = spread[:heads]
    at_row = lax.broadcasted_iota(jnp.int32, (rows, rows), 0)
    at_column = lax.broadcasted_iota(jnp.int32, (rows, rows), 1)

    def fade_of(last):
        return widen(jnp.exp(jnp.broadcast_to(last, (8, heads))), spread)[:1]

    states_ref[0] = carry_ref[...]
    for chunk in range(chunks - 1):
        cum = cum_ref[chunk]
        last = cum[rows - 1 : rows, :]
        act = act_ref[chunk]
        weighted = act[:, :inner] * widen(jnp.exp(last - cum) * step_ref[chunk], spread)
        states_ref[chunk + 1] = states_ref[chunk] * fade_of(last) + plain_dot(
            bf(act[:, inner : inner + STATE].T), bf(weighted)
        )
    grad_state_ref[...] = grad_end_ref[...]
    grad_skip_ref[...] = jnp.zeros_like(grad_skip_ref)
    sums_ref[...] = jnp.zeros_like(sums_ref)

    def one_chunk(turn, carried):
        chunk = chunks - 1 - turn
        act = act_ref[chunk]
        cum = cum_ref[chunk]
        cum_rows = cum_rows_ref[chunk]
        step = step_ref[chunk]
        grad_y = grad_ref[chunk]
        last = cum[rows - 1 : rows, :]
        inputs_x = act[:, :inner]
        step_wide = widen(step, spread)
        tail = jnp.exp(last - cum)
        tail_wide = widen(tail, spread)
        scaled = inputs_x * step_wide
        scaled_low = bf(scaled)
        grad_low = bf(grad_y)
        input_low = bf(act[:, inner : inner + STATE])
        output_mat = act[:, inner + STATE :]
        output_low = bf(output_mat)
        state = states_ref[chunk]
        state_low = bf(state)
        grad_state = grad_state_ref[...]
        grad_state_low = bf(grad_state)

        grown_grad = grad_y * widen(jnp.exp(cum), spread)
        grown_low = bf(grown_grad)
        from_row = head_sums(grown_grad * plain_dot(output_low, state_low), one_spread)
        grad_output = nt_dot(grown_low, state_low)
        back = plain_dot(input_low, grad_state_low)
        from_column = head_sums(scaled * back, one_spread) * tail
        grad_input = nt_dot(bf(scaled * tail_wide), grad_state_low)
        fade = fade_of(last)
        both = jnp.sum(grad_state * state, axis=0, keepdims=True) * fade
        from_last = head_sums(jnp.broadcast_to(both, (8, inner)), one_spread)[:1]
        grad_state_ref[...] = grad_state * fade + plain_dot(bf(output_mat.T), grown_low)

        mixing = nt_dot(input_low, output_low)
        grad_mixing = jnp.zeros((rows, rows), jnp.float32)
        column_sums = jnp.zeros((rows, rows), jnp.float32)
        grad_step = jnp.zeros((rows, rows), jnp.float32)
        for pair in range(heads // 2):
            span = slice(2 * pair * MHEAD_DIM, (2 * pair + 2) * MHEAD_DIM)
            apart = split_pair(grad_low[:, span], 0)
            grad_kernels = nt_dot(scaled_low[:, span], apart)
            kernels = []
            for side in range(2):
                head = 2 * pair + side
                gap = cum_rows[head : head + 1, :] - cum[:, head : head + 1]
                decay = jnp.exp(jnp.where(at_row <= at_column, gap, masked_score))
                part = grad_kernels[:, side * rows : (side + 1) * rows] * decay
                grad_mixing = grad_mixing + part
                moved = part * mixing
                sums_ref[head : head + 1, :] = jnp.sum(moved, axis=0, keepdims=True)
                column = jnp.sum(moved, axis=1, keepdims=True)
                column_sums = jnp.where(at_column == head, column, column_sums)
                kernels.append(bf(decay * mixing))
            grad_scaled = plain_dot(jnp.concatenate(kernels, axis=1), apart)
            grad_scaled = grad_scaled + back[:, span] * tail_wide[:, span]
            grad_act_ref[chunk, :, span] = (
                grad_scaled * step_wide[:, span] + skip_ref[:, span] * grad_y[:, span]
            )
            by_step = grad_scaled * inputs_x[:, span]
            lane = lax.broadcasted_iota(jnp.int32, by_step.shape, 1)
            for side in range(2):
                mine = jnp.where((lane < MHEAD_DIM) == (side == 0), by_step, 0.0)
                column = jnp.sum(mine, axis=1, keepdims=True)
                grad_step = jnp.where(at_column == 2 * pair + side, column, grad_step)
        grad_mixing_low = bf(grad_mixing)
        grad_act_ref[chunk, :, inner : inner + STATE] = grad_input + plain_dot(
            grad_mixing_low, output_low
        )
        grad_act_ref[chunk, :, inner + STATE :] = grad_output + plain_dot(
            bf(grad_mixing.T), input_low
        )
        grad_step_ref[chunk] = grad_step[:, :heads]
        row_sums = sums_ref[...].T[:, :heads]
        ahead = row_sums - column_sums[:, :heads] + from_row
        from_here = jnp.where(at_row <= at_column, 1.0, 0.0)
        before = jnp.where(at_row > at_column, 1.0, 0.0)
        grad_log_ref[chunk] = (
            jnp.dot(from_here, ahead, precision=highest_precision)
            + jnp.dot(before, from_column, precision=highest_precision)
            + from_last
        )
        grad_skip_ref[...] += jnp.sum(inputs_x * grad_y, axis=0, keepdims=True)
        return carried

    lax.fori_loop(0, chunks, one_chunk, 0)


def ssd_back(act, cum, step_size, grad_y, carry_state, grad_end, skip_row):
    shape = act.shape
    act, cum, step_size, grad_y = (by_chunks(a) for a in (act, cum, step_size, grad_y))
    chunks, rows, width = act.shape
    inner = MHEADS * MHEAD_DIM
    grad_act, grad_step, grad_log, grad_skip = pl.pallas_call(
        ssd_back_kernel,
        out_shape=(
            jax.ShapeDtypeStruct(act.shape, jnp.float32),
            jax.ShapeDtypeStruct(cum.shape, jnp.float32),
            jax.ShapeDtypeStruct(cum.shape, jnp.float32),
            jax.ShapeDtypeStruct((1, inner), jnp.float32),
        ),
        in_specs=in_vmem(9),
        out_specs=tuple(in_vmem(4)),
        scratch_shapes=[
            pltpu.VMEM((chunks, STATE, inner), jnp.float32),
            pltpu.VMEM((STATE, inner), jnp.float32),
            pltpu.VMEM((rows, rows), jnp.float32),
        ],
        compiler_params=compiler_room,
        cost_estimate=pl.CostEstimate(
            flops=chunks * rows * inner * 25000, bytes_accessed=act.size * 16, transcendentals=0
        ),
        name="ssd_back",
    )(
        act,
        cum,
        jnp.swapaxes(cum, 1, 2),
        step_size,
        grad_y,
        carry_state,
        grad_end,
        skip_row,
        head_columns(MHEADS, 3),
    )
    flat = (shape[0], MHEADS)
    return grad_act.reshape(shape), grad_step.reshape(flat), grad_log.reshape(flat), grad_skip


def shifted(block, axis, distance):
    count = lax.axis_size(axis)
    return lax.ppermute(block, axis, [(i, (i + distance) % count) for i in range(count)])


def moved_along(block, axis, distance):
    count = lax.axis_size(axis)
    route = [(i, i + distance) for i in range(count) if 0 <= i + distance < count]
    return lax.ppermute(block, axis, route)


def width_order(width, first):
    sizes = {axis: lax.axis_size(axis) for axis in every_axis}
    rows = width // math.prod(sizes.values())
    rest = lax.broadcasted_iota(jnp.int32, (width, width), 1)
    inside, rest = rest % rows, rest // rows
    owner = {}
    for axis in ("z", "xy".replace(first, ""), first, "core"):
        owner[axis] = (rest % sizes[axis] + lax.axis_index(axis)) % sizes[axis]
        rest = rest // sizes[axis]
    usual = owner["y"]
    for axis in ("core", "z", "x"):
        usual = usual * sizes[axis] + owner[axis]
    usual = usual * rows + inside
    return (lax.broadcasted_iota(jnp.int32, (width, width), 0) == usual).astype(jnp.bfloat16)


def after(values, *others):
    return lax.optimization_barrier((values, others))[0]


def gather_stages(shard, middle):
    parts = [shard] + [shifted(shard, "z", -k) for k in range(1, lax.axis_size("z"))]
    block = jnp.concatenate(parts, axis=0)
    halves = [block[:, :middle], block[:, middle:]]
    arrived = []
    for axes in ("xy", "yx"):
        got = [
            [half] + [shifted(half, axis, -k) for k in range(1, lax.axis_size(axis))]
            for half, axis in zip(halves, axes)
        ]
        arrived += [parts[1] for parts in got]
        halves = [jnp.concatenate(parts, axis=0) for parts in lax.optimization_barrier(got)]
    return [(half, shifted(half, "core", 1)) for half in halves], arrived[:2]


def times_rows(values, pair):
    half = values.shape[1] // 2
    return plain_dot(values[:, :half], pair[0]) + plain_dot(values[:, half:], pair[1])


def times_rows_back(values, pair):
    return jnp.concatenate([back_product(values, pair[0]), back_product(values, pair[1])], axis=1)


def keep_own(total, axis, received):
    kept = total[0]
    for step in range(1, lax.axis_size(axis)):
        got = shifted(total[step].astype(jnp.bfloat16), axis, step)
        received.append(got)
        kept = kept + got.astype(jnp.float32)
    return kept


def core_sum(left, right, first, received):
    half = left.shape[1] // 2
    sizes = [lax.axis_size(axis) for axis in (first, "xy".replace(first, ""), "z")]
    got = shifted(outer_product(left[:, half:], right).astype(jnp.bfloat16), "core", 1)
    received.append(got)
    total = outer_product(left[:, :half], right) + got.astype(jnp.float32)
    return total.reshape(*sizes, -1, right.shape[1])


def side_by_side(parts):
    return parts[0] if len(parts) == 1 else jnp.concatenate(parts, axis=-1)


def first_sums(by_x, by_y, received):
    by_x = side_by_side([keep_own(total, "x", received) for total in by_x])
    by_y = side_by_side([keep_own(total, "y", received) for total in by_y])
    return by_x, by_y


def layer_sums(by_x, by_y, received):
    by_x = keep_own(by_x, "y", received)
    by_y = keep_own(by_y, "x", received)
    return jnp.concatenate([by_x, by_y], axis=-1)


def send_layers(total):
    parts = [total[step].astype(jnp.bfloat16) for step in range(1, total.shape[0])]
    return [total[0]] + [shifted(part, "z", step + 1) for step, part in enumerate(parts)]


def sum_layers(parts):
    return sum(part.astype(jnp.float32) for part in parts)


def sum_everywhere(values, holds):
    for axis in ("core", "y", "x", "z"):
        if axis in holds:
            values = after(values, *holds[axis])
        count = lax.axis_size(axis)
        step = 1
        while step < count:
            values = values + lax.ppermute(values, axis, [(i, i ^ step) for i in range(count)])
            step *= 2
    return values


def send_states(state, tail, direction):
    depth, width = state.shape
    half = width // 2
    at_x = lax.axis_index("x")
    is_second = (at_x == 1) if direction == 1 else (at_x == 0)
    packed = jnp.concatenate([state, tail], axis=0).astype(jnp.bfloat16)
    other = shifted(packed, "x", 1)
    own = packed.astype(jnp.float32)
    first = jnp.where(is_second, other.astype(jnp.float32), own)
    second = jnp.where(is_second, own, other.astype(jnp.float32))
    pair = jnp.concatenate(
        [
            second[depth : depth + 1] * first[:depth] + second[:depth],
            first[depth:] * second[depth:],
        ],
        axis=0,
    )
    mine = jnp.where(at_x == 0, pair[:, :half], pair[:, half:]).astype(jnp.bfloat16)
    steps = range(1, lax.axis_size("z"))
    passed = [moved_along(mine, "z", direction * step) for step in steps]
    return jnp.where(is_second, first, 0.0), other, passed


def carried(behind, passed, direction, received):
    depth, half = behind.shape[0] - 8, behind.shape[1] // 2
    at_x = lax.axis_index("x")
    is_second = (at_x == 1) if direction == 1 else (at_x == 0)
    total = jnp.zeros((depth, half), jnp.float32)
    fade = jnp.ones((1, half), jnp.float32)
    for got in passed:
        total = total + fade * got[:depth].astype(jnp.float32)
        fade = fade * got[depth : depth + 1].astype(jnp.float32)
    total = total.astype(jnp.bfloat16)
    rest = shifted(total, "x", 1)
    received.append(rest)
    left, right = jnp.where(at_x == 0, total, rest), jnp.where(at_x == 0, rest, total)
    carry = jnp.concatenate([left, right], axis=1).astype(jnp.float32)
    return jnp.where(is_second, behind[depth : depth + 1], 1.0) * carry + behind[:depth]


def keys_behind(own):
    return [moved_along(own, "z", step) if step else own for step in range(lax.axis_size("z"))]


def all_slots(blocks):
    blocks = jnp.stack(blocks)
    slots = jnp.stack([blocks, shifted(blocks, "x", 1)], axis=1)
    return slots.reshape(-1, *blocks.shape[1:])


def sum_key_grads(kept, swapped, received):
    kept = kept + swapped.astype(jnp.float32)
    own = kept[0]
    for step in range(1, kept.shape[0]):
        got = moved_along(kept[step].astype(jnp.bfloat16), "z", -step)
        received.append(got)
        own = own + got.astype(jnp.float32)
    return own


def on_device(
    tokens,
    gain_one,
    w_in,
    w_step,
    conv_weight,
    conv_bias,
    mamba_heads,
    skip_weight,
    w_query,
    w_keyval,
    w_attn_out,
    w_mix_out,
    gain_two,
    w_gate_up,
    w_down,
    cotangent,
):
    width = tokens.shape[2]
    row_count = tokens.shape[1]
    inner_width = MHEADS * MHEAD_DIM
    device_count = math.prod(lax.axis_size(axis) for axis in every_axis)
    channels = conv_weight.shape[1] * device_count
    key_width = KVHEADS * HEAD_DIM
    query_width = QHEADS * HEAD_DIM
    own_rows = gain_one.shape[0]
    at_z, at_x = lax.axis_index("z"), lax.axis_index("x")
    place = jnp.stack([at_z, at_x]).astype(jnp.int32)

    taps = jnp.concatenate([conv_weight, conv_bias[None]], axis=0)
    tap_columns = -(-taps.size // own_rows)
    tap_shard = jnp.pad(taps.reshape(-1), (0, tap_columns * own_rows - taps.size))
    query_at = channels + w_keyval.shape[1]
    step_at = query_at + query_width
    gain_at = step_at + w_step.shape[1]
    tap_at = gain_at + 2
    conv_shard = jnp.concatenate(
        [
            w_in[:, inner_width:],
            w_keyval,
            w_query,
            w_step,
            gain_one[:, None],
            gain_two[:, None],
            tap_shard.reshape(tap_columns, own_rows).T,
            jnp.zeros((own_rows, -(tap_at + tap_columns) % 128), jnp.bfloat16),
        ],
        axis=1,
    )
    middle = conv_shard.shape[1] // 256 * 128
    (pair_a, pair_b), arrived = gather_stages(conv_shard, middle)
    late_shards = [w_in[:, :inner_width], w_mix_out.T, w_attn_out.T, w_gate_up, w_down.T]
    late_shard = after(jnp.concatenate(late_shards, axis=1), *arrived)
    late = lax.all_gather(late_shard, every_axis, axis=0, tiled=True)
    out_at = inner_width
    ff_at = out_at + inner_width + query_width
    full_gate_z, full_out, full_gate, full_up, full_down = jnp.split(
        late, [out_at, ff_at, ff_at + FF, ff_at + 2 * FF], axis=1
    )

    order_x, order_y = lax.optimization_barrier((width_order(width, "x"), width_order(width, "y")))
    inputs = tokens[0].astype(jnp.float32)
    grad_output = cotangent[0]
    small = jnp.concatenate(
        [half[:, gain_at - middle : tap_at + tap_columns - middle] for half in pair_b], axis=0
    )
    small_rows = lax.dot_general(
        small, order_x, (((0,), (1,)), ((), ())), preferred_element_type=jnp.float32
    )
    gain_one_float, gain_two_float = small_rows[0], small_rows[1]
    tap_all = small_rows[2:].reshape(tap_columns, device_count, own_rows)
    tap_all = jnp.swapaxes(tap_all, 0, 1).reshape(device_count, -1)[:, : taps.size]
    tap_all = jnp.swapaxes(tap_all.reshape(-1, *taps.shape), 0, 1).reshape(taps.shape[0], channels)

    def reordered(rows, order):
        return plain_dot(rows, order).astype(jnp.bfloat16)

    normed = rms_norm(inputs, gain_one_float).astype(jnp.bfloat16)
    normed_x, normed_y = reordered(normed, order_x), reordered(normed, order_y)
    projected_a = times_rows(normed_y, pair_a)
    projected_b = times_rows(normed_x, pair_b)
    conv_input = jnp.concatenate(
        [
            projected_a.astype(jnp.bfloat16),
            projected_b[:, : channels - middle].astype(jnp.bfloat16),
        ],
        axis=1,
    )
    keyval_raw = projected_b[:, channels - middle : query_at - middle]
    query_raw = projected_b[:, query_at - middle : step_at - middle]
    step_raw = projected_b[:, step_at - middle : gain_at - middle]
    positions = (at_z * lax.axis_size("x") + at_x) * row_count + jnp.arange(
        row_count, dtype=jnp.int32
    )
    cosine, sine = turn_columns(positions)
    keyval_cols = keyval_raw.T
    key_cols = turn_rows(keyval_cols[:key_width], cosine, sine)
    by_head = (KVHEADS, 1, HEAD_DIM, row_count)
    own_keyval = jnp.concatenate(
        [key_cols.reshape(by_head), keyval_cols[key_width:].reshape(by_head)], axis=1
    ).reshape(2 * key_width, row_count)
    key_blocks = keys_behind(own_keyval.T.astype(jnp.bfloat16))
    query_cols = turn_rows(query_raw.T, cosine, sine).astype(jnp.bfloat16)
    border = lax.ppermute(
        conv_input[row_count - (CONV - 1) :],
        seq_axes,
        [(i, i + 1) for i in range(lax.axis_size(seq_axes) - 1)],
    )
    extended = jnp.concatenate([border, conv_input], axis=0).astype(jnp.float32)
    act, pull_conv = jax.vjp(conv_act, extended, tap_all[:CONV], tap_all[CONV])
    step_size = jax.nn.softplus(step_raw + mamba_heads[1][None, :])
    log_decay = -jnp.exp(mamba_heads[0])[None, :] * step_size
    by_chunk = by_chunks(log_decay)
    chunk_rows = by_chunk.shape[1]
    lower = jnp.tril(jnp.ones((chunk_rows, chunk_rows), jnp.float32))
    cum = jnp.stack([jnp.dot(lower, c, precision=highest_precision) for c in by_chunk])
    cum = cum.reshape(log_decay.shape)
    y_local, grown, fresh_state, tail, *key_blocks = after(
        (*ssd_local(act, cum, step_size), *key_blocks)
    )
    all_keyval = all_slots(key_blocks)
    all_cols = jnp.swapaxes(all_keyval, 1, 2)
    y_local = y_local.reshape(row_count, inner_width)
    grown = grown.reshape(row_count, inner_width)
    behind, other_state, passed = send_states(fresh_state, tail, 1)
    attended_cols, logs = attend(place, after(query_cols, other_state), all_keyval, all_cols)
    attended_cols, logs, *passed = after((attended_cols, logs, *passed))
    carry_state = carried(behind, passed, 1, [])
    gate_z = plain_dot(normed, full_gate_z)
    attention_rows = attended_cols.T.astype(jnp.bfloat16)

    skip_row = jnp.repeat(skip_weight, MHEAD_DIM)[None, :]
    output_low = act[:, inner_width + STATE :].astype(jnp.bfloat16)
    ssm_y = (
        y_local
        + grown * plain_dot(output_low, carry_state.astype(jnp.bfloat16))
        + skip_row * act[:, :inner_width]
    )
    gate_sigmoid = jax.nn.sigmoid(gate_z)
    mixer = (ssm_y * gate_z * gate_sigmoid).astype(jnp.bfloat16)
    branches = jnp.concatenate([mixer, attention_rows], axis=1)
    hidden = inputs + back_product(branches, full_out)
    normed_two = rms_norm(hidden, gain_two_float).astype(jnp.bfloat16)
    gate_part = plain_dot(normed_two, full_gate)
    up_part = plain_dot(normed_two, full_up)
    activated = (jax.nn.silu(gate_part) * up_part).astype(jnp.bfloat16)
    result = hidden + back_product(activated, full_down)
    output = result.astype(jnp.bfloat16)[None]

    grad_activated = plain_dot(grad_output, full_down)
    core_got = []
    down_half = FF // 2
    ff_sigmoid = jax.nn.sigmoid(gate_part)
    grad_gate = grad_activated * up_part * ff_sigmoid * (1.0 + gate_part * (1.0 - ff_sigmoid))
    grad_gate = grad_gate.astype(jnp.bfloat16)
    grad_up = (grad_activated * gate_part * ff_sigmoid).astype(jnp.bfloat16)
    gate_total = core_sum(reordered(normed_two, order_x), grad_gate, "x", core_got)
    up_total = core_sum(reordered(normed_two, order_y), grad_up, "y", core_got)
    down_a = core_sum(reordered(grad_output, order_x), activated[:, :down_half], "x", [])
    down_b = core_sum(reordered(grad_output, order_y), activated[:, down_half:], "y", [])
    ff_got = []
    ff_later = []
    ff_parts = send_layers(
        layer_sums(*first_sums([gate_total, down_a], [up_total, down_b], ff_got), ff_later)
    )
    grad_normed_two = back_product(after(grad_gate, *core_got), full_gate) + back_product(
        grad_up, full_up
    )
    _, pull_two = jax.vjp(rms_norm, hidden, gain_two_float)
    grad_hidden_norm, grad_gain_two = pull_two(grad_normed_two)
    grad_hidden = grad_output.astype(jnp.float32) + grad_hidden_norm
    grad_branch = grad_hidden.astype(jnp.bfloat16)
    grad_branches = after(plain_dot(grad_branch, full_out), ff_got[1], ff_got[3])
    grad_mixer = grad_branches[:, :inner_width]
    grad_y = grad_mixer * gate_z * gate_sigmoid
    grad_gate_z = grad_mixer * ssm_y * gate_sigmoid * (1.0 + gate_z * (1.0 - gate_sigmoid))
    from_output = outer_product(output_low, (grown * grad_y).astype(jnp.bfloat16))
    behind, other_state, passed = send_states(from_output, tail, -1)

    grad_attention = grad_branches[:, inner_width:].astype(jnp.bfloat16)
    out_got = []
    out_total = core_sum(reordered(grad_branch, order_y), branches, "y", out_got)
    grad_gate_low = grad_gate_z.astype(jnp.bfloat16)
    in_gate_total = core_sum(normed_x, grad_gate_low, "x", out_got)
    grad_normed_part = back_product(grad_gate_low, full_gate_z)
    grad_cols = grad_attention.T
    query_rows = query_cols.T

    grad_query_cols, kept, other = attend_back(
        after(place, gate_total, up_total, other_state),
        query_cols,
        query_rows,
        grad_cols,
        grad_attention,
        attended_cols,
        logs,
        all_keyval,
        all_cols,
    )
    grad_query_cols, kept, other, *passed = after(
        (grad_query_cols, kept, other, *passed), ff_got[0], ff_got[2], *out_got
    )
    rested = []
    grad_end = carried(behind, passed, -1, rested)
    swapped = shifted(other, "x", 1)
    key_got = []
    own_grads = sum_key_grads(kept, swapped, key_got)
    mid_got = []
    mid_both = first_sums(
        [after(in_gate_total, *rested)], [after(out_total, *rested)], mid_got
    )
    mid_later = []
    mid_layer = layer_sums(*mid_both, mid_later)
    grad_query = turn_rows(grad_query_cols, cosine, -sine).T.astype(jnp.bfloat16)
    own_cols = own_grads.T.reshape(KVHEADS, 2, HEAD_DIM, row_count)
    grad_keys = turn_rows(own_cols[:, 0].reshape(key_width, row_count), cosine, -sine)
    grad_keyval = jnp.concatenate([grad_keys, own_cols[:, 1].reshape(key_width, row_count)], axis=0)
    grad_keyval = grad_keyval.T.astype(jnp.bfloat16)

    ssd_skip = after(
        skip_row, grad_normed_part
    )
    grad_act, grad_step_size, grad_log, grad_skip = ssd_back(
        act, cum, step_size, grad_y, carry_state, grad_end, ssd_skip
    )
    grad_act, grad_step_size, grad_log = after(
        (grad_act, grad_step_size, grad_log), *ff_later, swapped
    )
    grad_step_size = grad_step_size - grad_log * jnp.exp(mamba_heads[0])[None, :]
    grad_step_raw = grad_step_size * jax.nn.sigmoid(step_raw + mamba_heads[1][None, :])
    grad_heads = jnp.stack([jnp.sum(grad_log * log_decay, axis=0), jnp.sum(grad_step_raw, axis=0)])
    grad_extended, grad_conv_weight, grad_conv_bias = pull_conv(grad_act)
    grad_extended, *ff_parts = after((grad_extended, *ff_parts), *key_got, *mid_got)
    ff_sums = sum_layers(ff_parts)
    rim_back = lax.ppermute(
        grad_extended[: CONV - 1],
        seq_axes,
        [(i + 1, i) for i in range(lax.axis_size(seq_axes) - 1)],
    )
    grad_conv_input = grad_extended[CONV - 1 :] + jnp.pad(
        rim_back, ((row_count - (CONV - 1), 0), (0, 0))
    )
    grad_step_low = jnp.pad(
        grad_step_raw.astype(jnp.bfloat16), ((0, 0), (0, conv_shard.shape[1] - gain_at))
    )
    grad_few = jnp.concatenate([grad_keyval, grad_query, grad_step_low], axis=1)
    few_core_got, last_core_got = [], []
    few_total = core_sum(normed_y, grad_few, "y", few_core_got)
    grad_conv_low = after(
        grad_conv_input.astype(jnp.bfloat16), *few_core_got, *mid_later
    )
    conv_total = core_sum(normed_x, grad_conv_low, "x", last_core_got)
    last_got, last_later = [], []
    mid_parts = send_layers(after(mid_layer, *last_core_got))
    last_both = after(first_sums([conv_total], [few_total], last_got), *last_got)
    last_parts = send_layers(layer_sums(*last_both, last_later))
    last_parts, *mid_parts = after((tuple(last_parts), *mid_parts), *last_later)
    last_sums, mid_sums = sum_layers(last_parts), sum_layers(mid_parts)
    grad_normed = lax.dot_general(
        jnp.concatenate(
            [
                times_rows_back(grad_conv_low[:, :middle], pair_a),
                times_rows_back(
                    jnp.concatenate([grad_conv_low[:, middle:], grad_few], axis=1), pair_b
                ),
            ],
            axis=1,
        ),
        jnp.concatenate([order_y, order_x], axis=1).astype(jnp.float32),
        (((1,), (1,)), ((), ())),
        precision=lax.Precision.HIGH,
        preferred_element_type=jnp.float32,
    )
    _, pull_one = jax.vjp(rms_norm, inputs, gain_one_float)
    grad_input_norm, grad_gain_one = pull_one(grad_normed + grad_normed_part)
    input_grad = (grad_hidden + grad_input_norm)[None]
    gain_grads = jnp.stack([grad_gain_two, grad_gain_one])

    def padded(row):
        return jnp.pad(row, ((0, 0), (0, channels - row.shape[1])))

    head_row = jnp.concatenate(
        [grad_heads[:1], grad_heads[1:], jnp.sum(grad_skip.reshape(MHEADS, -1), axis=1)[None]],
        axis=1,
    )
    summed = sum_everywhere(
        after(
            jnp.concatenate(
                [
                    grad_conv_weight,
                    grad_conv_bias[None],
                    padded(gain_grads),
                    padded(head_row),
                ],
                axis=0,
            ),
            *last_core_got,
        ),
        {"x": last_got, "z": last_later},
    )
    device = lax.axis_index(every_axis)
    own_channels = conv_weight.shape[1]
    own_taps = lax.dynamic_slice_in_dim(summed[: CONV + 1], device * own_channels, own_channels, 1)
    own_gain_two = lax.dynamic_slice_in_dim(summed[CONV + 1], device * own_rows, own_rows)
    own_gain_one = lax.dynamic_slice_in_dim(summed[CONV + 2], device * own_rows, own_rows)
    head_sums_row = summed[CONV + 3]
    return (
        output,
        input_grad,
        own_gain_one,
        jnp.concatenate([mid_sums[:, :inner_width], last_sums[:, :channels]], axis=1),
        last_sums[:, step_at:gain_at],
        own_taps[:CONV],
        own_taps[CONV],
        head_sums_row[: 2 * MHEADS].reshape(2, MHEADS),
        head_sums_row[2 * MHEADS : 3 * MHEADS],
        last_sums[:, query_at:step_at],
        last_sums[:, channels:query_at],
        mid_sums[:, 2 * inner_width :].T,
        mid_sums[:, inner_width : 2 * inner_width].T,
        own_gain_two,
        jnp.concatenate([ff_sums[:, :FF], ff_sums[:, FF + down_half : 2 * FF + down_half]], axis=1),
        jnp.concatenate(
            [ff_sums[:, FF : FF + down_half], ff_sums[:, 2 * FF + down_half :]], axis=1
        ).T,
    )


def solution(mesh):
    dp, seq = mesh.shape["dp"], mesh.shape["seq"]
    by_axis = Mesh(mesh.devices.reshape(dp // 2, 2, seq // 2, 2), every_axis)
    pieces = P(("y", "core"), seq_axes, None)
    rows = P(every_axis, None)
    columns = P(None, every_axis)
    vector = P(every_axis)
    weights = (rows, rows, columns, columns, vector, rows, columns)
    return jax.shard_map(
        on_device,
        mesh=by_axis,
        in_specs=(pieces, vector, rows, rows, columns, vector, P(), P(), *weights, pieces),
        out_specs=(pieces, pieces, vector, rows, rows, columns, vector, P(), P(), *weights),
        check_vma=False,
    )
```
